32 devices in a mesh: video: 4 (over y, x), context: 8 (over z, core).
Axes of the slice: x: 2, y: 2, z: 4, core: 2. Of those that a mesh axis runs over, the one named last changes fastest.
Arguments:
- queries: bfloat16 [4096, 4096], P(('video', 'context')), parts along dimension 0, may hold values from -135 to 135
- keys: bfloat16 [4096, 4096], P(('video', 'context')), parts along dimension 0, may hold values from -5 to 5
- values: bfloat16 [4096, 4096], P(('video', 'context')), parts along dimension 0, may hold values from -6 to 6
- value_layer_input: bfloat16 [4096, 4096], P(('video', 'context')), parts along dimension 0, may hold values from -6 to 6
- adapter_down_weight: bfloat16 [4096, 64], replicated, may hold values from -0.09375 to 0.09375
- adapter_up_weight: bfloat16 [4096, 64], replicated, may hold values from -0.75 to 0.75
- neighbors: int32 [64, 4], P(('video', 'context')), parts along dimension 0, may hold values from 0 to 15, as said below
Outputs:
- student_out: bfloat16 [4096, 4096], P(('video', 'context')), parts along dimension 0
- grad_down: float32 [16384, 64], P(('video', 'context')), parts along dimension 0
- grad_up: float32 [16384, 64], P(('video', 'context')), parts along dimension 0
The draws below stay inside these ranges and needn't reach their ends.
There are 4 independent parts, one for each index of `video`. The reference program is written for one: setup_inputs(seed, part) draws one part's arguments, and reference() takes and returns one part's arrays. A program takes and returns all parts, laid end to end along the dimension named above; an argument that names none is the same for every part. Nothing has to cross between parts.
Inputs may be any that keep to these rules, and one draw needn't show every extreme that they name: `neighbors`: row i begins with i itself; its 4 entries are distinct tiles of the slab of tile i, the slab before or the slab after, where slab = tile // 2.
All inputs are finite; a program needn't handle non-finite values.
Results may differ from the reference program's by a relative error of at most 0.008.
Values may be sent and summed in bfloat16 or wider, within the bound.
No kernel may reach another device: no remote copies, remote signals or barrier semaphores. Data moves between devices by JAX's collectives and lax.ppermute only.
A program may use at most 64 MiB of HBM per device.

```python
import jax
import jax.numpy as jnp
from jax import lax

H = 32
HD = 128
MODEL_WIDTH = 4096
ADAPTER_RANK = 64
TOK_DEV = 128
TILE = 64
NB = 4
TOKENS = 1024
TPD = 2
NTILES = 16
N_CONTEXT = 8


def drawn_pair(key):
    query_key = jax.random.fold_in(key, 101)
    key_key = jax.random.fold_in(key, 202)
    keys = jax.random.truncated_normal(key_key, -5.0, 5.0, (TOKENS, MODEL_WIDTH), jnp.float32)
    queries = jax.random.truncated_normal(query_key, -5.0, 5.0, (TOKENS, MODEL_WIDTH), jnp.float32)
    return (queries, keys)


def draw_queries(key, part):
    return drawn_pair(key)[0].astype(jnp.bfloat16)


def draw_keys(key, part):
    return drawn_pair(key)[1].astype(jnp.bfloat16)


def draw_neighbors(key, part):
    tiles = jnp.arange(NTILES, dtype=jnp.int32)
    slots = jnp.arange(3 * TPD, dtype=jnp.int32)
    candidates = (tiles[:, None] // TPD - 1) * TPD + slots[None, :]
    valid = (candidates >= 0) & (candidates < NTILES)
    itself = candidates == tiles[:, None]
    scores = jax.random.randint(jax.random.fold_in(key, 404), (NTILES, 3 * TPD), 0, 1000) * (3 * TPD) + slots[None, :]
    scores = jnp.where(itself, 1000000, jnp.where(valid, scores, -1 - slots[None, :]))
    order = lax.top_k(scores, NB)[1]
    return jnp.take_along_axis(candidates, order, axis=1).astype(jnp.int32)


def block_scale(rng, shape, cuts, smallest, high):
    factor_of, own = 1.0, jax.random.fold_in(rng, 6)
    for position, parts in cuts:
        draws = jnp.exp(jax.random.uniform(jax.random.fold_in(own, position), (parts,), jnp.float32, smallest / len(cuts), high / len(cuts)))
        factor_of = factor_of * jnp.repeat(draws, shape[position] // parts).reshape([-1 if axis == position else 1 for axis in range(len(shape))])
    return factor_of


def scatter_about(own_key, shape, spread, bound, pieces=(), kind=jnp.bfloat16):
    loudness = block_scale(own_key, shape, pieces, -0.22, 0.18) if pieces else 1.0
    drawn = jax.random.normal(own_key, shape, jnp.float32) * spread * loudness
    return jnp.minimum(jnp.maximum(drawn, -bound), bound).astype(kind)


def setup_inputs(seed: int = 0, part: int = 0) -> dict:
    key_list = jax.random.split(jax.random.key(seed), 8)
    own_keys = jax.random.split(jax.random.fold_in(key_list[7], part), 8)
    queries = draw_queries(jax.random.fold_in(jax.random.fold_in(key_list[7], part), 71), part)
    keys = draw_keys(jax.random.fold_in(jax.random.fold_in(key_list[7], part), 71), part)
    values = scatter_about(own_keys[2], (TOKENS, MODEL_WIDTH), 1.0, 6.0, ((0, 8),))
    value_layer_input = scatter_about(own_keys[3], (TOKENS, MODEL_WIDTH), 1.0, 6.0, ((0, 8),))
    adapter_down_weight = scatter_about(key_list[4], (MODEL_WIDTH, ADAPTER_RANK), MODEL_WIDTH ** -0.5, 0.09375)
    adapter_up_weight = scatter_about(key_list[5], (MODEL_WIDTH, ADAPTER_RANK), ADAPTER_RANK ** -0.5, 0.75)
    neighbors = draw_neighbors(jax.random.fold_in(jax.random.fold_in(key_list[7], part), 71), part)
    return dict(queries=queries, keys=keys, values=values, value_layer_input=value_layer_input, adapter_down_weight=adapter_down_weight, adapter_up_weight=adapter_up_weight, neighbors=neighbors)


def full_heads(queries, keys, values):
    total = queries.shape[0]
    block = min(512, total)
    scale = HD ** -0.5
    keys_float = keys.astype(jnp.float32)
    values_float = values.astype(jnp.float32)

    def one_block(query_block):
        scores = jnp.einsum("qhd,khd->hqk", query_block.astype(jnp.float32), keys_float) * scale
        top = jnp.max(scores, axis=2, keepdims=True)
        expo = jnp.exp(scores - top)
        weights = (expo / jnp.sum(expo, axis=2, keepdims=True)).astype(jnp.bfloat16)
        return jnp.einsum("hqk,khd->qhd", weights.astype(jnp.float32), values_float).astype(jnp.bfloat16)

    blocks = queries.reshape(total // block, block, queries.shape[1], queries.shape[2])
    return lax.map(one_block, blocks).reshape(queries.shape)


def contract_rows(left, right):
    return lax.dot_general(left.astype(jnp.float32), right.astype(jnp.float32), (((0,), (0,)), ((), ())), precision=lax.Precision.HIGHEST, preferred_element_type=jnp.float32)


def reference(queries, keys, values, value_layer_input, adapter_down_weight, adapter_up_weight, neighbors):
    teacher = full_heads(queries.reshape(TOKENS, H, HD), keys.reshape(TOKENS, H, HD), values.reshape(TOKENS, H, HD)).reshape(TOKENS, MODEL_WIDTH)
    adapter_down_rows = jnp.dot(value_layer_input, adapter_down_weight, preferred_element_type=jnp.float32).astype(jnp.bfloat16)
    adapter_value_term = lax.dot_general(adapter_down_rows, adapter_up_weight, (((1,), (1,)), ((), ())), preferred_element_type=jnp.float32)
    learner_values = (values.astype(jnp.float32) + adapter_value_term).astype(jnp.bfloat16)
    up_float = adapter_up_weight.astype(jnp.float32)
    border_width = ((TOK_DEV, TOK_DEV), (0, 0))
    keys_pad = jnp.pad(keys, border_width)
    values_pad = jnp.pad(learner_values, border_width)
    input_pad = jnp.pad(value_layer_input, border_width)
    padded_down_rows = jnp.pad(adapter_down_rows, border_width)
    slots = jnp.arange(3 * TPD, dtype=jnp.int32)
    scale = HD ** -0.5
    factor = TOKENS ** -0.5

    def slab_step(carry, slab):
        start = (slab * TOK_DEV).astype(jnp.int32)
        win_keys = lax.dynamic_slice_in_dim(keys_pad, start, 3 * TOK_DEV, 0).reshape(3 * TOK_DEV, H, HD)
        win_values = lax.dynamic_slice_in_dim(values_pad, start, 3 * TOK_DEV, 0).reshape(3 * TOK_DEV, H, HD)
        win_input = lax.dynamic_slice_in_dim(input_pad, start, 3 * TOK_DEV, 0)
        win_down = lax.dynamic_slice_in_dim(padded_down_rows, start, 3 * TOK_DEV, 0)
        slab_queries = lax.dynamic_slice_in_dim(queries, start, TOK_DEV, 0).reshape(TOK_DEV, H, HD)
        slab_teacher = lax.dynamic_slice_in_dim(teacher, start, TOK_DEV, 0)
        slab_tiles = lax.dynamic_slice_in_dim(neighbors, (slab * TPD).astype(jnp.int32), TPD, 0)
        offsets = slab_tiles - (slab - 1) * TPD
        tile_mask = jnp.any(offsets[:, :, None] == slots[None, None, :], axis=1)
        token_mask = jnp.broadcast_to(tile_mask[:, None, :, None], (TPD, TILE, 3 * TPD, TILE)).reshape(TOK_DEV, 3 * TOK_DEV)
        scores = jnp.einsum("qhd,khd->hqk", slab_queries.astype(jnp.float32), win_keys.astype(jnp.float32)) * scale
        scores = jnp.where(token_mask[None], scores, -1e30)
        top = jnp.max(scores, axis=2, keepdims=True)
        expo = jnp.exp(scores - top)
        weights = (expo / jnp.sum(expo, axis=2, keepdims=True)).astype(jnp.bfloat16)
        student = jnp.einsum("hqk,khd->qhd", weights.astype(jnp.float32), win_values.astype(jnp.float32)).reshape(TOK_DEV, MODEL_WIDTH)
        output_grad = ((student - slab_teacher.astype(jnp.float32)) * factor).astype(jnp.bfloat16)
        key_gradient = jnp.einsum("hqk,qhd->khd", weights.astype(jnp.float32), output_grad.reshape(TOK_DEV, H, HD).astype(jnp.float32))
        key_gradient = key_gradient.reshape(3 * TOK_DEV, MODEL_WIDTH)
        adapter_latent_rows = jnp.dot(key_gradient, up_float, precision=lax.Precision.HIGHEST, preferred_element_type=jnp.float32)
        grad_down = carry[0] + contract_rows(win_input, adapter_latent_rows)
        grad_up = carry[1] + contract_rows(key_gradient, win_down)
        return (grad_down, grad_up), student.astype(jnp.bfloat16)

    zeros = jnp.zeros((MODEL_WIDTH, ADAPTER_RANK), jnp.float32)
    (grad_down, grad_up), outputs = lax.scan(slab_step, (zeros, zeros), jnp.arange(N_CONTEXT, dtype=jnp.int32))
    return outputs.reshape(TOKENS, MODEL_WIDTH), grad_down, grad_up
```

```python
import functools
import math

import jax
import jax.numpy as jnp
from jax import lax
from jax.experimental import pallas as pl
from jax.experimental.pallas import tpu as pltpu
from jax.sharding import PartitionSpec as P

H = 32
HIDDEN = -1e30
VMEM = 48 * 1024 * 1024
NT = (((1,), (1,)), ((), ()))
TN = (((0,), (0,)), ((), ()))
NN = (((1,), (0,)), ((), ()))


def mm(a, b, dims=NN):
    return lax.dot_general(a, b, dims, preferred_element_type=jnp.float32)


def params():
    return pltpu.CompilerParams(vmem_limit_bytes=VMEM)


SMEM = pl.BlockSpec(memory_space=pltpu.SMEM)
ANY = pl.BlockSpec(memory_space=pl.ANY)


def exchange(blocks, count):
    order = sorted(range(1, count), key=lambda k: -k)
    got = {0: blocks[0]}
    for k in order:
        got[k] = lax.ppermute(blocks[k], "context", [(i, i ^ k) for i in range(count)])
    return [got[k] for k in range(count)]


def pack_kernel(count, group, start, width, me_ref, q_ref, k_ref, v_ref, *rest):
    outs, sems = rest[:count], rest[count]
    me = me_ref[0]
    copies = []
    for k in range(count):
        column = pl.multiple_of((me ^ k) * group + start, 128)
        for t, ref in enumerate((q_ref, k_ref, v_ref)):
            copies.append(
                pltpu.make_async_copy(
                    ref.at[:, pl.ds(column, width)], outs[k].at[t], sems.at[3 * k + t]
                )
            )
    for copy in copies:
        copy.start()
    for copy in copies:
        copy.wait()


def pack(me, q, k, v, count, start, width):
    tok, model = q.shape
    return pl.pallas_call(
        functools.partial(pack_kernel, count, model // count, start, width),
        out_shape=[jax.ShapeDtypeStruct((3, tok, width), q.dtype)] * count,
        in_specs=[SMEM, ANY, ANY, ANY],
        out_specs=[ANY] * count,
        scratch_shapes=[pltpu.SemaphoreType.DMA((3 * count,))],
        compiler_params=params(),
        name="pack",
    )(me, q, k, v)


def unpack_kernel(count, group, spans, me_ref, *rest):
    total = count * len(spans)
    refs, out, sems = rest[:total], rest[total], rest[total + 1]
    me = me_ref[0]
    copies = []
    for c, (start, width) in enumerate(spans):
        for k in range(count):
            column = pl.multiple_of((me ^ k) * group + start, 128)
            copies.append(
                pltpu.make_async_copy(
                    refs[c * count + k],
                    out.at[:, pl.ds(column, width)],
                    sems.at[c * count + k],
                )
            )
    for copy in copies:
        copy.start()
    for copy in copies:
        copy.wait()


def unpack(me, blocks, count, spans, model):
    tok = blocks[0].shape[0]
    return pl.pallas_call(
        functools.partial(unpack_kernel, count, model // count, spans),
        out_shape=jax.ShapeDtypeStruct((tok, model), blocks[0].dtype),
        in_specs=[SMEM] + [ANY] * len(blocks),
        out_specs=ANY,
        scratch_shapes=[pltpu.SemaphoreType.DMA((len(blocks),))],
        compiler_params=params(),
        name="unpack",
    )(me, *blocks)


def attention_kernel(count, tok, hd, slots, rank, last, factor, me_ref, *rest):
    blocks, rest = rest[:count], rest[count:]
    notes, rest = rest[:count], rest[count:]
    up_ref, hid_ref, rest = rest[0], rest[1], rest[2:]
    outs, rest = rest[:count], rest[count:]
    gup_ref, rest = rest[0], rest[1:]
    nh = count if last else 1
    hid_out, rest = rest[:nh], rest[nh:]
    q_s, k_s, vt_s, svt_s, lora_s, grad_s, hid_s = rest
    head = pl.program_id(0)
    me = me_ref[0]
    tile = 3 * tok // slots
    scale = hd ** (-0.5) * math.log2(math.e)

    @pl.when(head == 0)
    def _():
        hid_s[...] = hid_ref[...]
        for p in range(count):
            lora_s[:, p * tok : (p + 1) * tok] = notes[p][:rank, :]

    for p in range(count):
        q_s[p] = blocks[p][0]
        k_s[p * tok : (p + 1) * tok, :] = blocks[p][1]
        vt_s[:, p * tok : (p + 1) * tok] = blocks[p][2].T
    up_t = up_ref[...]
    for p in range(count):
        cols = slice(p * tok, (p + 1) * tok)
        term = mm(up_t, lora_s[:, cols], TN)
        svt_s[p] = (vt_s[:, cols].astype(jnp.float32) + term).astype(jnp.bfloat16)
    grad_s[...] = jnp.zeros_like(grad_s)

    for p in range(count):
        query = q_s[p]
        scores = mm(k_s[...], query, NT)
        top = jnp.max(scores, axis=0, keepdims=True)
        expo = jnp.exp2((scores - top) * scale)
        norm = jnp.sum(expo, axis=0, keepdims=True)
        teacher = mm(vt_s[...], expo.astype(jnp.bfloat16)) / norm
        teacher = teacher.astype(jnp.bfloat16).astype(jnp.float32)

        slab = me ^ p
        low = jnp.where(slab > 0, (slab - 1) ^ me, p)
        high = jnp.where(slab < count - 1, (slab + 1) ^ me, p)
        places = (low, p, high)
        keys = jnp.concatenate(
            [k_s[pl.ds(pl.multiple_of(w * tok, tok), tok), :] for w in places], axis=0
        )
        seen = notes[p][rank:, :].astype(jnp.float32)[:slots]
        bias = (seen - 1.0) * (-HIDDEN)
        scores = mm(keys, query, NT).reshape(slots, tile, tok) + bias[:, None, :]
        scores = scores.reshape(3 * tok, tok)
        top = jnp.max(scores, axis=0, keepdims=True)
        expo = jnp.exp2((scores - top) * scale)
        norm = jnp.sum(expo, axis=0, keepdims=True)
        weights = (expo * (1.0 / norm)).astype(jnp.bfloat16)
        values = jnp.concatenate([svt_s[w] for w in places], axis=1)
        student = mm(values, weights)
        outs[p][...] = student.T.astype(jnp.bfloat16)
        delta = ((student - teacher) * factor).astype(jnp.bfloat16)
        grads = mm(weights, delta, NT)
        for n, w in enumerate(places):
            grad_s[w] += grads[n * tok : (n + 1) * tok]

    grad = grad_s[...].reshape(count * tok, hd).astype(jnp.bfloat16)
    gup_ref[...] = mm(lora_s[...], grad).T
    hid_s[...] += mm(up_t, grad, NT)

    @pl.when(head == pl.num_programs(0) - 1)
    def _():
        if last:
            for p in range(count):
                hid_out[p][...] = hid_s[:, p * tok : (p + 1) * tok].astype(jnp.bfloat16)
        else:
            hid_out[0][...] = hid_s[...]


def attention(me, blocks, notes, up_t, hid, first, hd, slots, last, total):
    count = len(blocks)
    tok = blocks[0].shape[1]
    nh = blocks[0].shape[2] // hd
    rank = up_t.shape[0]
    bf, f32 = jnp.bfloat16, jnp.float32
    whole = lambda shape: pl.BlockSpec(shape, lambda h: (0,) * len(shape))
    if last:
        hid_shape = [jax.ShapeDtypeStruct((rank, tok), bf)] * count
        hid_spec = [whole((rank, tok))] * count
    else:
        hid_shape = [jax.ShapeDtypeStruct((rank, count * tok), f32)]
        hid_spec = [whole((rank, count * tok))]
    keys = count * tok
    flops = nh * keys * (4 * keys * hd + 6 * 3 * tok * hd)
    out = pl.pallas_call(
        functools.partial(
            attention_kernel, count, tok, hd, slots, rank, last, total ** (-0.5)
        ),
        grid=(nh,),
        out_shape=[jax.ShapeDtypeStruct((tok, nh * hd), bf)] * count
        + [jax.ShapeDtypeStruct((nh * hd, rank), f32)]
        + hid_shape,
        in_specs=[SMEM]
        + [pl.BlockSpec((3, tok, hd), lambda h: (0, 0, h))] * count
        + [whole(notes[0].shape)] * count
        + [pl.BlockSpec((rank, hd), lambda h: (0, first + h)), whole((rank, keys))],
        out_specs=[pl.BlockSpec((tok, hd), lambda h: (0, h))] * count
        + [pl.BlockSpec((hd, rank), lambda h: (h, 0))]
        + hid_spec,
        scratch_shapes=[
            pltpu.VMEM((count, tok, hd), bf),
            pltpu.VMEM((keys, hd), bf),
            pltpu.VMEM((hd, keys), bf),
            pltpu.VMEM((count, hd, tok), bf),
            pltpu.VMEM((rank, keys), bf),
            pltpu.VMEM((count, tok, hd), f32),
            pltpu.VMEM((rank, keys), f32),
        ],
        compiler_params=params(),
        cost_estimate=pl.CostEstimate(
            flops=flops, bytes_accessed=4 * nh * keys * hd * 2, transcendentals=nh * keys * keys
        ),
        name="attention",
    )(me, *blocks, *notes, up_t, hid)
    return out[:count], out[count], out[count + 1 :]


def down_kernel(count, group, me_ref, *rest):
    parts, x_ref, outs = rest[:count], rest[count], rest[count + 1 :]
    me = me_ref[0]
    hidden = parts[0][...].astype(jnp.float32)
    for k in range(1, count):
        hidden += parts[k][...].astype(jnp.float32)
    hidden = hidden.astype(jnp.bfloat16)
    for k in range(count):
        column = pl.multiple_of((me ^ k) * group, 128)
        outs[k][...] = mm(hidden, x_ref[:, pl.ds(column, group)]).astype(jnp.bfloat16)


def down_terms(me, parts, x):
    count = len(parts)
    group = x.shape[1] // count
    rank = parts[0].shape[0]
    vm = pl.BlockSpec(memory_space=pltpu.VMEM)
    return pl.pallas_call(
        functools.partial(down_kernel, count, group),
        out_shape=[jax.ShapeDtypeStruct((rank, group), jnp.bfloat16)] * count,
        in_specs=[SMEM] + [vm] * (count + 1),
        out_specs=[vm] * count,
        compiler_params=params(),
        name="down_terms",
    )(me, *parts, x)


def sum_kernel(count, *refs):
    total = refs[0][...].astype(jnp.float32)
    for k in range(1, count):
        total += refs[k][...].astype(jnp.float32)
    refs[count][...] = total.T


def sum_terms(parts):
    rank, rows = parts[0].shape
    return pl.pallas_call(
        functools.partial(sum_kernel, len(parts)),
        out_shape=jax.ShapeDtypeStruct((rows, rank), jnp.float32),
        compiler_params=params(),
        name="sum_terms",
    )(*parts)


def head_chunks(per_group):
    if per_group < 2:
        return [(0, per_group)]
    return [(0, per_group - 1), (per_group - 1, 1)]


def local(
    queries, keys, values, value_layer_input, adapter_down_weight, adapter_up_weight, neighbors
):
    tok, model = queries.shape
    rank = adapter_down_weight.shape[1]
    count = lax.axis_size("context")
    index = lax.axis_index("context")
    me = index.astype(jnp.int32).reshape(1)
    hd = model // H
    group = model // count
    per_group = H // count
    tiles = neighbors.shape[0]
    slots = 3 * tiles
    tile = tok // tiles
    chunks = head_chunks(per_group)

    messages = [
        exchange(pack(me, queries, keys, values, count, first * hd, nh * hd), count)
        for first, nh in chunks
    ]

    lora = jnp.dot(
        value_layer_input, adapter_down_weight, preferred_element_type=jnp.float32
    ).astype(jnp.bfloat16)
    offsets = neighbors - (index - 1) * tiles
    seen = jnp.any(offsets[:, :, None] == jnp.arange(slots, dtype=jnp.int32), axis=1)
    seen = jnp.repeat(seen.T.astype(jnp.bfloat16), tile, axis=1)
    pad = -slots % 16
    note = jnp.concatenate([lora.T, jnp.pad(seen, ((0, pad), (0, 0)))], axis=0)
    notes = exchange([note] * count, count)

    up_t = lax.dynamic_slice_in_dim(adapter_up_weight, index * group, group, 0).T
    hid = jnp.zeros((rank, count * tok), jnp.float32)
    student, grad_up = [], []
    for c, (first, nh) in enumerate(chunks):
        last = c == len(chunks) - 1
        outs, gup, hid = attention(
            me, messages[c], notes, up_t, hid, first, hd, slots, last, tok * count
        )
        hid = hid if last else hid[0]
        student += exchange(outs, count)
        grad_up.append(gup)
    terms = exchange(down_terms(me, exchange(hid, count), value_layer_input), count)
    grad_down = sum_terms(terms)
    spans = [(first * hd, nh * hd) for first, nh in chunks]
    student_out = unpack(me, student, count, spans, model)
    return student_out, grad_down, jnp.concatenate(grad_up, axis=0)


def solution(mesh):
    rows = P(("video", "context"), None)
    return jax.shard_map(
        local,
        mesh=mesh,
        in_specs=(rows, rows, rows, rows, P(), P(), rows),
        out_specs=(rows, rows, rows),
        check_vma=False,
    )
```

```python
import functools
import math

import jax
import jax.numpy as jnp
from jax import lax
from jax.experimental import pallas as pl
from jax.experimental.pallas import tpu as pltpu
from jax.sharding import PartitionSpec as P

H = 32
HIDDEN = -1e30
VMEM = 48 * 1024 * 1024
NT = (((1,), (1,)), ((), ()))
TN = (((0,), (0,)), ((), ()))
NN = (((1,), (0,)), ((), ()))


def mm(a, b, dims=NN):
    return lax.dot_general(a, b, dims, preferred_element_type=jnp.float32)


def params():
    return pltpu.CompilerParams(vmem_limit_bytes=VMEM)


SMEM = pl.BlockSpec(memory_space=pltpu.SMEM)
HBM = pl.BlockSpec(memory_space=pltpu.HBM)
LANES = 128


def exchange(blocks, count, targets=None):
    got = {0: blocks[0]}
    for k in range(count - 1, 0, -1):
        pairs = [(i, i ^ k) for i in range(count) if targets is None or i ^ k in targets]
        got[k] = lax.ppermute(blocks[k], "context", pairs)
    return [got[k] for k in range(count)]


def pack_copies(count, group, hd, first, nh, me, refs, outs, sems):
    tok = refs[0].shape[0]
    copies = []
    for k in range(count):
        for h in range(nh):
            column = pl.multiple_of((me ^ k) * group + (first + h) * hd, LANES)
            for t, ref in enumerate(refs):
                n = h * 3 + t
                copies.append(
                    pltpu.make_async_copy(
                        ref.at[:, pl.ds(column, hd)],
                        outs[k].at[pl.ds(n * tok, tok), :],
                        sems.at[k * nh * 3 + n],
                    )
                )
    return copies


def pack_kernel(count, group, hd, first, nh, me_ref, q_ref, k_ref, v_ref, _, *rest):
    outs, sems = rest[:count], rest[count]
    copies = pack_copies(
        count, group, hd, first, nh, me_ref[0], (q_ref, k_ref, v_ref), outs, sems
    )
    for copy in copies:
        copy.start()
    for copy in copies:
        copy.wait()


def pack(me, q, k, v, after, count, hd, first, nh):
    tok, model = q.shape
    return pl.pallas_call(
        functools.partial(pack_kernel, count, model // count, hd, first, nh),
        out_shape=[jax.ShapeDtypeStruct((nh * 3 * tok, hd), q.dtype)] * count,
        in_specs=[SMEM, HBM, HBM, HBM, HBM],
        out_specs=[HBM] * count,
        scratch_shapes=[pltpu.SemaphoreType.DMA((3 * nh * count,))],
        compiler_params=params(),
        name="pack",
    )(me, q, k, v, after)


def first_kernel(count, group, hd, nh, mask_rows, tiles, me_ref, nb_ref, *rest):
    q_ref, k_ref, v_ref, x_ref, down_ref = rest[:5]
    outs, rest = rest[5 : 5 + count], rest[5 + count :]
    x_s, down_s, note_s, sems, in_sems, note_sems = rest
    me = me_ref[0]
    tok = q_ref.shape[0]
    rank = down_ref.shape[1]
    loads = [
        pltpu.make_async_copy(x_ref, x_s, in_sems.at[0]),
        pltpu.make_async_copy(down_ref, down_s, in_sems.at[1]),
    ]
    copies = pack_copies(count, group, hd, 0, nh, me, (q_ref, k_ref, v_ref), outs, sems)
    for copy in loads + copies:
        copy.start()
    rows = lax.broadcasted_iota(jnp.int32, (mask_rows, tok), 0)
    lane_tile = lax.broadcasted_iota(jnp.int32, (mask_rows, tok), 1) // (tok // tiles)
    seen = jnp.zeros((mask_rows, tok), jnp.float32)
    for t in range(tiles):
        for n in range(nb_ref.shape[1]):
            slot = nb_ref[t, n] - (me - 1) * tiles
            seen = jnp.where((rows == slot) & (lane_tile == t), 1.0, seen)
    note_s[rank:, :] = seen.astype(jnp.bfloat16)
    for copy in loads:
        copy.wait()
    note_s[:rank, :] = mm(x_s[...], down_s[...]).T.astype(jnp.bfloat16)
    notes = [
        pltpu.make_async_copy(
            note_s, outs[k].at[pl.ds(nh * 3 * tok, rank + mask_rows), :], note_sems.at[k]
        )
        for k in range(count)
    ]
    for copy in notes:
        copy.start()
    for copy in copies + notes:
        copy.wait()


def first_pack(me, nb, q, k, v, x, down, count, hd, nh, mask_rows):
    tok, model = q.shape
    rank = down.shape[1]
    rows = nh * 3 * tok + rank + mask_rows
    bf = q.dtype
    return pl.pallas_call(
        functools.partial(
            first_kernel, count, model // count, hd, nh, mask_rows, nb.shape[0]
        ),
        out_shape=[jax.ShapeDtypeStruct((rows, hd), bf)] * count,
        in_specs=[SMEM, SMEM] + [HBM] * 5,
        out_specs=[HBM] * count,
        scratch_shapes=[
            pltpu.VMEM(x.shape, bf),
            pltpu.VMEM(down.shape, bf),
            pltpu.VMEM((rank + mask_rows, tok), bf),
            pltpu.SemaphoreType.DMA((3 * nh * count,)),
            pltpu.SemaphoreType.DMA((2,)),
            pltpu.SemaphoreType.DMA((count,)),
        ],
        compiler_params=params(),
        name="first_pack",
    )(me, nb, q, k, v, x, down)


def assemble_kernel(count, group, me_ref, home_ref, *rest):
    refs, out, sems = rest[:count], rest[count], rest[count + 1]
    me = me_ref[0]

    @pl.when((me == count // 2 - 1) | (me == count // 2))
    def _():
        copies = []
        for k in range(count):
            column = pl.multiple_of((me ^ k) * group, LANES)
            copies.append(
                pltpu.make_async_copy(refs[k], out.at[:, pl.ds(column, group)], sems.at[k])
            )
        for copy in copies:
            copy.start()
        for copy in copies:
            copy.wait()


def assemble(me, home, blocks):
    count = len(blocks)
    return pl.pallas_call(
        functools.partial(assemble_kernel, count, home.shape[1] // count),
        out_shape=jax.ShapeDtypeStruct(home.shape, home.dtype),
        in_specs=[SMEM] + [HBM] * (count + 1),
        out_specs=HBM,
        input_output_aliases={1: 0},
        scratch_shapes=[pltpu.SemaphoreType.DMA((count,))],
        compiler_params=params(),
        name="assemble",
    )(me, home, *blocks)


def soft(scores, scale):
    top = jnp.max(scores, axis=0, keepdims=True)
    expo = jnp.exp2((scores - top) * scale)
    return expo, jnp.sum(expo, axis=0, keepdims=True)


def tile_weights(keys, query, mask, slots, scale):
    tok = query.shape[0]
    bias = (mask.astype(jnp.float32)[:slots] - 1.0) * (-HIDDEN)
    scores = mm(keys, query, NT).reshape(slots, 3 * tok // slots, tok) + bias[:, None, :]
    expo, norm = soft(scores.reshape(3 * tok, tok), scale)
    return (expo * (1.0 / norm)).astype(jnp.bfloat16)


def window(me, p, count):
    slab = me ^ p
    low = jnp.where(slab > 0, (slab - 1) ^ me, p)
    high = jnp.where(slab < count - 1, (slab + 1) ^ me, p)
    return low, p, high


def log_scale(hd):
    return hd ** (-0.5) * math.log2(math.e)


def home_kernel(count, slots, rank, me_ref, *rest):
    notes, rest = rest[:count], rest[count:]
    q_ref, k_refs, v_refs, up_ref, out_ref, note_s = (
        rest[0],
        rest[1:4],
        rest[4:7],
        rest[7],
        rest[8],
        rest[9],
    )
    hd = q_ref.shape[1]

    @pl.when(pl.program_id(0) == 0)
    def _():
        for p in range(count):
            note_s[p] = notes[p][...]

    keys = jnp.concatenate([ref[...] for ref in k_refs], axis=0)
    weights = tile_weights(keys, q_ref[...], notes[0][rank:, :], slots, log_scale(hd))
    values = []
    for ref, w in zip(v_refs, window(me_ref[0], 0, count)):
        term = mm(up_ref[...], note_s[w][:rank, :])
        values.append((ref[...].T.astype(jnp.float32) + term).astype(jnp.bfloat16))
    out_ref[...] = mm(jnp.concatenate(values, axis=1), weights).T.astype(jnp.bfloat16)


def home_student(me, notes, q, ks, vs, up, hd, slots):
    count = len(notes)
    tok, model = q.shape
    heads = model // hd
    rank = up.shape[1]
    column = pl.BlockSpec((tok, hd), lambda h: (0, h))
    return pl.pallas_call(
        functools.partial(home_kernel, count, slots, rank),
        grid=(heads,),
        out_shape=jax.ShapeDtypeStruct(q.shape, q.dtype),
        in_specs=[SMEM]
        + [pl.BlockSpec(notes[0].shape, lambda h: (0, 0))] * count
        + [column] * 7
        + [pl.BlockSpec((hd, rank), lambda h: (h, 0))],
        out_specs=column,
        scratch_shapes=[pltpu.VMEM((count,) + notes[0].shape, q.dtype)],
        compiler_params=params(),
        cost_estimate=pl.CostEstimate(
            flops=12 * 10**9, bytes_accessed=9 * tok * model * 2, transcendentals=0
        ),
        name="home_student",
    )(me, *notes, q, *ks, *vs, up)


def attention_kernel(count, tok, hd, slots, rank, before, last, factor, me_ref, *rest):
    blocks, rest = rest[:count], rest[count:]
    notes, rest = rest[:count], rest[count:]
    up_ref, hid_ref, rest = rest[0], rest[1], rest[2:]
    if before:
        given, rest = rest[:count], rest[count:]
    outs, rest = rest[:count], rest[count:]
    gup_ref, rest = rest[0], rest[1:]
    nh = count if last else 1
    hid_out, rest = rest[:nh], rest[nh:]
    q_s, k_s, vt_s, svt_s, lora_s, grad_s, hid_s, out_s = rest
    head = pl.program_id(0)
    me = me_ref[0]
    scale = log_scale(hd)

    @pl.when(head == 0)
    def _():
        hid_s[...] = hid_ref[...]
        for p in range(count):
            lora_s[:, p * tok : (p + 1) * tok] = notes[p][:rank, :]
            if before:
                outs[p][:, : before * hd] = given[p][...]

    start = pl.multiple_of(head * 3 * tok, tok)
    for p in range(count):
        q_s[p] = blocks[p][pl.ds(start, tok), :]
        k_s[p * tok : (p + 1) * tok, :] = blocks[p][pl.ds(start + tok, tok), :]
        vt_s[:, p * tok : (p + 1) * tok] = blocks[p][pl.ds(start + 2 * tok, tok), :].T
    up_t = up_ref[...]
    for p in range(count):
        cols = slice(p * tok, (p + 1) * tok)
        term = mm(up_t, lora_s[:, cols], TN)
        svt_s[p] = (vt_s[:, cols].astype(jnp.float32) + term).astype(jnp.bfloat16)
    grad_s[...] = jnp.zeros_like(grad_s)

    for p in range(count):
        query = q_s[p]
        expo, norm = soft(mm(k_s[...], query, NT), scale)
        teacher = mm(vt_s[...], expo.astype(jnp.bfloat16)) / norm
        teacher = teacher.astype(jnp.bfloat16).astype(jnp.float32)

        places = window(me, p, count)
        keys = jnp.concatenate(
            [k_s[pl.ds(pl.multiple_of(w * tok, tok), tok), :] for w in places], axis=0
        )
        weights = tile_weights(keys, query, notes[p][rank:, :], slots, scale)
        values = jnp.concatenate([svt_s[w] for w in places], axis=1)
        student = mm(values, weights)
        out_s[p] = student.T.astype(jnp.bfloat16)
        delta = ((student - teacher) * factor).astype(jnp.bfloat16)
        grads = mm(weights, delta, NT)
        for n, w in enumerate(places):
            grad_s[w] += grads[n * tok : (n + 1) * tok]

    column = pl.multiple_of((before + head) * hd, LANES)
    for p in range(count):
        outs[p][:, pl.ds(column, hd)] = out_s[p]
    grad = grad_s[...].reshape(count * tok, hd).astype(jnp.bfloat16)
    gup_ref[...] = mm(lora_s[...], grad).T
    hid_s[...] += mm(up_t, grad, NT)

    @pl.when(head == pl.num_programs(0) - 1)
    def _():
        if last:
            for p in range(count):
                hid_out[p][...] = hid_s[:, p * tok : (p + 1) * tok].astype(jnp.bfloat16)
        else:
            hid_out[0][...] = hid_s[...]


def attention(me, blocks, notes, up_t, hid, given, first, nh, tok, hd, slots, last):
    count = len(blocks)
    rank = up_t.shape[0]
    bf, f32 = jnp.bfloat16, jnp.float32
    whole = lambda shape: pl.BlockSpec(shape, lambda h: (0,) * len(shape))
    if last:
        hid_shape = [jax.ShapeDtypeStruct((rank, tok), bf)] * count
    else:
        hid_shape = [jax.ShapeDtypeStruct((rank, count * tok), f32)]
    keys = count * tok
    wide = (first + nh) * hd
    out = pl.pallas_call(
        functools.partial(
            attention_kernel, count, tok, hd, slots, rank, first, last, keys ** (-0.5)
        ),
        grid=(nh,),
        out_shape=[jax.ShapeDtypeStruct((tok, wide), bf)] * count
        + [jax.ShapeDtypeStruct((nh * hd, rank), f32)]
        + hid_shape,
        in_specs=[SMEM]
        + [whole(blocks[0].shape)] * count
        + [whole(notes[0].shape)] * count
        + [pl.BlockSpec((rank, hd), lambda h: (0, first + h)), whole((rank, keys))]
        + [whole(g.shape) for g in given],
        out_specs=[whole((tok, wide))] * count
        + [pl.BlockSpec((hd, rank), lambda h: (h, 0))]
        + [whole(s.shape) for s in hid_shape],
        scratch_shapes=[
            pltpu.VMEM((count, tok, hd), bf),
            pltpu.VMEM((keys, hd), bf),
            pltpu.VMEM((hd, keys), bf),
            pltpu.VMEM((count, hd, tok), bf),
            pltpu.VMEM((rank, keys), bf),
            pltpu.VMEM((count, tok, hd), f32),
            pltpu.VMEM((rank, keys), f32),
            pltpu.VMEM((count, tok, hd), bf),
        ],
        compiler_params=params(),
        cost_estimate=pl.CostEstimate(
            flops=nh * 6 * 10**9, bytes_accessed=4 * nh * keys * hd * 2, transcendentals=0
        ),
        name="attention",
    )(me, *blocks, *notes, up_t, hid, *given)
    return out[:count], out[count], out[count + 1 :]


def down_kernel(count, group, me_ref, *rest):
    parts, x_ref, outs = rest[:count], rest[count], rest[count + 1 :]
    me = me_ref[0]
    hidden = parts[0][...].astype(jnp.float32)
    for k in range(1, count):
        hidden += parts[k][...].astype(jnp.float32)
    hidden = hidden.astype(jnp.bfloat16)
    for k in range(count):
        column = pl.multiple_of((me ^ k) * group, 128)
        outs[k][...] = mm(hidden, x_ref[:, pl.ds(column, group)]).astype(jnp.bfloat16)


def down_terms(me, parts, x):
    count = len(parts)
    group = x.shape[1] // count
    rank = parts[0].shape[0]
    vm = pl.BlockSpec(memory_space=pltpu.VMEM)
    return pl.pallas_call(
        functools.partial(down_kernel, count, group),
        out_shape=[jax.ShapeDtypeStruct((rank, group), jnp.bfloat16)] * count,
        in_specs=[SMEM] + [vm] * (count + 1),
        out_specs=[vm] * count,
        compiler_params=params(),
        name="down_terms",
    )(me, *parts, x)


def sum_kernel(count, *refs):
    total = refs[0][...].astype(jnp.float32)
    for k in range(1, count):
        total += refs[k][...].astype(jnp.float32)
    refs[count][...] = total.T


def sum_terms(parts):
    rank, rows = parts[0].shape
    return pl.pallas_call(
        functools.partial(sum_kernel, len(parts)),
        out_shape=jax.ShapeDtypeStruct((rows, rank), jnp.float32),
        compiler_params=params(),
        name="sum_terms",
    )(*parts)


def head_chunks(per_group):
    if per_group < 2:
        return [(0, per_group)]
    return [(0, per_group - 1), (per_group - 1, 1)]


def local(
    queries, keys, values, value_layer_input, adapter_down_weight, adapter_up_weight, neighbors
):
    tok, model = queries.shape
    rank = adapter_down_weight.shape[1]
    count = lax.axis_size("context")
    index = lax.axis_index("context")
    me = index.astype(jnp.int32).reshape(1)
    hd = model // H
    group = model // count
    per_group = H // count
    tiles = neighbors.shape[0]
    slots = 3 * tiles
    chunks = head_chunks(per_group)

    mask_rows = slots + -slots % 16

    rows = chunks[0][1] * 3 * tok
    messages = []
    for c, (first, nh) in enumerate(chunks):
        if c == 0:
            blocks = first_pack(
                me, neighbors, queries, keys, values, value_layer_input, adapter_down_weight,
                count, hd, nh, mask_rows,
            )
        else:
            after = messages[-1][-1]
            blocks = pack(me, queries, keys, values, after, count, hd, first, nh)
        messages.append(exchange(blocks, count))
    notes = [message[rows:] for message in messages[0]]

    half = count // 2
    up_pairs = [(i, i + 1) for i in range(count - 1) if i + 1 != half]
    down_pairs = [(i + 1, i) for i, _ in up_pairs]

    def halo(array):
        low = lax.ppermute(array, "context", up_pairs)
        return low, array, lax.ppermute(array, "context", down_pairs)

    home = home_student(
        me, notes, queries, halo(keys), halo(values), adapter_up_weight, hd, slots
    )

    up_t = lax.dynamic_slice_in_dim(adapter_up_weight, index * group, group, 0).T
    hid = jnp.zeros((rank, count * tok), jnp.float32)
    outs, grad_up = [], []
    for c, (first, nh) in enumerate(chunks):
        last = c == len(chunks) - 1
        outs, gup, hid = attention(
            me, messages[c], notes, up_t, hid, outs, first, nh, tok, hd, slots, last
        )
        hid = hid if last else hid[0]
        grad_up.append(gup)
    terms = exchange(down_terms(me, exchange(hid, count), value_layer_input), count)
    grad_down = sum_terms(terms)
    student_out = assemble(me, home, exchange(outs, count, (half - 1, half)))
    return student_out, grad_down, jnp.concatenate(grad_up, axis=0)


def solution(mesh):
    rows = P(("video", "context"), None)
    return jax.shard_map(
        local,
        mesh=mesh,
        in_specs=(rows, rows, rows, rows, P(), P(), rows),
        out_specs=(rows, rows, rows),
        check_vma=False,
    )
```

```python
import functools
import math

import jax
import jax.numpy as jnp
from jax import lax
from jax.experimental import pallas as pl
from jax.experimental.pallas import tpu as pltpu
from jax.sharding import PartitionSpec as P

H = 32
HIDDEN = -1e30
VMEM = 60 * 1024 * 1024
NT = (((1,), (1,)), ((), ()))
TN = (((0,), (0,)), ((), ()))
NN = (((1,), (0,)), ((), ()))


def mm(a, b, dims=NN):
    return lax.dot_general(a, b, dims, preferred_element_type=jnp.float32)


def params():
    return pltpu.CompilerParams(vmem_limit_bytes=VMEM)


SMEM = pl.BlockSpec(memory_space=pltpu.SMEM)
HBM = pl.BlockSpec(memory_space=pltpu.HBM)
LANES = 128


def swap(block, count, bits, targets=None):
    pairs = [(i, i ^ bits) for i in range(count) if targets is None or i ^ bits in targets]
    return lax.ppermute(block, "context", pairs)


def exchange(blocks, count):
    got = {0: blocks[0]}
    for k in range(count - 1, 0, -1):
        got[k] = swap(blocks[k], count, k)
    return [got[k] for k in range(count)]


def pack_copies(count, group, hd, first, nh, me, refs, outs, sems):
    tok = refs[0].shape[0]
    copies = []
    for k in range(count):
        for h in range(nh):
            column = pl.multiple_of((me ^ k) * group + (first + h) * hd, LANES)
            for t, ref in enumerate(refs):
                n = h * 3 + t
                copies.append(
                    pltpu.make_async_copy(
                        ref.at[:, pl.ds(column, hd)],
                        outs[k].at[pl.ds(n * tok, tok), :],
                        sems.at[k * nh * 3 + n],
                    )
                )
    return copies


def pack_kernel(count, group, hd, first, nh, me_ref, q_ref, k_ref, v_ref, _, *rest):
    outs, sems = rest[:count], rest[count]
    copies = pack_copies(
        count, group, hd, first, nh, me_ref[0], (q_ref, k_ref, v_ref), outs, sems
    )
    for copy in copies:
        copy.start()
    for copy in copies:
        copy.wait()


def pack(me, q, k, v, after, count, hd, first, nh):
    tok, model = q.shape
    return pl.pallas_call(
        functools.partial(pack_kernel, count, model // count, hd, first, nh),
        out_shape=[jax.ShapeDtypeStruct((nh * 3 * tok, hd), q.dtype)] * count,
        in_specs=[SMEM, HBM, HBM, HBM, HBM],
        out_specs=[HBM] * count,
        scratch_shapes=[pltpu.SemaphoreType.DMA((3 * nh * count,))],
        compiler_params=params(),
        name="pack",
    )(me, q, k, v, after)


def first_kernel(count, group, hd, nh, mask_rows, tiles, me_ref, nb_ref, *rest):
    q_ref, k_ref, v_ref, x_ref, down_ref = rest[:5]
    outs, rest = rest[5 : 5 + count], rest[5 + count :]
    x_s, down_s, note_s, sems, in_sems, note_sems = rest
    me = me_ref[0]
    tok = q_ref.shape[0]
    rank = down_ref.shape[0]
    loads = [
        pltpu.make_async_copy(x_ref, x_s, in_sems.at[0]),
        pltpu.make_async_copy(down_ref, down_s, in_sems.at[1]),
    ]
    copies = pack_copies(count, group, hd, 0, nh, me, (q_ref, k_ref, v_ref), outs, sems)
    for copy in loads + copies:
        copy.start()
    rows = lax.broadcasted_iota(jnp.int32, (mask_rows, tok), 0)
    lane_tile = lax.broadcasted_iota(jnp.int32, (mask_rows, tok), 1) // (tok // tiles)
    seen = jnp.zeros((mask_rows, tok), jnp.float32)
    for t in range(tiles):
        for n in range(nb_ref.shape[1]):
            slot = nb_ref[t, n] - (me - 1) * tiles
            seen = jnp.where((rows == slot) & (lane_tile == t), 1.0, seen)
    note_s[rank:, :] = seen.astype(jnp.bfloat16)
    for copy in loads:
        copy.wait()
    note_s[:rank, :] = mm(down_s[...], x_s[...], NT).astype(jnp.bfloat16)
    notes = [
        pltpu.make_async_copy(
            note_s, outs[k].at[pl.ds(nh * 3 * tok, rank + mask_rows), :], note_sems.at[k]
        )
        for k in range(count)
    ]
    for copy in notes:
        copy.start()
    for copy in copies + notes:
        copy.wait()


def first_pack(me, nb, q, k, v, x, down, count, hd, nh, mask_rows):
    tok, model = q.shape
    rank = down.shape[0]
    rows = nh * 3 * tok + rank + mask_rows
    bf = q.dtype
    return pl.pallas_call(
        functools.partial(
            first_kernel, count, model // count, hd, nh, mask_rows, nb.shape[0]
        ),
        out_shape=[jax.ShapeDtypeStruct((rows, hd), bf)] * count,
        in_specs=[SMEM, SMEM] + [HBM] * 5,
        out_specs=[HBM] * count,
        scratch_shapes=[
            pltpu.VMEM(x.shape, bf),
            pltpu.VMEM(down.shape, bf),
            pltpu.VMEM((rank + mask_rows, tok), bf),
            pltpu.SemaphoreType.DMA((3 * nh * count,)),
            pltpu.SemaphoreType.DMA((2,)),
            pltpu.SemaphoreType.DMA((count,)),
        ],
        compiler_params=params(),
        name="first_pack",
    )(me, nb, q, k, v, x, down)


def assemble_kernel(count, group, me_ref, home_ref, *rest):
    refs, out, sems = rest[: count // 2], rest[count // 2], rest[count // 2 + 1]
    me = me_ref[0]

    @pl.when((me == count // 2 - 1) | (me == count // 2))
    def _():
        copies = []
        for k in range(count):
            column = pl.multiple_of((me ^ k) * group, LANES)
            copies.append(
                pltpu.make_async_copy(
                    refs[k // 2].at[k % 2], out.at[:, pl.ds(column, group)], sems.at[k]
                )
            )
        for copy in copies:
            copy.start()
        for copy in copies:
            copy.wait()


def assemble(me, home, blocks):
    count = 2 * len(blocks)
    return pl.pallas_call(
        functools.partial(assemble_kernel, count, home.shape[1] // count),
        out_shape=jax.ShapeDtypeStruct(home.shape, home.dtype),
        in_specs=[SMEM] + [HBM] * (len(blocks) + 1),
        out_specs=HBM,
        input_output_aliases={1: 0},
        scratch_shapes=[pltpu.SemaphoreType.DMA((count,))],
        compiler_params=params(),
        name="assemble",
    )(me, home, *blocks)


def soft(scores, scale):
    top = jnp.max(scores, axis=0, keepdims=True)
    expo = jnp.exp2((scores - top) * scale)
    return expo, jnp.sum(expo, axis=0, keepdims=True)


def tile_weights(keys, query, mask, slots, scale):
    tok = query.shape[0]
    bias = (mask.astype(jnp.float32)[:slots] - 1.0) * (-HIDDEN)
    scores = mm(keys, query, NT).reshape(slots, 3 * tok // slots, tok) + bias[:, None, :]
    expo, norm = soft(scores.reshape(3 * tok, tok), scale)
    return (expo * (1.0 / norm)).astype(jnp.bfloat16)


def window(me, p, count):
    slab = me ^ p
    low = jnp.where(slab > 0, (slab - 1) ^ me, p)
    high = jnp.where(slab < count - 1, (slab + 1) ^ me, p)
    return low, p, high


def log_scale(hd):
    return hd ** (-0.5) * math.log2(math.e)


def home_kernel(count, slots, rank, hd, me_ref, *rest):
    notes, rest = rest[:count], rest[count:]
    q_ref, k_ref, v_ref, low_ref, high_ref, up_ref, out_ref, note_s, sems = rest
    tok = q_ref.shape[0]

    @pl.when(pl.program_id(0) == 0)
    def _():
        size = note_s.shape[1]
        copies = [
            pltpu.make_async_copy(
                ref.at[pl.ds(ref.shape[0] - size, size), :], note_s.at[p], sems.at[p]
            )
            for p, ref in enumerate(notes)
        ]
        for copy in copies:
            copy.start()
        for copy in copies:
            copy.wait()

    mask = note_s[0][rank:, :]
    loras = [note_s[w][:rank, :] for w in window(me_ref[0], 0, count)]
    for h in range(q_ref.shape[1] // hd):
        cols = slice(h * hd, (h + 1) * hd)
        keys = jnp.concatenate([low_ref[0, :, cols], k_ref[:, cols], high_ref[0, :, cols]], axis=0)
        weights = tile_weights(keys, q_ref[:, cols], mask, slots, log_scale(hd))
        values = []
        for value, lora in zip((low_ref[1, :, cols], v_ref[:, cols], high_ref[1, :, cols]), loras):
            term = mm(up_ref[:, cols], lora, TN)
            values.append((value.T.astype(jnp.float32) + term).astype(jnp.bfloat16))
        student = mm(jnp.concatenate(values, axis=1), weights)
        out_ref[:, cols] = student.T.astype(jnp.bfloat16)


def home_student(me, messages, mask_rows, q, k, v, low, high, up_t, hd, slots):
    count = len(messages)
    tok, model = q.shape
    rank = up_t.shape[0]
    width = min(4 * hd, model)
    column = pl.BlockSpec((tok, width), lambda h: (0, h))
    pair = pl.BlockSpec((2, tok, width), lambda h: (0, 0, h))
    return pl.pallas_call(
        functools.partial(home_kernel, count, slots, rank, hd),
        grid=(model // width,),
        out_shape=jax.ShapeDtypeStruct(q.shape, q.dtype),
        in_specs=[SMEM]
        + [HBM] * count
        + [column] * 3
        + [pair] * 2
        + [pl.BlockSpec((rank, width), lambda h: (0, h))],
        out_specs=column,
        scratch_shapes=[
            pltpu.VMEM((count, rank + mask_rows, tok), q.dtype),
            pltpu.SemaphoreType.DMA((count,)),
        ],
        compiler_params=params(),
        cost_estimate=pl.CostEstimate(
            flops=12 * 10**9, bytes_accessed=9 * tok * model * 2, transcendentals=0
        ),
        name="home_student",
    )(me, *messages, q, k, v, low, high, up_t)


def attention_kernel(
    count, tok, hd, nh, slots, rank, before, last, factor, sizes, me_ref, *rest
):
    blocks, rest = rest[:count], rest[count:]
    noted, rest = rest[:count], rest[count:]
    up_ref, _, rest = rest[0], rest[1], rest[2:]
    if before:
        (hid_ref, gup_in, out_in), rest = rest[:3], rest[3:]
    if last:
        keep_ref, send_ref, hid_keep, hid_send, gup_ref, rest = *rest[:5], rest[5:]
    else:
        hid_ref_out, gup_ref, out_ref, rest = *rest[:3], rest[3:]
    b_s, note_s, q_s, k_s, vt_s, svt_s, lora_s, grad_s, hid_s, out_s, sems, note_sems = rest
    head = pl.program_id(0)
    me = me_ref[0]
    scale = log_scale(hd)
    size, rows = note_s.shape[1], 3 * tok

    def block_copies(h):
        return [
            pltpu.make_async_copy(
                blocks[p].at[pl.ds(pl.multiple_of(h * rows, rows), rows), :],
                b_s.at[lax.rem(h, 2), p],
                sems.at[lax.rem(h, 2), p],
            )
            for p in range(count)
        ]

    @pl.when(head == 0)
    def _():
        copies = [
            pltpu.make_async_copy(
                ref.at[pl.ds(sizes - size, size), :], note_s.at[p], note_sems.at[p]
            )
            for p, ref in enumerate(noted)
        ]
        for copy in copies + block_copies(0):
            copy.start()
        for copy in copies:
            copy.wait()
        for p in range(count):
            lora_s[:, p * tok : (p + 1) * tok] = note_s[p, :rank, :]
        if before:
            hid_s[...] = hid_ref[...]
            gup_ref[:, : before * hd] = gup_in[...]
            out_s[:before] = out_in[...]
        else:
            hid_s[...] = jnp.zeros_like(hid_s)

    @pl.when(head + 1 < nh)
    def _():
        for copy in block_copies(head + 1):
            copy.start()

    for copy in block_copies(head):
        copy.wait()
    at = lax.rem(head, 2)
    for p in range(count):
        q_s[p * tok : (p + 1) * tok, :] = b_s[at, p, :tok, :]
        k_s[p * tok : (p + 1) * tok, :] = b_s[at, p, tok : 2 * tok, :]
        vt_s[:, p * tok : (p + 1) * tok] = b_s[at, p, 2 * tok :, :].T
    up_t = up_ref[...]
    for p in range(count):
        cols = slice(p * tok, (p + 1) * tok)
        term = mm(up_t, lora_s[:, cols], TN)
        svt_s[p] = (vt_s[:, cols].astype(jnp.float32) + term).astype(jnp.bfloat16)
    grad_s[...] = jnp.zeros_like(grad_s)

    for pair in range(count // 2):
        queries = q_s[2 * pair * tok : 2 * (pair + 1) * tok, :]
        expo, norm = soft(mm(k_s[...], queries, NT), scale)
        teachers = mm(vt_s[...], expo.astype(jnp.bfloat16)) / norm
        teachers = teachers.astype(jnp.bfloat16).astype(jnp.float32)
        for p in (2 * pair, 2 * pair + 1):
            teacher = teachers[:, (p % 2) * tok : (p % 2 + 1) * tok]
            places = window(me, p, count)
            keys = jnp.concatenate(
                [k_s[pl.ds(pl.multiple_of(w * tok, tok), tok), :] for w in places], axis=0
            )
            query = q_s[p * tok : (p + 1) * tok, :]
            weights = tile_weights(keys, query, note_s[p, rank:, :], slots, scale)
            values = jnp.concatenate([svt_s[w] for w in places], axis=1)
            student = mm(values, weights)
            out_s[before + head, p] = student.astype(jnp.bfloat16)
            delta = ((student - teacher) * factor).astype(jnp.bfloat16)
            grads = mm(weights, delta, NT)
            for n, w in enumerate(places):
                grad_s[w] += grads[n * tok : (n + 1) * tok]

    grad = grad_s[...].reshape(count * tok, hd).astype(jnp.bfloat16)
    column = pl.multiple_of((before + head) * hd, LANES)
    gup_ref[:, pl.ds(column, hd)] = mm(lora_s[...], grad)
    hid_s[...] += mm(up_t, grad, NT)

    @pl.when(head == nh - 1)
    def _():
        if last:
            for m in range(count // 2):
                to = slice(m * tok, (m + 1) * tok)
                hid_keep[:, to] = hid_s[:, 2 * m * tok : (2 * m + 1) * tok]
                odd = hid_s[:, (2 * m + 1) * tok : (2 * m + 2) * tok]
                hid_send[:, to] = odd.astype(jnp.bfloat16)
            core = lax.rem(me, 2)
            half = count // 2
            same = jnp.where(core == (half - 1) % 2, half - 1, half)
            other = jnp.where(core == (half - 1) % 2, half, half - 1)
            for ref, slab in ((keep_ref, same), (send_ref, other)):
                for h in range(before + nh):
                    ref[:, h * hd : (h + 1) * hd] = out_s[h, me ^ slab].T
        else:
            hid_ref_out[...] = hid_s[...]
            out_ref[...] = out_s[...]


def attention(me, blocks, noted, up_t, after, given, first, nh, tok, hd, slots, mask_rows, last):
    count = len(blocks)
    rank = up_t.shape[0]
    bf, f32 = jnp.bfloat16, jnp.float32
    whole = lambda shape: pl.BlockSpec(shape, lambda h: (0,) * len(shape))
    keys = count * tok
    heads = first + nh
    shapes = [
        jax.ShapeDtypeStruct((rank, keys), f32),
        jax.ShapeDtypeStruct((rank, heads * hd), f32),
        jax.ShapeDtypeStruct((heads, count, hd, tok), bf),
    ]
    if last:
        shapes = [
            jax.ShapeDtypeStruct((tok, heads * hd), bf),
            jax.ShapeDtypeStruct((tok, heads * hd), bf),
            jax.ShapeDtypeStruct((rank, keys // 2), f32),
            jax.ShapeDtypeStruct((rank, keys // 2), bf),
            jax.ShapeDtypeStruct((rank, heads * hd), f32),
        ]
    return pl.pallas_call(
        functools.partial(
            attention_kernel,
            count,
            tok,
            hd,
            nh,
            slots,
            rank,
            first,
            last,
            keys ** (-0.5),
            noted[0].shape[0],
        ),
        grid=(nh,),
        out_shape=shapes,
        in_specs=[SMEM]
        + [HBM] * (2 * count)
        + [pl.BlockSpec((rank, hd), lambda h: (0, first + h)), HBM]
        + [whole(g.shape) for g in given],
        out_specs=[whole(s.shape) for s in shapes],
        scratch_shapes=[
            pltpu.VMEM((2, count, 3 * tok, hd), bf),
            pltpu.VMEM((count, rank + mask_rows, tok), bf),
            pltpu.VMEM((keys, hd), bf),
            pltpu.VMEM((keys, hd), bf),
            pltpu.VMEM((hd, keys), bf),
            pltpu.VMEM((count, hd, tok), bf),
            pltpu.VMEM((rank, keys), bf),
            pltpu.VMEM((count, tok, hd), f32),
            pltpu.VMEM((rank, keys), f32),
            pltpu.VMEM((heads, count, hd, tok), bf),
            pltpu.SemaphoreType.DMA((2, count)),
            pltpu.SemaphoreType.DMA((count,)),
        ],
        compiler_params=params(),
        cost_estimate=pl.CostEstimate(
            flops=nh * 6 * 10**9, bytes_accessed=4 * nh * keys * hd * 2, transcendentals=0
        ),
        name="attention",
    )(me, *blocks, *noted, up_t, after, *given)


VM = pl.BlockSpec(memory_space=pltpu.VMEM)


def pair_kernel(parts, keep_ref, got_ref, *outs):
    width = keep_ref.shape[1] // parts
    for m in range(parts):
        cols = slice(m * width, (m + 1) * width)
        total = keep_ref[:, cols] + got_ref[:, cols].astype(jnp.float32)
        outs[m][...] = total.astype(outs[m].dtype)


def pair_sum(keep, got, parts):
    rank, width = keep.shape[0], keep.shape[1] // parts
    shapes = [
        jax.ShapeDtypeStruct((rank, width), jnp.bfloat16 if m else jnp.float32)
        for m in range(parts)
    ]
    return pl.pallas_call(
        functools.partial(pair_kernel, parts),
        out_shape=shapes,
        in_specs=[VM, VM],
        out_specs=[VM] * parts,
        compiler_params=params(),
        name="pair_sum",
    )(keep, got)


def chip_terms(keep, send, count):
    totals = pair_sum(keep, swap(send, count, 1), count // 2)
    got = {m: swap(totals[m], count, 2 * m) for m in range(count // 2 - 1, 0, -1)}
    return [totals[0]] + [got[m] for m in range(1, count // 2)]


def down_kernel(count, group, me_ref, *rest):
    parts = rest[: count // 2]
    x_ref, keep_ref, send_ref = rest[count // 2 :]
    me = me_ref[0]
    hidden = parts[0][...]
    for part in parts[1:]:
        hidden += part[...].astype(jnp.float32)
    hidden = hidden.astype(jnp.bfloat16)
    for k in range(count):
        column = pl.multiple_of((me ^ k) * group, LANES)
        term = mm(hidden, x_ref[:, pl.ds(column, group)])
        to = (send_ref, keep_ref)[k % 2 == 0]
        to[:, k // 2 * group : (k // 2 + 1) * group] = term.astype(to.dtype)


def down_terms(me, parts, x):
    count = 2 * len(parts)
    model = x.shape[1]
    rank = parts[0].shape[0]
    return pl.pallas_call(
        functools.partial(down_kernel, count, model // count),
        out_shape=[
            jax.ShapeDtypeStruct((rank, model // 2), jnp.float32),
            jax.ShapeDtypeStruct((rank, model // 2), jnp.bfloat16),
        ],
        in_specs=[SMEM] + [VM] * (len(parts) + 1),
        out_specs=[VM, VM],
        compiler_params=params(),
        name="down_terms",
    )(me, *parts, x)


def sum_kernel(*refs):
    total = refs[0][...]
    for ref in refs[1:-1]:
        total += ref[...].astype(jnp.float32)
    refs[-1][...] = total


def sum_terms(parts):
    return pl.pallas_call(
        sum_kernel,
        out_shape=jax.ShapeDtypeStruct(parts[0].shape, jnp.float32),
        in_specs=[VM] * len(parts),
        out_specs=VM,
        compiler_params=params(),
        name="sum_terms",
    )(*parts)


def head_chunks(per_group):
    if per_group < 2:
        return [(0, per_group)]
    return [(0, per_group - 1), (per_group - 1, 1)]


def local(
    queries, keys, values, value_layer_input, adapter_down_weight, adapter_up_weight, neighbors
):
    tok, model = queries.shape
    rank = adapter_down_weight.shape[1]
    count = lax.axis_size("context")
    index = lax.axis_index("context")
    me = index.astype(jnp.int32).reshape(1)
    hd = model // H
    group = model // count
    per_group = H // count
    tiles = neighbors.shape[0]
    slots = 3 * tiles
    chunks = head_chunks(per_group)

    mask_rows = slots + -slots % 16

    down_t = adapter_down_weight.T
    up_t = adapter_up_weight.T

    messages = []
    for c, (first, nh) in enumerate(chunks):
        if c == 0:
            blocks = first_pack(
                me, neighbors, queries, keys, values, value_layer_input, down_t,
                count, hd, nh, mask_rows,
            )
        else:
            after = messages[-1][-1]
            blocks = pack(me, queries, keys, values, after, count, hd, first, nh)
        messages.append(exchange(blocks, count))
    noted = messages[0]

    half = count // 2
    ups = [(i, i + 1) for i in range(count - 1) if i + 1 != half]
    both = jnp.stack([keys, values])
    low = lax.ppermute(both, "context", ups)
    high = lax.ppermute(both, "context", [(j, i) for i, j in ups])
    home = home_student(
        me, noted, mask_rows, queries, keys, values, low, high, up_t, hd, slots
    )

    own_up = lax.dynamic_slice_in_dim(up_t, index * group, group, 1)
    given = []
    for c, (first, nh) in enumerate(chunks):
        last = c == len(chunks) - 1
        given = attention(
            me, messages[c], noted, own_up, home, given, first, nh, tok, hd, slots, mask_rows, last
        )
    keep, send, hid_keep, hid_send, grad_up = given
    hidden = chip_terms(hid_keep, hid_send, count)
    grad_down = sum_terms(chip_terms(*down_terms(me, hidden, value_layer_input), count))

    middle = jnp.stack([keep, swap(send, count, 1)])
    blocks = [middle] + [swap(middle, count, 2 * m, (half - 1, half)) for m in range(1, half)]
    return assemble(me, home, blocks), grad_down.T, grad_up.T


def solution(mesh):
    rows = P(("video", "context"), None)
    return jax.shard_map(
        local,
        mesh=mesh,
        in_specs=(rows, rows, rows, rows, P(), P(), rows),
        out_specs=(rows, rows, rows),
        check_vma=False,
    )
```

```python
import functools
import math

import jax
import jax.numpy as jnp
from jax import lax
from jax.experimental import pallas as pl
from jax.experimental.pallas import tpu as pltpu
from jax.sharding import PartitionSpec as P

H = 32
HIDDEN = -1e30
NT = (((1,), (1,)), ((), ()))
TN = (((0,), (0,)), ((), ()))
NN = (((1,), (0,)), ((), ()))


def mm(a, b, dims=NN):
    return lax.dot_general(a, b, dims, preferred_element_type=jnp.float32)


def params(mib):
    return pltpu.CompilerParams(vmem_limit_bytes=mib * 1024 * 1024)


SMEM = pl.BlockSpec(memory_space=pltpu.SMEM)
HBM = pl.BlockSpec(memory_space=pltpu.HBM)
ANY = pl.BlockSpec(memory_space=pl.ANY)
VM = pl.BlockSpec(memory_space=pltpu.VMEM)
LANES = 128


def swap(block, count, bits, targets=None):
    pairs = [(i, i ^ bits) for i in range(count) if targets is None or i ^ bits in targets]
    return lax.ppermute(block, "context", pairs)


def exchange(blocks, count):
    got = {0: blocks[0]}
    for k in range(count - 1, 0, -1):
        got[k] = swap(blocks[k], count, k)
    return [got[k] for k in range(count)]


def pack_copies(count, group, hd, first, nh, me, refs, outs, sems):
    tok = refs[0].shape[0]
    copies = []
    for k in range(count):
        for h in range(nh):
            column = pl.multiple_of((me ^ k) * group + (first + h) * hd, LANES)
            for t, ref in enumerate(refs):
                n = h * 3 + t
                copies.append(
                    pltpu.make_async_copy(
                        ref.at[:, pl.ds(column, hd)],
                        outs[k].at[pl.ds(n * tok, tok), :],
                        sems.at[k * nh * 3 + n],
                    )
                )
    return copies


def pack_kernel(count, group, hd, first, nh, me_ref, q_ref, k_ref, v_ref, _, *rest):
    outs, sems = rest[:count], rest[count]
    copies = pack_copies(
        count, group, hd, first, nh, me_ref[0], (q_ref, k_ref, v_ref), outs, sems
    )
    for copy in copies:
        copy.start()
    for copy in copies:
        copy.wait()


def pack(me, q, k, v, after, count, hd, first, nh):
    tok, model = q.shape
    return pl.pallas_call(
        functools.partial(pack_kernel, count, model // count, hd, first, nh),
        out_shape=[jax.ShapeDtypeStruct((nh * 3 * tok, hd), q.dtype)] * count,
        in_specs=[SMEM, VM, VM, VM, ANY],
        out_specs=[ANY] * count,
        scratch_shapes=[pltpu.SemaphoreType.DMA((3 * nh * count,))],
        compiler_params=params(4),
        name="pack",
    )(me, q, k, v, after)


def first_kernel(count, group, hd, nh, mask_rows, tiles, me_ref, nb_ref, *rest):
    q_ref, k_ref, v_ref, x_ref, down_ref = rest[:5]
    outs, rest = rest[5 : 5 + count], rest[5 + count :]
    q_s, k_s, v_s, x_s, down_s, note_s, sems, in_sems, note_sems = rest
    me = me_ref[0]
    tok = q_ref.shape[0]
    rank = down_ref.shape[0]
    pairs = ((q_ref, q_s), (k_ref, k_s), (v_ref, v_s), (x_ref, x_s), (down_ref, down_s))
    loads = [
        pltpu.make_async_copy(ref, to, in_sems.at[n]) for n, (ref, to) in enumerate(pairs)
    ]
    for copy in loads:
        copy.start()
    rows = lax.broadcasted_iota(jnp.int32, (mask_rows, tok), 0)
    lane_tile = lax.broadcasted_iota(jnp.int32, (mask_rows, tok), 1) // (tok // tiles)
    seen = jnp.zeros((mask_rows, tok), jnp.float32)
    for t in range(tiles):
        for n in range(nb_ref.shape[1]):
            slot = nb_ref[t, n] - (me - 1) * tiles
            seen = jnp.where((rows == slot) & (lane_tile == t), 1.0, seen)
    note_s[rank:, :] = seen.astype(jnp.bfloat16)
    for copy in loads[:3]:
        copy.wait()
    copies = pack_copies(count, group, hd, 0, nh, me, (q_s, k_s, v_s), outs, sems)
    for copy in copies:
        copy.start()
    for copy in loads[3:]:
        copy.wait()
    note_s[:rank, :] = mm(down_s[...], x_s[...], NT).astype(jnp.bfloat16)
    notes = [
        pltpu.make_async_copy(
            note_s, outs[k].at[pl.ds(nh * 3 * tok, rank + mask_rows), :], note_sems.at[k]
        )
        for k in range(count)
    ]
    for copy in notes:
        copy.start()
    for copy in copies + notes:
        copy.wait()


def first_pack(me, nb, q, k, v, x, down, count, hd, nh, mask_rows):
    tok, model = q.shape
    rank = down.shape[0]
    rows = nh * 3 * tok + rank + mask_rows
    bf = q.dtype
    return pl.pallas_call(
        functools.partial(
            first_kernel, count, model // count, hd, nh, mask_rows, nb.shape[0]
        ),
        out_shape=[jax.ShapeDtypeStruct((rows, hd), bf)] * count,
        in_specs=[SMEM, SMEM] + [HBM] * 5,
        out_specs=[HBM] * count,
        scratch_shapes=[pltpu.VMEM(x.shape, bf)] * 4
        + [
            pltpu.VMEM(down.shape, bf),
            pltpu.VMEM((rank + mask_rows, tok), bf),
            pltpu.SemaphoreType.DMA((3 * nh * count,)),
            pltpu.SemaphoreType.DMA((5,)),
            pltpu.SemaphoreType.DMA((count,)),
        ],
        compiler_params=params(60),
        name="first_pack",
    )(me, nb, q, k, v, x, down)


def assemble_kernel(count, group, me_ref, home_ref, *rest):
    refs, out, sems = rest[: count // 2], rest[count // 2], rest[count // 2 + 1]
    me = me_ref[0]

    @pl.when((me == count // 2 - 1) | (me == count // 2))
    def _():
        copies = []
        for k in range(count):
            column = pl.multiple_of((me ^ k) * group, LANES)
            copies.append(
                pltpu.make_async_copy(
                    refs[k // 2].at[k % 2], out.at[:, pl.ds(column, group)], sems.at[k]
                )
            )
        for copy in copies:
            copy.start()
        for copy in copies:
            copy.wait()


def assemble(me, home, blocks):
    count = 2 * len(blocks)
    return pl.pallas_call(
        functools.partial(assemble_kernel, count, home.shape[1] // count),
        out_shape=jax.ShapeDtypeStruct(home.shape, home.dtype),
        in_specs=[SMEM] + [ANY] * (len(blocks) + 1),
        out_specs=ANY,
        input_output_aliases={1: 0},
        scratch_shapes=[pltpu.SemaphoreType.DMA((count,))],
        compiler_params=params(4),
        name="assemble",
    )(me, home, *blocks)


def soft(scores, scale):
    top = jnp.max(scores, axis=0, keepdims=True)
    expo = jnp.exp2((scores - top) * scale)
    return expo, jnp.sum(expo, axis=0, keepdims=True)


def tile_weights(keys, query, mask, slots, scale):
    tok = query.shape[0]
    bias = (mask.astype(jnp.float32)[:slots] - 1.0) * (-HIDDEN)
    scores = mm(keys, query, NT).reshape(slots, 3 * tok // slots, tok) + bias[:, None, :]
    expo, norm = soft(scores.reshape(3 * tok, tok), scale)
    return (expo * (1.0 / norm)).astype(jnp.bfloat16)


def window(me, p, count):
    slab = me ^ p
    low = jnp.where(slab > 0, (slab - 1) ^ me, p)
    high = jnp.where(slab < count - 1, (slab + 1) ^ me, p)
    return low, p, high


def log_scale(hd):
    return hd ** (-0.5) * math.log2(math.e)


def home_kernel(count, slots, rank, hd, me_ref, *rest):
    notes, rest = rest[:count], rest[count:]
    q_ref, k_ref, v_ref, low_ref, high_ref, up_ref, out_ref, note_s = rest
    tok = q_ref.shape[0]

    size = note_s.shape[1]

    @pl.when(pl.program_id(0) == 0)
    def _():
        for p, ref in enumerate(notes):
            note_s[p] = ref[ref.shape[0] - size :, :]

    mask = note_s[0][rank:, :]
    loras = [note_s[w][:rank, :] for w in window(me_ref[0], 0, count)]
    for h in range(q_ref.shape[1] // hd):
        cols = slice(h * hd, (h + 1) * hd)
        keys = jnp.concatenate([low_ref[0, :, cols], k_ref[:, cols], high_ref[0, :, cols]], axis=0)
        weights = tile_weights(keys, q_ref[:, cols], mask, slots, log_scale(hd))
        values = []
        for value, lora in zip((low_ref[1, :, cols], v_ref[:, cols], high_ref[1, :, cols]), loras):
            term = mm(up_ref[:, cols], lora, TN)
            values.append((value.T.astype(jnp.float32) + term).astype(jnp.bfloat16))
        student = mm(jnp.concatenate(values, axis=1), weights)
        out_ref[:, cols] = student.T.astype(jnp.bfloat16)


def home_student(me, messages, mask_rows, q, k, v, low, high, up_t, hd, slots):
    count = len(messages)
    tok, model = q.shape
    rank = up_t.shape[0]
    width = min(4 * hd, model)
    column = pl.BlockSpec((tok, width), lambda h: (0, h))
    pair = pl.BlockSpec((2, tok, width), lambda h: (0, 0, h))
    return pl.pallas_call(
        functools.partial(home_kernel, count, slots, rank, hd),
        grid=(model // width,),
        out_shape=jax.ShapeDtypeStruct(q.shape, q.dtype),
        in_specs=[SMEM]
        + [VM] * count
        + [column] * 3
        + [pair] * 2
        + [pl.BlockSpec((rank, width), lambda h: (0, h))],
        out_specs=column,
        scratch_shapes=[pltpu.VMEM((count, rank + mask_rows, tok), q.dtype)],
        compiler_params=params(16),
        cost_estimate=pl.CostEstimate(
            flops=12 * 10**9, bytes_accessed=9 * tok * model * 2, transcendentals=0
        ),
        name="home_student",
    )(me, *messages, q, k, v, low, high, up_t)


def attention_kernel(
    count, tok, hd, nh, slots, rank, before, last, factor, sizes, me_ref, *rest
):
    blocks, rest = rest[:count], rest[count:]
    noted, rest = rest[:count], rest[count:]
    up_ref, _, rest = rest[0], rest[1], rest[2:]
    if before:
        (hid_ref, gup_in, out_in), rest = rest[:3], rest[3:]
    if last:
        keep_ref, send_ref, hid_keep, hid_send, gup_ref, rest = *rest[:5], rest[5:]
    else:
        hid_ref_out, gup_ref, out_ref, rest = *rest[:3], rest[3:]
    note_s, q_s, k_s, vt_s, svt_s, lora_s, grad_s, hid_s, out_s = rest
    head = pl.program_id(0)
    me = me_ref[0]
    scale = log_scale(hd)
    size = note_s.shape[1]

    @pl.when(head == 0)
    def _():
        for p, ref in enumerate(noted):
            note_s[p] = ref[sizes - size :, :]
            lora_s[:, p * tok : (p + 1) * tok] = note_s[p, :rank, :]
        if before:
            hid_s[...] = hid_ref[...]
            gup_ref[:, : before * hd] = gup_in[...]
            out_s[:before] = out_in[...]
        else:
            hid_s[...] = jnp.zeros_like(hid_s)

    start = pl.multiple_of(head * 3 * tok, tok)
    for p in range(count):
        q_s[p * tok : (p + 1) * tok, :] = blocks[p][pl.ds(start, tok), :]
        k_s[p * tok : (p + 1) * tok, :] = blocks[p][pl.ds(start + tok, tok), :]
        vt_s[:, p * tok : (p + 1) * tok] = blocks[p][pl.ds(start + 2 * tok, tok), :].T
    up_t = up_ref[...]
    for p in range(count):
        cols = slice(p * tok, (p + 1) * tok)
        term = mm(up_t, lora_s[:, cols], TN)
        svt_s[p] = (vt_s[:, cols].astype(jnp.float32) + term).astype(jnp.bfloat16)
    grad_s[...] = jnp.zeros_like(grad_s)

    for p in range(count):
        query = q_s[p * tok : (p + 1) * tok, :]
        expo, norm = soft(mm(k_s[...], query, NT), scale)
        teacher = mm(vt_s[...], expo.astype(jnp.bfloat16)) / norm
        teacher = teacher.astype(jnp.bfloat16).astype(jnp.float32)
        places = window(me, p, count)
        keys = jnp.concatenate(
            [k_s[pl.ds(pl.multiple_of(w * tok, tok), tok), :] for w in places], axis=0
        )
        weights = tile_weights(keys, query, note_s[p, rank:, :], slots, scale)
        values = jnp.concatenate([svt_s[w] for w in places], axis=1)
        student = mm(values, weights)
        out_s[before + head, p] = student.astype(jnp.bfloat16)
        delta = ((student - teacher) * factor).astype(jnp.bfloat16)
        grads = mm(weights, delta, NT)
        for n, w in enumerate(places):
            grad_s[w] += grads[n * tok : (n + 1) * tok]

    grad = grad_s[...].reshape(count * tok, hd).astype(jnp.bfloat16)
    column = pl.multiple_of((before + head) * hd, LANES)
    gup_ref[:, pl.ds(column, hd)] = mm(lora_s[...], grad)
    hid_s[...] += mm(up_t, grad, NT)

    @pl.when(head == nh - 1)
    def _():
        if last:
            for m in range(count // 2):
                to = slice(m * tok, (m + 1) * tok)
                hid_keep[:, to] = hid_s[:, 2 * m * tok : (2 * m + 1) * tok]
                odd = hid_s[:, (2 * m + 1) * tok : (2 * m + 2) * tok]
                hid_send[:, to] = odd.astype(jnp.bfloat16)
            core = lax.rem(me, 2)
            half = count // 2
            same = jnp.where(core == (half - 1) % 2, half - 1, half)
            other = jnp.where(core == (half - 1) % 2, half, half - 1)
            for ref, slab in ((keep_ref, same), (send_ref, other)):
                for h in range(before + nh):
                    ref[:, h * hd : (h + 1) * hd] = out_s[h, me ^ slab].T
        else:
            hid_ref_out[...] = hid_s[...]
            out_ref[...] = out_s[...]


def attention(me, blocks, noted, up_t, after, given, first, nh, tok, hd, slots, mask_rows, last):
    count = len(blocks)
    rank = up_t.shape[0]
    bf, f32 = jnp.bfloat16, jnp.float32
    whole = lambda shape: pl.BlockSpec(shape, lambda h: (0,) * len(shape))
    keys = count * tok
    heads = first + nh
    shapes = [
        jax.ShapeDtypeStruct((rank, keys), f32),
        jax.ShapeDtypeStruct((rank, heads * hd), f32),
        jax.ShapeDtypeStruct((heads, count, hd, tok), bf),
    ]
    if last:
        shapes = [
            jax.ShapeDtypeStruct((tok, heads * hd), bf),
            jax.ShapeDtypeStruct((tok, heads * hd), bf),
            jax.ShapeDtypeStruct((rank, keys // 2), f32),
            jax.ShapeDtypeStruct((rank, keys // 2), bf),
            jax.ShapeDtypeStruct((rank, heads * hd), f32),
        ]
    return pl.pallas_call(
        functools.partial(
            attention_kernel,
            count,
            tok,
            hd,
            nh,
            slots,
            rank,
            first,
            last,
            keys ** (-0.5),
            noted[0].shape[0],
        ),
        grid=(nh,),
        out_shape=shapes,
        in_specs=[SMEM]
        + [VM] * (2 * count)
        + [pl.BlockSpec((rank, hd), lambda h: (0, first + h)), ANY]
        + [whole(g.shape) for g in given],
        out_specs=[whole(s.shape) for s in shapes],
        scratch_shapes=[
            pltpu.VMEM((count, rank + mask_rows, tok), bf),
            pltpu.VMEM((keys, hd), bf),
            pltpu.VMEM((keys, hd), bf),
            pltpu.VMEM((hd, keys), bf),
            pltpu.VMEM((count, hd, tok), bf),
            pltpu.VMEM((rank, keys), bf),
            pltpu.VMEM((count, tok, hd), f32),
            pltpu.VMEM((rank, keys), f32),
            pltpu.VMEM((heads, count, hd, tok), bf),
        ],
        compiler_params=params(30),
        cost_estimate=pl.CostEstimate(
            flops=nh * 6 * 10**9, bytes_accessed=4 * nh * keys * hd * 2, transcendentals=0
        ),
        name="attention",
    )(me, *blocks, *noted, up_t, after, *given)


def pair_kernel(parts, keep_ref, got_ref, *outs):
    width = keep_ref.shape[1] // parts
    for m in range(parts):
        cols = slice(m * width, (m + 1) * width)
        total = keep_ref[:, cols] + got_ref[:, cols].astype(jnp.float32)
        outs[m][...] = total.astype(outs[m].dtype)


def pair_sum(keep, got, parts):
    rank, width = keep.shape[0], keep.shape[1] // parts
    shapes = [
        jax.ShapeDtypeStruct((rank, width), jnp.bfloat16 if m else jnp.float32)
        for m in range(parts)
    ]
    return pl.pallas_call(
        functools.partial(pair_kernel, parts),
        out_shape=shapes,
        in_specs=[VM, VM],
        out_specs=[VM] * parts,
        compiler_params=params(8),
        name="pair_sum",
    )(keep, got)


def chip_terms(keep, send, count):
    totals = pair_sum(keep, swap(send, count, 1), count // 2)
    got = {m: swap(totals[m], count, 2 * m) for m in range(count // 2 - 1, 0, -1)}
    return [totals[0]] + [got[m] for m in range(1, count // 2)]


def down_kernel(count, group, me_ref, *rest):
    parts = rest[: count // 2]
    x_ref, keep_ref, send_ref = rest[count // 2 :]
    me = me_ref[0]
    hidden = parts[0][...]
    for part in parts[1:]:
        hidden += part[...].astype(jnp.float32)
    hidden = hidden.astype(jnp.bfloat16)
    for k in range(count):
        column = pl.multiple_of((me ^ k) * group, LANES)
        term = mm(hidden, x_ref[:, pl.ds(column, group)])
        to = (send_ref, keep_ref)[k % 2 == 0]
        to[:, k // 2 * group : (k // 2 + 1) * group] = term.astype(to.dtype)


def down_terms(me, parts, x):
    count = 2 * len(parts)
    model = x.shape[1]
    rank = parts[0].shape[0]
    return pl.pallas_call(
        functools.partial(down_kernel, count, model // count),
        out_shape=[
            jax.ShapeDtypeStruct((rank, model // 2), jnp.float32),
            jax.ShapeDtypeStruct((rank, model // 2), jnp.bfloat16),
        ],
        in_specs=[SMEM] + [VM] * (len(parts) + 1),
        out_specs=[VM, VM],
        compiler_params=params(8),
        name="down_terms",
    )(me, *parts, x)


def sum_kernel(*refs):
    total = refs[0][...]
    for ref in refs[1:-1]:
        total += ref[...].astype(jnp.float32)
    refs[-1][...] = total


def sum_terms(parts):
    return pl.pallas_call(
        sum_kernel,
        out_shape=jax.ShapeDtypeStruct(parts[0].shape, jnp.float32),
        in_specs=[VM] * len(parts),
        out_specs=VM,
        compiler_params=params(8),
        name="sum_terms",
    )(*parts)


def head_chunks(per_group):
    if per_group < 2:
        return [(0, per_group)]
    return [(0, per_group - 1), (per_group - 1, 1)]


def local(
    queries, keys, values, value_layer_input, adapter_down_weight, adapter_up_weight, neighbors
):
    tok, model = queries.shape
    rank = adapter_down_weight.shape[1]
    count = lax.axis_size("context")
    index = lax.axis_index("context")
    me = index.astype(jnp.int32).reshape(1)
    hd = model // H
    group = model // count
    per_group = H // count
    tiles = neighbors.shape[0]
    slots = 3 * tiles
    chunks = head_chunks(per_group)

    mask_rows = slots + -slots % 16

    down_t = adapter_down_weight.T
    up_t = adapter_up_weight.T

    messages = []
    for c, (first, nh) in enumerate(chunks):
        if c == 0:
            blocks = first_pack(
                me, neighbors, queries, keys, values, value_layer_input, down_t,
                count, hd, nh, mask_rows,
            )
        else:
            after = messages[-1][-1]
            blocks = pack(me, queries, keys, values, after, count, hd, first, nh)
        messages.append(exchange(blocks, count))
    noted = messages[0]

    half = count // 2
    ups = [(i, i + 1) for i in range(count - 1) if i + 1 != half]
    both = jnp.stack([keys, values])
    low = lax.ppermute(both, "context", ups)
    high = lax.ppermute(both, "context", [(j, i) for i, j in ups])
    home = home_student(
        me, noted, mask_rows, queries, keys, values, low, high, up_t, hd, slots
    )

    own_up = lax.dynamic_slice_in_dim(up_t, index * group, group, 1)
    given = []
    for c, (first, nh) in enumerate(chunks):
        last = c == len(chunks) - 1
        given = attention(
            me, messages[c], noted, own_up, home, given, first, nh, tok, hd, slots, mask_rows, last
        )
    keep, send, hid_keep, hid_send, grad_up = given
    hidden = chip_terms(hid_keep, hid_send, count)
    grad_down = sum_terms(chip_terms(*down_terms(me, hidden, value_layer_input), count))

    middle = jnp.stack([keep, swap(send, count, 1)])
    blocks = [middle] + [swap(middle, count, 2 * m, (half - 1, half)) for m in range(1, half)]
    return assemble(me, home, blocks), grad_down.T, grad_up.T


def solution(mesh):
    rows = P(("video", "context"), None)
    return jax.shard_map(
        local,
        mesh=mesh,
        in_specs=(rows, rows, rows, rows, P(), P(), rows),
        out_specs=(rows, rows, rows),
        check_vma=False,
    )
```

```python
import functools
import math

import jax
import jax.numpy as jnp
from jax import lax
from jax.experimental import pallas as pl
from jax.experimental.pallas import tpu as pltpu
from jax.sharding import PartitionSpec as P

H = 32
HIDDEN = -1e30
NT = (((1,), (1,)), ((), ()))
TN = (((0,), (0,)), ((), ()))
NN = (((1,), (0,)), ((), ()))


def mm(a, b, dims=NN):
    return lax.dot_general(a, b, dims, preferred_element_type=jnp.float32)


def params(mib):
    return pltpu.CompilerParams(vmem_limit_bytes=mib * 1024 * 1024)


SMEM = pl.BlockSpec(memory_space=pltpu.SMEM)
HBM = pl.BlockSpec(memory_space=pltpu.HBM)
ANY = pl.BlockSpec(memory_space=pl.ANY)
VM = pl.BlockSpec(memory_space=pltpu.VMEM)
LANES = 128


def swap(block, count, bits, targets=None):
    pairs = [(i, i ^ bits) for i in range(count) if targets is None or i ^ bits in targets]
    return lax.ppermute(block, "context", pairs)


def far_first(count):
    half = count // 2
    return list(range(half, count)) + list(range(half - 1, -1, -1))


def exchange(blocks, count):
    got = {0: blocks[0]}
    for k in far_first(count)[:-1]:
        got[k] = swap(blocks[k], count, k)
    return [got[k] for k in range(count)]


def pack_copies(count, group, hd, first, nh, me, refs, outs, sems):
    tok = refs[0].shape[0]
    copies = []
    for k in range(count):
        for h in range(nh):
            column = pl.multiple_of((me ^ k) * group + (first + h) * hd, LANES)
            for t, ref in enumerate(refs):
                n = h * 3 + t
                copies.append(
                    pltpu.make_async_copy(
                        ref.at[:, pl.ds(column, hd)],
                        outs[k].at[pl.ds(n * tok, tok), :],
                        sems.at[k * nh * 3 + n],
                    )
                )
    return copies


def pack_kernel(count, group, hd, first, nh, me_ref, q_ref, k_ref, v_ref, _, *rest):
    outs, sems = rest[:count], rest[count]
    copies = pack_copies(
        count, group, hd, first, nh, me_ref[0], (q_ref, k_ref, v_ref), outs, sems
    )
    for copy in copies:
        copy.start()
    for copy in copies:
        copy.wait()


def pack(me, q, k, v, after, count, hd, first, nh):
    tok, model = q.shape
    return pl.pallas_call(
        functools.partial(pack_kernel, count, model // count, hd, first, nh),
        out_shape=[jax.ShapeDtypeStruct((nh * 3 * tok, hd), q.dtype)] * count,
        in_specs=[SMEM, HBM, HBM, HBM, ANY],
        out_specs=[VM] * count,
        scratch_shapes=[pltpu.SemaphoreType.DMA((3 * nh * count,))],
        compiler_params=params(4),
        name="pack",
    )(me, q, k, v, after)


def first_kernel(count, group, hd, nh, mask_rows, tiles, me_ref, nb_ref, *rest):
    q_ref, k_ref, v_ref, x_ref, down_ref = rest[:5]
    outs, rest = rest[5 : 5 + count], rest[5 + count :]
    both_ref, x_s, down_s, sems, in_sems = rest
    me = me_ref[0]
    tok = q_ref.shape[0]
    rank = down_ref.shape[0]
    copies = pack_copies(count, group, hd, 0, nh, me, (q_ref, k_ref, v_ref), outs, sems)
    loads = [
        pltpu.make_async_copy(x_ref, x_s, in_sems.at[0]),
        pltpu.make_async_copy(down_ref, down_s, in_sems.at[1]),
    ]
    pair = [
        pltpu.make_async_copy(k_ref, both_ref.at[0], in_sems.at[2]),
        pltpu.make_async_copy(v_ref, both_ref.at[1], in_sems.at[3]),
    ]
    for copy in loads + copies + pair:
        copy.start()
    rows = lax.broadcasted_iota(jnp.int32, (mask_rows, tok), 0)
    lane_tile = lax.broadcasted_iota(jnp.int32, (mask_rows, tok), 1) // (tok // tiles)
    seen = jnp.zeros((mask_rows, tok), jnp.float32)
    for t in range(tiles):
        for n in range(nb_ref.shape[1]):
            slot = nb_ref[t, n] - (me - 1) * tiles
            seen = jnp.where((rows == slot) & (lane_tile == t), 1.0, seen)
    for copy in loads:
        copy.wait()
    lora = mm(down_s[...], x_s[...], NT).astype(jnp.bfloat16)
    note = jnp.concatenate([lora, seen.astype(jnp.bfloat16)], axis=0)
    for out in outs:
        out[nh * 3 * tok :, :] = note
    for copy in copies + pair:
        copy.wait()


def first_pack(me, nb, q, k, v, x, down, count, hd, nh, mask_rows):
    tok, model = q.shape
    rank = down.shape[0]
    rows = nh * 3 * tok + rank + mask_rows
    bf = q.dtype
    out = pl.pallas_call(
        functools.partial(
            first_kernel, count, model // count, hd, nh, mask_rows, nb.shape[0]
        ),
        out_shape=[jax.ShapeDtypeStruct((rows, hd), bf)] * count
        + [jax.ShapeDtypeStruct((2, tok, model), bf)],
        in_specs=[SMEM, SMEM] + [HBM] * 5,
        out_specs=[VM] * (count + 1),
        scratch_shapes=[
            pltpu.VMEM(x.shape, bf),
            pltpu.VMEM(down.shape, bf),
            pltpu.SemaphoreType.DMA((3 * nh * count,)),
            pltpu.SemaphoreType.DMA((4,)),
        ],
        compiler_params=params(50),
        name="first_pack",
    )(me, nb, q, k, v, x, down)
    return out[:count], out[count]


def assemble_kernel(count, group, me_ref, home_ref, *rest):
    refs, out, sems = rest[: count // 2], rest[count // 2], rest[count // 2 + 1]
    me = me_ref[0]

    @pl.when((me == count // 2 - 1) | (me == count // 2))
    def _():
        copies = []
        for k in range(count):
            column = pl.multiple_of((me ^ k) * group, LANES)
            copies.append(
                pltpu.make_async_copy(
                    refs[k // 2].at[k % 2], out.at[:, pl.ds(column, group)], sems.at[k]
                )
            )
        for copy in copies:
            copy.start()
        for copy in copies:
            copy.wait()


def assemble(me, home, blocks):
    count = 2 * len(blocks)
    return pl.pallas_call(
        functools.partial(assemble_kernel, count, home.shape[1] // count),
        out_shape=jax.ShapeDtypeStruct(home.shape, home.dtype),
        in_specs=[SMEM] + [ANY] * (len(blocks) + 1),
        out_specs=ANY,
        input_output_aliases={1: 0},
        scratch_shapes=[pltpu.SemaphoreType.DMA((count,))],
        compiler_params=params(4),
        name="assemble",
    )(me, home, *blocks)


def soft(scores, scale):
    top = jnp.max(scores, axis=0, keepdims=True)
    expo = jnp.exp2((scores - top) * scale)
    return expo, jnp.sum(expo, axis=0, keepdims=True)


def masked_weights(scores, mask, slots, scale):
    rows, tok = scores.shape
    bias = (mask.astype(jnp.float32)[:slots] - 1.0) * (-HIDDEN)
    scores = scores.reshape(slots, rows // slots, tok) + bias[:, None, :]
    expo, norm = soft(scores.reshape(rows, tok), scale)
    return (expo * (1.0 / norm)).astype(jnp.bfloat16)


def window(me, p, count):
    slab = me ^ p
    low = jnp.where(slab > 0, (slab - 1) ^ me, p)
    high = jnp.where(slab < count - 1, (slab + 1) ^ me, p)
    return low, p, high


def log_scale(hd):
    return hd ** (-0.5) * math.log2(math.e)


def home_kernel(count, slots, rank, hd, me_ref, *rest):
    notes = {p: ref for p, ref in zip(far_first(count), rest)}
    rest = rest[count:]
    q_ref, k_ref, v_ref, low_ref, high_ref, up_ref, out_ref, note_s = rest
    tok = q_ref.shape[0]

    size = note_s.shape[1]

    @pl.when(pl.program_id(0) == 0)
    def _():
        for p, ref in notes.items():
            note_s[p] = ref[ref.shape[0] - size :, :]

    mask = note_s[0][rank:, :]
    loras = [note_s[w][:rank, :] for w in window(me_ref[0], 0, count)]
    heads = [slice(h * hd, (h + 1) * hd) for h in range(q_ref.shape[1] // hd)]
    keys = jnp.concatenate([low_ref[0], k_ref[...], high_ref[0]], axis=0)
    scores = [mm(keys[:, cols], q_ref[:, cols], NT) for cols in heads]
    terms = [[mm(up_ref[:, cols], lora, TN) for lora in loras] for cols in heads]
    weights = [masked_weights(x, mask, slots, log_scale(hd)) for x in scores]
    values = [
        jnp.concatenate(
            [
                (v.T.astype(jnp.float32) + t).astype(jnp.bfloat16)
                for v, t in zip((low_ref[1, :, cols], v_ref[:, cols], high_ref[1, :, cols]), term)
            ],
            axis=1,
        )
        for cols, term in zip(heads, terms)
    ]
    students = [mm(v, w) for v, w in zip(values, weights)]
    for cols, student in zip(heads, students):
        out_ref[:, cols] = student.T.astype(jnp.bfloat16)


def home_student(me, messages, mask_rows, q, k, v, low, high, up_t, hd, slots):
    count = len(messages)
    tok, model = q.shape
    rank = up_t.shape[0]
    width = min(8 * hd, model)
    column = pl.BlockSpec((tok, width), lambda h: (0, h))
    pair = pl.BlockSpec((2, tok, width), lambda h: (0, 0, h))
    return pl.pallas_call(
        functools.partial(home_kernel, count, slots, rank, hd),
        grid=(model // width,),
        out_shape=jax.ShapeDtypeStruct(q.shape, q.dtype),
        in_specs=[SMEM]
        + [VM] * count
        + [column] * 3
        + [pair] * 2
        + [pl.BlockSpec((rank, width), lambda h: (0, h))],
        out_specs=column,
        scratch_shapes=[pltpu.VMEM((count, rank + mask_rows, tok), q.dtype)],
        compiler_params=params(16),
        cost_estimate=pl.CostEstimate(
            flops=12 * 10**9, bytes_accessed=9 * tok * model * 2, transcendentals=0
        ),
        name="home_student",
    )(me, *[messages[p] for p in far_first(count)], q, k, v, low, high, up_t)


def attention_kernel(
    count, tok, hd, nh, slots, rank, before, last, factor, sizes, me_ref, *rest
):
    blocks = {p: ref for p, ref in zip(far_first(count), rest)}
    noted = {p: ref for p, ref in zip(far_first(count), rest[count:])}
    rest = rest[2 * count :]
    up_ref, _, rest = rest[0], rest[1], rest[2:]
    if before:
        (hid_ref, gup_in, out_in), rest = rest[:3], rest[3:]
    if last:
        keep_ref, send_ref, hid_keep, hid_send, gup_ref, rest = *rest[:5], rest[5:]
    else:
        hid_ref_out, gup_ref, out_ref, rest = *rest[:3], rest[3:]
    note_s, q_s, k_s, vt_s, svt_s, lora_s, grad_s, hid_s, out_s = rest
    head = pl.program_id(0)
    me = me_ref[0]
    scale = log_scale(hd)
    size = note_s.shape[1]

    @pl.when(head == 0)
    def _():
        for p, ref in noted.items():
            note_s[p] = ref[sizes - size :, :]
            lora_s[:, p * tok : (p + 1) * tok] = note_s[p, :rank, :]
        if before:
            hid_s[...] = hid_ref[...]
            gup_ref[:, : before * hd] = gup_in[...]
            out_s[:before] = out_in[...]
        else:
            hid_s[...] = jnp.zeros_like(hid_s)

    start = pl.multiple_of(head * 3 * tok, tok)
    for p in range(count):
        q_s[p * tok : (p + 1) * tok, :] = blocks[p][pl.ds(start, tok), :]
        k_s[p * tok : (p + 1) * tok, :] = blocks[p][pl.ds(start + tok, tok), :]
        vt_s[:, p * tok : (p + 1) * tok] = blocks[p][pl.ds(start + 2 * tok, tok), :].T
    up_t = up_ref[...]
    for p in range(count):
        cols = slice(p * tok, (p + 1) * tok)
        term = mm(up_t, lora_s[:, cols], TN)
        svt_s[p] = (vt_s[:, cols].astype(jnp.float32) + term).astype(jnp.bfloat16)
    grad_s[...] = jnp.zeros_like(grad_s)

    for start in range(0, count, 4):
        slabs = range(start, min(start + 4, count))
        queries = [q_s[p * tok : (p + 1) * tok, :] for p in slabs]
        places = [window(me, p, count) for p in slabs]
        full = [mm(k_s[...], query, NT) for query in queries]
        seen = [
            mm(
                jnp.concatenate(
                    [k_s[pl.ds(pl.multiple_of(w * tok, tok), tok), :] for w in place], axis=0
                ),
                query,
                NT,
            )
            for place, query in zip(places, queries)
        ]
        full = [soft(x, scale) for x in full]
        teachers = [mm(vt_s[...], expo.astype(jnp.bfloat16)) for expo, _ in full]
        weights = [
            masked_weights(x, note_s[p, rank:, :], slots, scale) for p, x in zip(slabs, seen)
        ]
        students = [
            mm(jnp.concatenate([svt_s[w] for w in place], axis=1), weight)
            for place, weight in zip(places, weights)
        ]
        deltas = []
        for (_, norm), teacher, student in zip(full, teachers, students):
            teacher = (teacher / norm).astype(jnp.bfloat16).astype(jnp.float32)
            deltas.append(((student - teacher) * factor).astype(jnp.bfloat16))
        grads = [mm(weight, delta, NT) for weight, delta in zip(weights, deltas)]
        for p, place, student, grad in zip(slabs, places, students, grads):
            out_s[before + head, p] = student.astype(jnp.bfloat16)
            for n, w in enumerate(place):
                grad_s[w] += grad[n * tok : (n + 1) * tok]

    grad = grad_s[...].reshape(count * tok, hd).astype(jnp.bfloat16)
    column = pl.multiple_of((before + head) * hd, LANES)
    gup_ref[:, pl.ds(column, hd)] = mm(lora_s[...], grad)
    hid_s[...] += mm(up_t, grad, NT)

    @pl.when(head == nh - 1)
    def _():
        if last:
            for m in range(count // 2):
                to = slice(m * tok, (m + 1) * tok)
                hid_keep[:, to] = hid_s[:, 2 * m * tok : (2 * m + 1) * tok]
                odd = hid_s[:, (2 * m + 1) * tok : (2 * m + 2) * tok]
                hid_send[:, to] = odd.astype(jnp.bfloat16)
            core = lax.rem(me, 2)
            half = count // 2
            same = jnp.where(core == (half - 1) % 2, half - 1, half)
            other = jnp.where(core == (half - 1) % 2, half, half - 1)
            for ref, slab in ((keep_ref, same), (send_ref, other)):
                for h in range(before + nh):
                    ref[:, h * hd : (h + 1) * hd] = out_s[h, me ^ slab].T
        else:
            hid_ref_out[...] = hid_s[...]
            out_ref[...] = out_s[...]


def attention(me, blocks, noted, up_t, after, given, first, nh, tok, hd, slots, mask_rows, last):
    count = len(blocks)
    rank = up_t.shape[0]
    bf, f32 = jnp.bfloat16, jnp.float32
    whole = lambda shape: pl.BlockSpec(shape, lambda h: (0,) * len(shape))
    keys = count * tok
    heads = first + nh
    shapes = [
        jax.ShapeDtypeStruct((rank, keys), f32),
        jax.ShapeDtypeStruct((rank, heads * hd), f32),
        jax.ShapeDtypeStruct((heads, count, hd, tok), bf),
    ]
    if last:
        shapes = [
            jax.ShapeDtypeStruct((tok, heads * hd), bf),
            jax.ShapeDtypeStruct((tok, heads * hd), bf),
            jax.ShapeDtypeStruct((rank, keys // 2), f32),
            jax.ShapeDtypeStruct((rank, keys // 2), bf),
            jax.ShapeDtypeStruct((rank, heads * hd), f32),
        ]
    return pl.pallas_call(
        functools.partial(
            attention_kernel,
            count,
            tok,
            hd,
            nh,
            slots,
            rank,
            first,
            last,
            keys ** (-0.5),
            noted[0].shape[0],
        ),
        grid=(nh,),
        out_shape=shapes,
        in_specs=[SMEM]
        + [VM] * (2 * count)
        + [pl.BlockSpec((rank, hd), lambda h: (0, first + h)), ANY]
        + [whole(g.shape) for g in given],
        out_specs=[whole(s.shape) for s in shapes],
        scratch_shapes=[
            pltpu.VMEM((count, rank + mask_rows, tok), bf),
            pltpu.VMEM((keys, hd), bf),
            pltpu.VMEM((keys, hd), bf),
            pltpu.VMEM((hd, keys), bf),
            pltpu.VMEM((count, hd, tok), bf),
            pltpu.VMEM((rank, keys), bf),
            pltpu.VMEM((count, tok, hd), f32),
            pltpu.VMEM((rank, keys), f32),
            pltpu.VMEM((heads, count, hd, tok), bf),
        ],
        compiler_params=params(30),
        cost_estimate=pl.CostEstimate(
            flops=nh * 6 * 10**9, bytes_accessed=4 * nh * keys * hd * 2, transcendentals=0
        ),
        name="attention",
    )(
        me,
        *[blocks[p] for p in far_first(count)],
        *[noted[p] for p in far_first(count)],
        up_t,
        after,
        *given,
    )


def pair_kernel(parts, keep_ref, got_ref, *outs):
    width = keep_ref.shape[1] // parts
    for m in range(parts):
        cols = slice(m * width, (m + 1) * width)
        total = keep_ref[:, cols] + got_ref[:, cols].astype(jnp.float32)
        outs[m][...] = total.astype(outs[m].dtype)


def pair_sum(keep, got, parts):
    rank, width = keep.shape[0], keep.shape[1] // parts
    shapes = [
        jax.ShapeDtypeStruct((rank, width), jnp.bfloat16 if m else jnp.float32)
        for m in range(parts)
    ]
    return pl.pallas_call(
        functools.partial(pair_kernel, parts),
        out_shape=shapes,
        in_specs=[VM, VM],
        out_specs=[VM] * parts,
        compiler_params=params(8),
        name="pair_sum",
    )(keep, got)


def chip_terms(keep, send, count):
    totals = pair_sum(keep, swap(send, count, 1), count // 2)
    got = {m: swap(totals[m], count, 2 * m) for m in range(count // 2 - 1, 0, -1)}
    return [totals[0]] + [got[m] for m in range(1, count // 2)]


def down_kernel(count, group, me_ref, *rest):
    parts = rest[: count // 2]
    x_ref, keep_ref, send_ref = rest[count // 2 :]
    me = me_ref[0]
    hidden = parts[0][...]
    for part in parts[1:]:
        hidden += part[...].astype(jnp.float32)
    hidden = hidden.astype(jnp.bfloat16)
    for k in range(count):
        column = pl.multiple_of((me ^ k) * group, LANES)
        term = mm(hidden, x_ref[:, pl.ds(column, group)])
        to = (send_ref, keep_ref)[k % 2 == 0]
        to[:, k // 2 * group : (k // 2 + 1) * group] = term.astype(to.dtype)


def down_terms(me, parts, x):
    count = 2 * len(parts)
    model = x.shape[1]
    rank = parts[0].shape[0]
    return pl.pallas_call(
        functools.partial(down_kernel, count, model // count),
        out_shape=[
            jax.ShapeDtypeStruct((rank, model // 2), jnp.float32),
            jax.ShapeDtypeStruct((rank, model // 2), jnp.bfloat16),
        ],
        in_specs=[SMEM] + [VM] * (len(parts) + 1),
        out_specs=[VM, VM],
        compiler_params=params(8),
        name="down_terms",
    )(me, *parts, x)


def sum_kernel(*refs):
    total = refs[0][...]
    for ref in refs[1:-1]:
        total += ref[...].astype(jnp.float32)
    refs[-1][...] = total


def sum_terms(parts):
    return pl.pallas_call(
        sum_kernel,
        out_shape=jax.ShapeDtypeStruct(parts[0].shape, jnp.float32),
        in_specs=[VM] * len(parts),
        out_specs=VM,
        compiler_params=params(8),
        name="sum_terms",
    )(*parts)


def head_chunks(per_group):
    if per_group < 2:
        return [(0, per_group)]
    return [(0, per_group - 1), (per_group - 1, 1)]


def local(
    queries, keys, values, value_layer_input, adapter_down_weight, adapter_up_weight, neighbors
):
    tok, model = queries.shape
    rank = adapter_down_weight.shape[1]
    count = lax.axis_size("context")
    index = lax.axis_index("context")
    me = index.astype(jnp.int32).reshape(1)
    hd = model // H
    group = model // count
    per_group = H // count
    tiles = neighbors.shape[0]
    slots = 3 * tiles
    chunks = head_chunks(per_group)

    mask_rows = slots + -slots % 16

    down_t = adapter_down_weight.T
    up_t = adapter_up_weight.T

    messages = []
    for c, (first, nh) in enumerate(chunks):
        if c == 0:
            blocks, both = first_pack(
                me, neighbors, queries, keys, values, value_layer_input, down_t,
                count, hd, nh, mask_rows,
            )
        else:
            after = messages[-1][-1]
            blocks = pack(me, queries, keys, values, after, count, hd, first, nh)
        messages.append(exchange(blocks, count))
    noted = messages[0]

    half = count // 2
    ups = [(i, i + 1) for i in range(count - 1) if i + 1 != half]
    low = lax.ppermute(both, "context", ups)
    high = lax.ppermute(both, "context", [(j, i) for i, j in ups])
    home = home_student(
        me, noted, mask_rows, queries, keys, values, low, high, up_t, hd, slots
    )

    own_up = lax.dynamic_slice_in_dim(up_t, index * group, group, 1)
    given = []
    for c, (first, nh) in enumerate(chunks):
        last = c == len(chunks) - 1
        given = attention(
            me, messages[c], noted, own_up, home, given, first, nh, tok, hd, slots, mask_rows, last
        )
    keep, send, hid_keep, hid_send, grad_up = given
    hidden = chip_terms(hid_keep, hid_send, count)
    grad_down = sum_terms(chip_terms(*down_terms(me, hidden, value_layer_input), count))

    middle = jnp.stack([keep, swap(send, count, 1)])
    blocks = [middle] + [swap(middle, count, 2 * m, (half - 1, half)) for m in range(1, half)]
    return assemble(me, home, blocks), grad_down.T, grad_up.T


def solution(mesh):
    rows = P(("video", "context"), None)
    return jax.shard_map(
        local,
        mesh=mesh,
        in_specs=(rows, rows, rows, rows, P(), P(), rows),
        out_specs=(rows, rows, rows),
        check_vma=False,
    )
```

```python
import functools
import math

import jax
import jax.numpy as jnp
from jax import lax
from jax.experimental import pallas as pl
from jax.experimental.pallas import tpu as pltpu
from jax.sharding import PartitionSpec as P

H = 32
HIDDEN = -1e30
NT = (((1,), (1,)), ((), ()))
TN = (((0,), (0,)), ((), ()))
NN = (((1,), (0,)), ((), ()))


def mm(a, b, dims=NN):
    return lax.dot_general(a, b, dims, preferred_element_type=jnp.float32)


def params(mib):
    return pltpu.CompilerParams(vmem_limit_bytes=mib * 1024 * 1024)


SMEM = pl.BlockSpec(memory_space=pltpu.SMEM)
HBM = pl.BlockSpec(memory_space=pltpu.HBM)
ANY = pl.BlockSpec(memory_space=pl.ANY)
VM = pl.BlockSpec(memory_space=pltpu.VMEM)
LANES = 128
ROWS = 16


def swap(block, count, bits, targets=None):
    pairs = [(i, i ^ bits) for i in range(count) if targets is None or i ^ bits in targets]
    return lax.ppermute(block, "context", pairs)


def chips(blocks, count, targets=None):
    got = [blocks[0]] + [None] * (len(blocks) - 1)
    for m in sorted(range(1, len(blocks)), key=lambda m: -m):
        got[m] = swap(blocks[m], count, 2 * m, targets)
    return got


def pack_copies(count, group, hd, first, nh, me, refs, place, sems):
    tok = refs[0].shape[0]
    copies = []
    for k in range(count):
        for h in range(nh):
            column = pl.multiple_of((me ^ k) * group + (first + h) * hd, LANES)
            for t, ref in enumerate(refs):
                row = (h * 3 + t) * tok
                copies.append(
                    pltpu.make_async_copy(
                        ref.at[:, pl.ds(column, hd)],
                        place(k, row, tok),
                        sems.at[(k * nh + h) * 3 + t],
                    )
                )
    return copies


def pack_kernel(count, group, hd, first, nh, me_ref, q_ref, k_ref, v_ref, _, *rest):
    outs, sems = rest[:-1], rest[-1]
    chunk = nh * 3 * q_ref.shape[0]

    def place(k, row, size):
        if k % 2:
            return outs[-1].at[pl.ds(k // 2 * chunk + row, size), :]
        return outs[k // 2].at[pl.ds(row, size), :]

    copies = pack_copies(
        count, group, hd, first, nh, me_ref[0], (q_ref, k_ref, v_ref), place, sems
    )
    for copy in copies:
        copy.start()
    for copy in copies:
        copy.wait()


def pack(me, q, k, v, after, count, hd, first, nh):
    tok, model = q.shape
    rows = nh * 3 * tok
    shapes = [jax.ShapeDtypeStruct((2 * rows, hd), q.dtype)] * (count // 2)
    return pl.pallas_call(
        functools.partial(pack_kernel, count, model // count, hd, first, nh),
        out_shape=shapes + [jax.ShapeDtypeStruct((count // 2 * rows, hd), q.dtype)],
        in_specs=[SMEM, HBM, HBM, HBM, ANY],
        out_specs=[VM] * (count // 2 + 1),
        scratch_shapes=[pltpu.SemaphoreType.DMA((3 * nh * count,))],
        compiler_params=params(8),
        name="pack",
    )(me, q, k, v, after)


def first_kernel(count, group, hd, nh, mask_rows, tiles, me_ref, nb_ref, *rest):
    q_ref, k_ref, v_ref, x_ref, down_ref = rest[:5]
    outs, rest = rest[5 : 5 + count // 2], rest[5 + count // 2 :]
    x_s, down_s, sems, in_sems = rest
    me = me_ref[0]
    tok = q_ref.shape[0]
    rank = down_ref.shape[0]
    chunk = nh * 3 * tok

    def place(k, row, size):
        return outs[k // 2].at[pl.ds(k % 2 * chunk + row, size), :]

    copies = pack_copies(count, group, hd, 0, nh, me, (q_ref, k_ref, v_ref), place, sems)
    loads = [
        pltpu.make_async_copy(x_ref, x_s, in_sems.at[0]),
        pltpu.make_async_copy(down_ref, down_s, in_sems.at[1]),
    ]
    for copy in loads + copies:
        copy.start()
    rows = lax.broadcasted_iota(jnp.int32, (mask_rows, tok), 0)
    lane_tile = lax.broadcasted_iota(jnp.int32, (mask_rows, tok), 1) // (tok // tiles)
    seen = jnp.zeros((mask_rows, tok), jnp.float32)
    for t in range(tiles):
        for n in range(nb_ref.shape[1]):
            slot = nb_ref[t, n] - (me - 1) * tiles
            seen = jnp.where((rows == slot) & (lane_tile == t), 1.0, seen)
    for copy in loads:
        copy.wait()
    lora = mm(down_s[...], x_s[...], NT).astype(jnp.bfloat16)
    note = jnp.concatenate([lora, seen.astype(jnp.bfloat16)], axis=0)
    for out in outs:
        out[2 * chunk :, :] = note
    for copy in copies:
        copy.wait()


def first_pack(me, nb, q, k, v, x, down, count, hd, nh, mask_rows):
    tok, model = q.shape
    rows = 2 * nh * 3 * tok + down.shape[0] + mask_rows
    bf = q.dtype
    return pl.pallas_call(
        functools.partial(
            first_kernel, count, model // count, hd, nh, mask_rows, nb.shape[0]
        ),
        out_shape=[jax.ShapeDtypeStruct((rows, hd), bf)] * (count // 2),
        in_specs=[SMEM, SMEM] + [HBM] * 5,
        out_specs=[VM] * (count // 2),
        scratch_shapes=[
            pltpu.VMEM(x.shape, bf),
            pltpu.VMEM(down.shape, bf),
            pltpu.SemaphoreType.DMA((3 * nh * count,)),
            pltpu.SemaphoreType.DMA((2,)),
        ],
        compiler_params=params(60),
        name="first_pack",
    )(me, nb, q, k, v, x, down)


def forward_kernel(parts, rows, *refs):
    size = refs[0].shape[0] - rows
    for m in range(parts):
        refs[-1][m * size : (m + 1) * size, :] = refs[m][rows:, :]


def forward(blocks, note, after):
    parts = len(blocks)
    rows = (blocks[0].shape[0] - note) // 2
    size = blocks[0].shape[0] - rows
    return pl.pallas_call(
        functools.partial(forward_kernel, parts, rows),
        out_shape=jax.ShapeDtypeStruct((parts * size, blocks[0].shape[1]), blocks[0].dtype),
        in_specs=[VM] * parts + [ANY] * len(after),
        out_specs=VM,
        compiler_params=params(4),
        name="forward",
    )(*blocks, *after)


def join_kernel(parts, got_ref, *rest):
    rows = got_ref.shape[0] // parts
    for m, out in enumerate(rest[parts:]):
        out[rows:, :] = got_ref[m * rows : (m + 1) * rows, :]


def join(blocks, got):
    parts = len(blocks)
    return pl.pallas_call(
        functools.partial(join_kernel, parts),
        out_shape=[jax.ShapeDtypeStruct(block.shape, block.dtype) for block in blocks],
        in_specs=[VM] * (1 + parts),
        out_specs=[VM] * parts,
        input_output_aliases={1 + m: m for m in range(parts)},
        compiler_params=params(4),
        name="join",
    )(got, *blocks)


def forward_rows_kernel(tok, hd, pieces, *refs):
    for m, row in enumerate(pieces):
        for head, (n, start, lane) in enumerate(row):
            block = refs[n][start + tok : start + 2 * tok, lane : lane + hd]
            refs[-1][m * tok : (m + 1) * tok, head * hd : (head + 1) * hd] = block


def forward_rows(arrays, pieces, tok, hd, after):
    return pl.pallas_call(
        functools.partial(forward_rows_kernel, tok, hd, pieces),
        out_shape=jax.ShapeDtypeStruct(
            (len(pieces) * tok, len(pieces[0]) * hd), arrays[0].dtype
        ),
        in_specs=[VM] * len(arrays) + [ANY],
        out_specs=VM,
        compiler_params=params(4),
        name="forward_rows",
    )(*arrays, after)


def assemble_kernel(tok, hd, pieces, me_ref, *rest):
    refs, got, out, sems = rest[:-3], rest[-3], rest[-2], rest[-1]
    me = me_ref[0]
    heads = len(pieces[0])
    moves = []
    for m, row in enumerate(pieces):
        for head, (n, start, lane) in enumerate(row):
            column = (me ^ (2 * m)) * heads * hd + head * hd
            moves.append((refs[n].at[pl.ds(start, tok), pl.ds(lane, hd)], column, hd))
        column = (me ^ (2 * m + 1)) * heads * hd
        moves.append((got.at[pl.ds(m * tok, tok), :], column, heads * hd))
    copies = [
        pltpu.make_async_copy(
            source, out.at[:, pl.ds(pl.multiple_of(column, LANES), width)], sems.at[n]
        )
        for n, (source, column, width) in enumerate(moves)
    ]
    for copy in copies:
        copy.start()
    for copy in copies:
        copy.wait()


def assemble(me, arrays, pieces, got, tok, hd):
    half, heads = len(pieces), len(pieces[0])
    return pl.pallas_call(
        functools.partial(assemble_kernel, tok, hd, pieces),
        out_shape=jax.ShapeDtypeStruct((tok, 2 * half * heads * hd), got.dtype),
        in_specs=[SMEM] + [VM] * (len(arrays) + 1),
        out_specs=ANY,
        scratch_shapes=[pltpu.SemaphoreType.DMA((half * (heads + 1),))],
        compiler_params=params(4),
        name="assemble",
    )(me, *arrays, got)


def soft(scores, scale):
    top = jnp.max(scores, axis=0, keepdims=True)
    expo = jnp.exp2((scores - top) * scale)
    return expo, jnp.sum(expo, axis=0, keepdims=True)


def masked_weights(scores, mask, slots, scale):
    rows, tok = scores.shape
    bias = (mask.astype(jnp.float32)[:slots] - 1.0) * (-HIDDEN)
    scores = scores.reshape(slots, rows // slots, tok) + bias[:, None, :]
    expo, norm = soft(scores.reshape(rows, tok), scale)
    return (expo * (1.0 / norm)).astype(jnp.bfloat16)


def window(me, p, count):
    slab = me ^ p
    low = jnp.where(slab > 0, (slab - 1) ^ me, p)
    high = jnp.where(slab < count - 1, (slab + 1) ^ me, p)
    return low, p, high


def log_scale(hd):
    return hd ** (-0.5) * math.log2(math.e)


def attention_kernel(
    count, tok, hd, nh, slots, rank, before, last, factor, me_ref, *rest
):
    half = count // 2
    noted, rest = rest[: half + 1], rest[half + 1 :]
    if before:
        blocks, rest = rest[:half], rest[half:]
    up_ref, rest = rest[0], rest[1:]
    if before:
        hid_ref, gup_in, *rest = rest
    outs, rest = rest[:half], rest[half:]
    if last:
        hid_keep, hid_send, gup_ref, *rest = rest
    else:
        hid_out, gup_ref, *rest = rest
    note_s, q_s, k_s, vt_s, svt_s, lora_s, grad_s, hid_s, out_s = rest
    head = pl.program_id(0)
    me = me_ref[0]
    scale = log_scale(hd)
    size = note_s.shape[1]

    @pl.when(head == 0)
    def _():
        part = noted[half].shape[0] // half
        for p in range(count):
            m = p // 2
            if p % 2:
                note_s[p] = noted[half][(m + 1) * part - size : (m + 1) * part, :]
            else:
                note_s[p] = noted[m][noted[m].shape[0] - size :, :]
            lora_s[:, p * tok : (p + 1) * tok] = note_s[p, :rank, :]
        if before:
            hid_s[...] = hid_ref[...]
            gup_ref[:, : before * hd] = gup_in[...]
        else:
            hid_s[...] = jnp.zeros_like(hid_s)

    for p in range(count):
        if before:
            ref, start = blocks[p // 2], p % 2 * nh * 3 * tok
        elif p % 2:
            ref, start = noted[half], p // 2 * (noted[half].shape[0] // half)
        else:
            ref, start = noted[p // 2], 0
        start = pl.multiple_of(start + head * 3 * tok, ROWS)
        q_s[p * tok : (p + 1) * tok, :] = ref[pl.ds(start, tok), :]
        k_s[p * tok : (p + 1) * tok, :] = ref[pl.ds(start + tok, tok), :]
        vt_s[:, p * tok : (p + 1) * tok] = ref[pl.ds(start + 2 * tok, tok), :].T
    up_t = up_ref[...]
    for p in range(count):
        cols = slice(p * tok, (p + 1) * tok)
        term = mm(up_t, lora_s[:, cols], TN)
        svt_s[p] = (vt_s[:, cols].astype(jnp.float32) + term).astype(jnp.bfloat16)
    grad_s[...] = jnp.zeros_like(grad_s)

    for start in range(0, count, 4):
        slabs = range(start, min(start + 4, count))
        queries = [q_s[p * tok : (p + 1) * tok, :] for p in slabs]
        places = [window(me, p, count) for p in slabs]
        full = [mm(k_s[...], query, NT) for query in queries]
        seen = [
            mm(
                jnp.concatenate(
                    [k_s[pl.ds(pl.multiple_of(w * tok, tok), tok), :] for w in place], axis=0
                ),
                query,
                NT,
            )
            for place, query in zip(places, queries)
        ]
        full = [soft(x, scale) for x in full]
        teachers = [mm(vt_s[...], expo.astype(jnp.bfloat16)) for expo, _ in full]
        weights = [
            masked_weights(x, note_s[p, rank:, :], slots, scale) for p, x in zip(slabs, seen)
        ]
        students = [
            mm(jnp.concatenate([svt_s[w] for w in place], axis=1), weight)
            for place, weight in zip(places, weights)
        ]
        deltas = []
        for (_, norm), teacher, student in zip(full, teachers, students):
            teacher = (teacher / norm).astype(jnp.bfloat16).astype(jnp.float32)
            deltas.append(((student - teacher) * factor).astype(jnp.bfloat16))
        grads = [mm(weight, delta, NT) for weight, delta in zip(weights, deltas)]
        for p, place, student, grad in zip(slabs, places, students, grads):
            out_s[p] = student.T.astype(jnp.bfloat16)
            for n, w in enumerate(place):
                grad_s[w] += grad[n * tok : (n + 1) * tok]

    grad = grad_s[...].reshape(count * tok, hd).astype(jnp.bfloat16)
    column = pl.multiple_of(head * hd, LANES)
    for p in range(count):
        outs[p // 2][p % 2 * tok : (p % 2 + 1) * tok, pl.ds(column, hd)] = out_s[p]
    column = pl.multiple_of((before + head) * hd, LANES)
    gup_ref[:, pl.ds(column, hd)] = mm(lora_s[...], grad)
    hid_s[...] += mm(up_t, grad, NT)

    @pl.when(head == nh - 1)
    def _():
        if last:
            for m in range(half):
                to = slice(m * tok, (m + 1) * tok)
                hid_keep[:, to] = hid_s[:, 2 * m * tok : (2 * m + 1) * tok]
                odd = hid_s[:, (2 * m + 1) * tok : (2 * m + 2) * tok]
                hid_send[:, to] = odd.astype(jnp.bfloat16)
        else:
            hid_out[...] = hid_s[...]


def attention(me, blocks, noted, up_t, given, first, nh, tok, hd, slots, mask_rows, last):
    count = 2 * len(noted) - 2
    rank = up_t.shape[0]
    bf, f32 = jnp.bfloat16, jnp.float32
    keys = count * tok
    heads = first + nh
    shapes = [jax.ShapeDtypeStruct((2 * tok, nh * hd), bf)] * (count // 2)
    if last:
        shapes += [
            jax.ShapeDtypeStruct((rank, keys // 2), f32),
            jax.ShapeDtypeStruct((rank, keys // 2), bf),
        ]
    else:
        shapes += [jax.ShapeDtypeStruct((rank, keys), f32)]
    shapes += [jax.ShapeDtypeStruct((rank, heads * hd), f32)]
    return pl.pallas_call(
        functools.partial(
            attention_kernel,
            count,
            tok,
            hd,
            nh,
            slots,
            rank,
            first,
            last,
            keys ** (-0.5),
        ),
        grid=(nh,),
        out_shape=shapes,
        in_specs=[SMEM]
        + [VM] * (len(noted) + len(blocks))
        + [pl.BlockSpec((rank, hd), lambda h: (0, first + h))]
        + [VM] * len(given),
        out_specs=[VM] * len(shapes),
        scratch_shapes=[
            pltpu.VMEM((count, rank + mask_rows, tok), bf),
            pltpu.VMEM((keys, hd), bf),
            pltpu.VMEM((keys, hd), bf),
            pltpu.VMEM((hd, keys), bf),
            pltpu.VMEM((count, hd, tok), bf),
            pltpu.VMEM((rank, keys), bf),
            pltpu.VMEM((count, tok, hd), f32),
            pltpu.VMEM((rank, keys), f32),
            pltpu.VMEM((count, tok, hd), bf),
        ],
        compiler_params=params(30),
        cost_estimate=pl.CostEstimate(
            flops=nh * 4 * 10**9, bytes_accessed=4 * nh * keys * hd * 2, transcendentals=0
        ),
        name="attention",
    )(
        me,
        *noted,
        *blocks,
        up_t,
        *given,
    )


def pair_kernel(parts, counts, keep_ref, got_ref, *rest):
    riders, outs = rest[:-parts], rest[-parts:]
    rank, width = keep_ref.shape[0], keep_ref.shape[1] // parts
    for m in range(parts):
        cols = slice(m * width, (m + 1) * width)
        total = keep_ref[:, cols] + got_ref[:, cols].astype(jnp.float32)
        outs[m][:rank, :] = total.astype(outs[m].dtype)
        row = rank
        for rider in riders[sum(counts[:m]) : sum(counts[: m + 1])]:
            size = rider.shape[0]
            for lane in range(0, rider.shape[1], width):
                outs[m][row : row + size, :] = rider[:, lane : lane + width]
                row += size


def pair_sum(keep, got, parts, riders):
    rank, width = keep.shape[0], keep.shape[1] // parts
    extra = [sum(rider.size for rider in group) // width for group in riders]
    shapes = [
        jax.ShapeDtypeStruct((rank + more, width), jnp.bfloat16 if m else jnp.float32)
        for m, more in enumerate(extra)
    ]
    counts = [len(group) for group in riders]
    return pl.pallas_call(
        functools.partial(pair_kernel, parts, counts),
        out_shape=shapes,
        in_specs=[VM] * (2 + sum(counts)),
        out_specs=[VM] * parts,
        compiler_params=params(4),
        name="pair_sum",
    )(keep, got, *[rider for group in riders for rider in group])


def chip_terms(keep, send, count, riders=None):
    half = count // 2
    return chips(pair_sum(keep, swap(send, count, 1), half, riders or [[]] * half), count)


def down_kernel(count, group, me_ref, *rest):
    parts = rest[: count // 2]
    x_ref, keep_ref, send_ref = rest[count // 2 :]
    me = me_ref[0]
    hidden = parts[0][...]
    for part in parts[1:]:
        hidden += part[: hidden.shape[0], :].astype(jnp.float32)
    hidden = hidden.astype(jnp.bfloat16)
    for k in range(count):
        column = pl.multiple_of((me ^ k) * group, LANES)
        term = mm(hidden, x_ref[:, pl.ds(column, group)])
        to = (send_ref, keep_ref)[k % 2 == 0]
        to[:, k // 2 * group : (k // 2 + 1) * group] = term.astype(to.dtype)


def down_terms(me, parts, x):
    count = 2 * len(parts)
    model = x.shape[1]
    rank = parts[0].shape[0]
    return pl.pallas_call(
        functools.partial(down_kernel, count, model // count),
        out_shape=[
            jax.ShapeDtypeStruct((rank, model // 2), jnp.float32),
            jax.ShapeDtypeStruct((rank, model // 2), jnp.bfloat16),
        ],
        in_specs=[SMEM] + [VM] * (len(parts) + 1),
        out_specs=[VM, VM],
        compiler_params=params(8),
        name="down_terms",
    )(me, *parts, x)


def sum_kernel(*refs):
    total = refs[0][...]
    for ref in refs[1:-1]:
        total += ref[...].astype(jnp.float32)
    refs[-1][...] = total


def sum_terms(parts):
    return pl.pallas_call(
        sum_kernel,
        out_shape=jax.ShapeDtypeStruct(parts[0].shape, jnp.float32),
        in_specs=[VM] * len(parts),
        out_specs=VM,
        compiler_params=params(8),
        name="sum_terms",
    )(*parts)


def apart(always, phase, *operands):
    def never(*operands):
        shapes = jax.eval_shape(phase, *operands)
        return jax.tree.map(lambda shape: jnp.zeros(shape.shape, shape.dtype), shapes)

    return lax.cond(always, phase, never, *operands)


def head_chunks(per_group):
    if per_group < 2:
        return [(0, per_group)]
    return [(0, per_group - 1), (per_group - 1, 1)]


def local(
    queries, keys, values, value_layer_input, adapter_down_weight, adapter_up_weight, neighbors
):
    tok, model = queries.shape
    rank = adapter_down_weight.shape[1]
    count = lax.axis_size("context")
    index = lax.axis_index("context")
    me = index.astype(jnp.int32).reshape(1)
    hd = model // H
    group = model // count
    per_group = H // count
    tiles = neighbors.shape[0]
    slots = 3 * tiles
    chunks = head_chunks(per_group)

    mask_rows = slots + -slots % 16

    down_t = adapter_down_weight.T
    up_t = adapter_up_weight.T

    note = rank + mask_rows
    first_own = first_pack(
        me, neighbors, queries, keys, values, value_layer_input, down_t,
        count, hd, chunks[0][1], mask_rows,
    )
    joined = [[]]
    for first, nh in chunks[1:]:
        *own, send = pack(me, queries, keys, values, first_own[0], count, hd, first, nh)
        joined.append(join(own, swap(send, count, 1)))
    noted = chips(first_own, count)
    ready = [own[0] for own in joined[1:]]
    noted = noted + [swap(forward(noted, note, ready), count, 1)]
    messages = [chips(own, count) if own else [] for own in joined]

    own_up = lax.dynamic_slice_in_dim(up_t, index * group, group, 1)
    half = count // 2
    given, arrays = [], []
    riders = [[] for _ in range(half)]
    pieces = [[] for _ in range(half)]
    rows = [rank] * half
    for c, (first, nh) in enumerate(chunks):
        last = c == len(chunks) - 1
        out = attention(
            me, messages[c], noted, own_up, given, first, nh, tok, hd, slots, mask_rows, last
        )
        given = out[half:]
        for m in range(half):
            if m and (last or m == 1):
                riders[m].append(out[m])
                for _ in range(nh):
                    pieces[m].append((m - half, rows[m], 0))
                    rows[m] += 2 * tok
            else:
                pieces[m] += [(len(arrays), 0, h * hd) for h in range(nh)]
                arrays.append(swap(out[m], count, 2 * m) if m else out[0])
    hid_keep, hid_send, grad_up = given

    def hidden_phase(hid_keep, hid_send, riders):
        return chip_terms(hid_keep, hid_send, count, riders)

    def grad_phase(keep, send, _):
        return sum_terms(chip_terms(keep, send, count))

    hidden = apart(index < count, hidden_phase, hid_keep, hid_send, riders)
    keep, send = down_terms(me, hidden, value_layer_input)
    pieces = [
        [(n if n >= 0 else len(arrays) + n + half - 1, row, lane) for n, row, lane in group]
        for group in pieces
    ]
    arrays += hidden[1:]
    passed = forward_rows(arrays, pieces, tok, hd, keep)
    got = swap(passed, count, 1)
    grad_down = apart(index < count, grad_phase, keep, send, passed)
    student_out = assemble(me, arrays, pieces, got, tok, hd)
    return student_out, grad_down.T, grad_up.T


def solution(mesh):
    rows = P(("video", "context"), None)
    return jax.shard_map(
        local,
        mesh=mesh,
        in_specs=(rows, rows, rows, rows, P(), P(), rows),
        out_specs=(rows, rows, rows),
        check_vma=False,
    )
```

```python
import functools
import math

import jax
import jax.numpy as jnp
from jax import lax
from jax.experimental import pallas as pl
from jax.experimental.pallas import tpu as pltpu
from jax.sharding import PartitionSpec as P

H = 32
HIDDEN = -1e30
NT = (((1,), (1,)), ((), ()))
TN = (((0,), (0,)), ((), ()))
NN = (((1,), (0,)), ((), ()))


def mm(a, b, dims=NN):
    return lax.dot_general(a, b, dims, preferred_element_type=jnp.float32)


def params(mib):
    return pltpu.CompilerParams(vmem_limit_bytes=mib * 1024 * 1024)


SMEM = pl.BlockSpec(memory_space=pltpu.SMEM)
HBM = pl.BlockSpec(memory_space=pltpu.HBM)
ANY = pl.BlockSpec(memory_space=pl.ANY)
VM = pl.BlockSpec(memory_space=pltpu.VMEM)
LANES = 128
ROWS = 16
SMALL = pl.CostEstimate(flops=0, bytes_accessed=1 << 20, transcendentals=0)


def swap(block, count, bits, targets=None):
    pairs = [(i, i ^ bits) for i in range(count) if targets is None or i ^ bits in targets]
    return lax.ppermute(block, "context", pairs)


def chips(blocks, count, targets=None):
    got = [blocks[0]] + [None] * (len(blocks) - 1)
    for m in sorted(range(1, len(blocks)), key=lambda m: -m):
        got[m] = swap(blocks[m], count, 2 * m, targets)
    return got


def pack_copies(count, group, hd, first, nh, me, refs, place, sems):
    tok = refs[0].shape[0]
    copies = []
    for k in range(count):
        for h in range(nh):
            column = pl.multiple_of((me ^ k) * group + (first + h) * hd, LANES)
            for t, ref in enumerate(refs):
                row = (h * 3 + t) * tok
                copies.append(
                    pltpu.make_async_copy(
                        ref.at[:, pl.ds(column, hd)],
                        place(k, row, tok),
                        sems.at[(k * nh + h) * 3 + t],
                    )
                )
    return copies


def pack_kernel(count, group, hd, first, nh, me_ref, q_ref, k_ref, v_ref, _, *rest):
    outs, sems = rest[:-1], rest[-1]
    chunk = nh * 3 * q_ref.shape[0]

    def place(k, row, size):
        if k % 2:
            return outs[-1].at[pl.ds(k // 2 * chunk + row, size), :]
        return outs[k // 2].at[pl.ds(row, size), :]

    copies = pack_copies(
        count, group, hd, first, nh, me_ref[0], (q_ref, k_ref, v_ref), place, sems
    )
    for copy in copies:
        copy.start()
    for copy in copies:
        copy.wait()


def pack(me, q, k, v, after, count, hd, first, nh):
    tok, model = q.shape
    rows = nh * 3 * tok
    shapes = [jax.ShapeDtypeStruct((2 * rows, hd), q.dtype)] * (count // 2)
    return pl.pallas_call(
        functools.partial(pack_kernel, count, model // count, hd, first, nh),
        out_shape=shapes + [jax.ShapeDtypeStruct((count // 2 * rows, hd), q.dtype)],
        in_specs=[SMEM, HBM, HBM, HBM, ANY],
        out_specs=[VM] * (count // 2 + 1),
        scratch_shapes=[pltpu.SemaphoreType.DMA((3 * nh * count,))],
        compiler_params=params(8),
        cost_estimate=SMALL,
        name="pack",
    )(me, q, k, v, after)


def first_kernel(count, group, hd, nh, mask_rows, tiles, me_ref, nb_ref, *rest):
    q_ref, k_ref, v_ref, x_ref, down_ref = rest[:5]
    outs, rest = rest[5 : 5 + count // 2], rest[5 + count // 2 :]
    x_s, down_s, sems, in_sems = rest
    me = me_ref[0]
    tok = q_ref.shape[0]
    rank = down_ref.shape[0]
    chunk = nh * 3 * tok

    def place(k, row, size):
        return outs[k // 2].at[pl.ds(k % 2 * chunk + row, size), :]

    copies = pack_copies(count, group, hd, 0, nh, me, (q_ref, k_ref, v_ref), place, sems)
    loads = [
        pltpu.make_async_copy(x_ref, x_s, in_sems.at[0]),
        pltpu.make_async_copy(down_ref, down_s, in_sems.at[1]),
    ]
    for copy in loads + copies:
        copy.start()
    rows = lax.broadcasted_iota(jnp.int32, (mask_rows, tok), 0)
    lane_tile = lax.broadcasted_iota(jnp.int32, (mask_rows, tok), 1) // (tok // tiles)
    seen = jnp.zeros((mask_rows, tok), jnp.float32)
    for t in range(tiles):
        for n in range(nb_ref.shape[1]):
            slot = nb_ref[t, n] - (me - 1) * tiles
            seen = jnp.where((rows == slot) & (lane_tile == t), 1.0, seen)
    for copy in loads:
        copy.wait()
    lora = mm(down_s[...], x_s[...], NT).astype(jnp.bfloat16)
    note = jnp.concatenate([lora, seen.astype(jnp.bfloat16)], axis=0)
    for out in outs:
        out[2 * chunk :, :] = note
    for copy in copies:
        copy.wait()


def first_pack(me, nb, q, k, v, x, down, count, hd, nh, mask_rows):
    tok, model = q.shape
    rows = 2 * nh * 3 * tok + down.shape[0] + mask_rows
    bf = q.dtype
    return pl.pallas_call(
        functools.partial(
            first_kernel, count, model // count, hd, nh, mask_rows, nb.shape[0]
        ),
        out_shape=[jax.ShapeDtypeStruct((rows, hd), bf)] * (count // 2),
        in_specs=[SMEM, SMEM] + [HBM] * 5,
        out_specs=[VM] * (count // 2),
        scratch_shapes=[
            pltpu.VMEM(x.shape, bf),
            pltpu.VMEM(down.shape, bf),
            pltpu.SemaphoreType.DMA((3 * nh * count,)),
            pltpu.SemaphoreType.DMA((2,)),
        ],
        compiler_params=params(60),
        name="first_pack",
    )(me, nb, q, k, v, x, down)


def forward_kernel(parts, rows, *refs):
    size = refs[0].shape[0] - rows
    for m in range(parts):
        refs[-1][m * size : (m + 1) * size, :] = refs[m][rows:, :]


def forward(blocks, note, after):
    parts = len(blocks)
    rows = (blocks[0].shape[0] - note) // 2
    size = blocks[0].shape[0] - rows
    return pl.pallas_call(
        functools.partial(forward_kernel, parts, rows),
        out_shape=jax.ShapeDtypeStruct((parts * size, blocks[0].shape[1]), blocks[0].dtype),
        in_specs=[VM] * parts + [ANY] * len(after),
        out_specs=VM,
        compiler_params=params(4),
        cost_estimate=SMALL,
        name="forward",
    )(*blocks, *after)


def join_kernel(parts, got_ref, *rest):
    rows = got_ref.shape[0] // parts
    for m, out in enumerate(rest[parts:]):
        out[rows:, :] = got_ref[m * rows : (m + 1) * rows, :]


def join(blocks, got):
    parts = len(blocks)
    return pl.pallas_call(
        functools.partial(join_kernel, parts),
        out_shape=[jax.ShapeDtypeStruct(block.shape, block.dtype) for block in blocks],
        in_specs=[VM] * (1 + parts),
        out_specs=[VM] * parts,
        input_output_aliases={1 + m: m for m in range(parts)},
        compiler_params=params(4),
        cost_estimate=SMALL,
        name="join",
    )(got, *blocks)


def release_kernel(*refs):
    pass


def release(blocks, after):
    return pl.pallas_call(
        release_kernel,
        out_shape=[jax.ShapeDtypeStruct(block.shape, block.dtype) for block in blocks],
        in_specs=[ANY] * (len(blocks) + len(after)),
        out_specs=[ANY] * len(blocks),
        input_output_aliases={n: n for n in range(len(blocks))},
        compiler_params=params(4),
        cost_estimate=SMALL,
        name="release",
    )(*blocks, *after)


def forward_rows_kernel(tok, hd, pieces, *refs):
    for m, row in enumerate(pieces):
        for head, (n, start, lane) in enumerate(row):
            block = refs[n][start + tok : start + 2 * tok, lane : lane + hd]
            refs[-1][m * tok : (m + 1) * tok, head * hd : (head + 1) * hd] = block


def forward_rows(arrays, pieces, tok, hd):
    return pl.pallas_call(
        functools.partial(forward_rows_kernel, tok, hd, pieces),
        out_shape=jax.ShapeDtypeStruct(
            (len(pieces) * tok, len(pieces[0]) * hd), arrays[0].dtype
        ),
        in_specs=[VM] * len(arrays),
        out_specs=VM,
        compiler_params=params(4),
        cost_estimate=SMALL,
        name="forward_rows",
    )(*arrays)


def assemble_kernel(group, moves, me_ref, *rest):
    refs, out, sems = rest[:-2], rest[-2], rest[-1]
    me = me_ref[0]
    copies = []
    for n, (array, row, size, lane, width, k, start, to) in enumerate(moves):
        column = pl.multiple_of((me ^ k) * group + start, LANES)
        copies.append(
            pltpu.make_async_copy(
                refs[array].at[pl.ds(row, size), pl.ds(lane, width)],
                out.at[pl.ds(to, size), pl.ds(column, width)],
                sems.at[n],
            )
        )
    for copy in copies:
        copy.start()
    for copy in copies:
        copy.wait()


def assemble(me, arrays, moves, group, tok, model, base=None):
    given = [] if base is None else [base]
    kernel = functools.partial(assemble_kernel, group, moves)
    if given:
        kernel = lambda me_ref, _, *rest: assemble_kernel(group, moves, me_ref, *rest)
    return pl.pallas_call(
        kernel,
        out_shape=jax.ShapeDtypeStruct((tok, model), arrays[0].dtype),
        in_specs=[SMEM] + [ANY] * len(given) + [VM] * len(arrays),
        out_specs=ANY,
        input_output_aliases={1: 0} if given else {},
        scratch_shapes=[pltpu.SemaphoreType.DMA((len(moves),))],
        compiler_params=params(4),
        cost_estimate=SMALL,
        name="assemble",
    )(me, *given, *arrays)


def soft(scores, scale):
    top = jnp.max(scores, axis=0, keepdims=True)
    expo = jnp.exp2((scores - top) * scale)
    return expo, jnp.sum(expo, axis=0, keepdims=True)


def masked_weights(scores, mask, slots, scale):
    rows, tok = scores.shape
    bias = (mask.astype(jnp.float32)[:slots] - 1.0) * (-HIDDEN)
    scores = scores.reshape(slots, rows // slots, tok) + bias[:, None, :]
    expo, norm = soft(scores.reshape(rows, tok), scale)
    return (expo * (1.0 / norm)).astype(jnp.bfloat16)


def window(me, p, count):
    slab = me ^ p
    low = jnp.where(slab > 0, (slab - 1) ^ me, p)
    high = jnp.where(slab < count - 1, (slab + 1) ^ me, p)
    return low, p, high


def log_scale(hd):
    return hd ** (-0.5) * math.log2(math.e)


def attention_kernel(
    count, tok, hd, nh, slots, rank, before, last, factor, me_ref, *rest
):
    half = count // 2
    noted, rest = rest[: half + 1], rest[half + 1 :]
    if before:
        blocks, rest = rest[:half], rest[half:]
    up_ref, rest = rest[0], rest[1:]
    if before:
        hid_ref, gup_in, *rest = rest
    outs, rest = rest[:half], rest[half:]
    if last:
        send_ref, *rest = rest
    hid_out, gup_ref, *rest = rest
    note_s, q_s, k_s, vt_s, svt_s, lora_s, grad_s, hid_s, out_s = rest
    head = pl.program_id(0)
    me = me_ref[0]
    scale = log_scale(hd)
    size = note_s.shape[1]

    @pl.when(head == 0)
    def _():
        part = noted[half].shape[0] // half
        for p in range(count):
            m = p // 2
            if p % 2:
                note_s[p] = noted[half][(m + 1) * part - size : (m + 1) * part, :]
            else:
                note_s[p] = noted[m][noted[m].shape[0] - size :, :]
            lora_s[:, p * tok : (p + 1) * tok] = note_s[p, :rank, :]
        if before:
            hid_s[...] = hid_ref[...]
            gup_ref[:, : before * hd] = gup_in[...]
        else:
            hid_s[...] = jnp.zeros_like(hid_s)

    for p in range(count):
        if before:
            ref, start = blocks[p // 2], p % 2 * nh * 3 * tok
        elif p % 2:
            ref, start = noted[half], p // 2 * (noted[half].shape[0] // half)
        else:
            ref, start = noted[p // 2], 0
        start = pl.multiple_of(start + head * 3 * tok, ROWS)
        q_s[p * tok : (p + 1) * tok, :] = ref[pl.ds(start, tok), :]
        k_s[p * tok : (p + 1) * tok, :] = ref[pl.ds(start + tok, tok), :]
        vt_s[:, p * tok : (p + 1) * tok] = ref[pl.ds(start + 2 * tok, tok), :].T
    up_t = up_ref[...]
    for p in range(count):
        cols = slice(p * tok, (p + 1) * tok)
        term = mm(up_t, lora_s[:, cols], TN)
        svt_s[p] = (vt_s[:, cols].astype(jnp.float32) + term).astype(jnp.bfloat16)
    grad_s[...] = jnp.zeros_like(grad_s)

    for start in range(0, count, 4):
        slabs = range(start, min(start + 4, count))
        queries = [q_s[p * tok : (p + 1) * tok, :] for p in slabs]
        places = [window(me, p, count) for p in slabs]
        full = [mm(k_s[...], query, NT) for query in queries]
        seen = [
            mm(
                jnp.concatenate(
                    [k_s[pl.ds(pl.multiple_of(w * tok, tok), tok), :] for w in place], axis=0
                ),
                query,
                NT,
            )
            for place, query in zip(places, queries)
        ]
        full = [soft(x, scale) for x in full]
        teachers = [mm(vt_s[...], expo.astype(jnp.bfloat16)) for expo, _ in full]
        weights = [
            masked_weights(x, note_s[p, rank:, :], slots, scale) for p, x in zip(slabs, seen)
        ]
        students = [
            mm(jnp.concatenate([svt_s[w] for w in place], axis=1), weight)
            for place, weight in zip(places, weights)
        ]
        deltas = []
        for (_, norm), teacher, student in zip(full, teachers, students):
            teacher = (teacher / norm).astype(jnp.bfloat16).astype(jnp.float32)
            deltas.append(((student - teacher) * factor).astype(jnp.bfloat16))
        grads = [mm(weight, delta, NT) for weight, delta in zip(weights, deltas)]
        for p, place, student, grad in zip(slabs, places, students, grads):
            out_s[p] = student.T.astype(jnp.bfloat16)
            for n, w in enumerate(place):
                grad_s[w] += grad[n * tok : (n + 1) * tok]

    grad = grad_s[...].reshape(count * tok, hd).astype(jnp.bfloat16)
    column = pl.multiple_of(head * hd, LANES)
    for p in range(count):
        to, row = outs[p // 2], p % 2 * tok
        if last and p % 2:
            to, row = send_ref, p // 2 * tok
        to[row : row + tok, pl.ds(column, hd)] = out_s[p]
    column = pl.multiple_of((before + head) * hd, LANES)
    gup_ref[:, pl.ds(column, hd)] = mm(lora_s[...], grad)
    hid_s[...] += mm(up_t, grad, NT)

    @pl.when(head == nh - 1)
    def _():
        if last:
            for m in range(half):
                even = slice(2 * m * tok, (2 * m + 1) * tok)
                odd = slice((2 * m + 1) * tok, (2 * m + 2) * tok)
                row = half * tok + m * rank
                hid_out[:, m * tok : (m + 1) * tok] = hid_s[:, even]
                send_ref[row : row + rank, :] = hid_s[:, odd].astype(jnp.bfloat16)
        else:
            hid_out[...] = hid_s[...]


def attention(me, blocks, noted, up_t, given, first, nh, tok, hd, slots, mask_rows, last):
    count = 2 * len(noted) - 2
    rank = up_t.shape[0]
    bf, f32 = jnp.bfloat16, jnp.float32
    keys = count * tok
    heads = first + nh
    half = count // 2
    shapes = [jax.ShapeDtypeStruct(((1 if last else 2) * tok, nh * hd), bf)] * half
    if last:
        shapes.append(jax.ShapeDtypeStruct((half * (tok + rank), nh * hd), bf))
    shapes += [
        jax.ShapeDtypeStruct((rank, keys // 2 if last else keys), f32),
        jax.ShapeDtypeStruct((rank, heads * hd), f32),
    ]
    return pl.pallas_call(
        functools.partial(
            attention_kernel,
            count,
            tok,
            hd,
            nh,
            slots,
            rank,
            first,
            last,
            keys ** (-0.5),
        ),
        grid=(nh,),
        out_shape=shapes,
        in_specs=[SMEM]
        + [VM] * (len(noted) + len(blocks))
        + [pl.BlockSpec((rank, hd), lambda h: (0, first + h))]
        + [VM] * len(given),
        out_specs=[VM] * len(shapes),
        scratch_shapes=[
            pltpu.VMEM((count, rank + mask_rows, tok), bf),
            pltpu.VMEM((keys, hd), bf),
            pltpu.VMEM((keys, hd), bf),
            pltpu.VMEM((hd, keys), bf),
            pltpu.VMEM((count, hd, tok), bf),
            pltpu.VMEM((rank, keys), bf),
            pltpu.VMEM((count, tok, hd), f32),
            pltpu.VMEM((rank, keys), f32),
            pltpu.VMEM((count, tok, hd), bf),
        ],
        compiler_params=params(30),
        cost_estimate=pl.CostEstimate(
            flops=nh * 4 * 10**9, bytes_accessed=4 * nh * keys * hd * 2, transcendentals=0
        ),
        name="attention",
    )(
        me,
        *noted,
        *blocks,
        up_t,
        *given,
    )


def pair_kernel(parts, keep_ref, got_ref, *rest):
    riders, outs = rest[:-parts], rest[-parts:]
    rank, width = keep_ref.shape[0], keep_ref.shape[1] // parts
    for m in range(parts):
        cols = slice(m * width, (m + 1) * width)
        total = keep_ref[:, cols] + got_ref[:, cols].astype(jnp.float32)
        outs[m][:rank, :] = total.astype(outs[m].dtype)
        if m:
            rider = riders[m - 1]
            lanes = rider.shape[1]
            size = outs[m].shape[0] - rank
            for n in range(width // lanes):
                block = rider[n * size : (n + 1) * size, :]
                outs[m][rank:, n * lanes : (n + 1) * lanes] = block


def pair_sum(keep, got, parts, riders):
    rank, width = keep.shape[0], keep.shape[1] // parts
    shapes = [jax.ShapeDtypeStruct((rank, width), jnp.float32)] + [
        jax.ShapeDtypeStruct((rank + rider.size // width, width), rider.dtype)
        for rider in riders
    ]
    return pl.pallas_call(
        functools.partial(pair_kernel, parts),
        out_shape=shapes,
        in_specs=[VM] * (2 + len(riders)),
        out_specs=[VM] * parts,
        compiler_params=params(4),
        cost_estimate=SMALL,
        name="pair_sum",
    )(keep, got, *riders)


def riding_kernel(parts, keep_ref, got_ref, *rest):
    blocks, rest = rest[:parts], rest[parts:]
    riders, (total_ref, *outs) = rest[: -2 * parts], rest[-2 * parts :]
    joined, sends = outs[:parts], outs[parts:]
    rank, tok = total_ref.shape
    for m in range(parts):
        row = parts * tok + m * rank
        total = keep_ref[:, m * tok : (m + 1) * tok]
        total += got_ref[row : row + rank, :].astype(jnp.float32)
        if m:
            sends[m - 1][:rank, :] = total.astype(jnp.bfloat16)
        else:
            total_ref[...] = total
        joined[m][:tok, :] = blocks[m][...]
        joined[m][tok:, :] = got_ref[m * tok : (m + 1) * tok, :]
    row = rank
    for rider in riders:
        for lane in range(0, rider.shape[1], tok):
            sends[0][row : row + 2 * tok, :] = rider[:, lane : lane + tok]
            row += 2 * tok


def riding_sum(keep, got, blocks, riders):
    parts = len(blocks)
    (tok, hd), rank, bf = blocks[0].shape, keep.shape[0], blocks[0].dtype
    extra = sum(rider.size for rider in riders) // tok
    shapes = (
        [jax.ShapeDtypeStruct((rank, tok), jnp.float32)]
        + [jax.ShapeDtypeStruct((2 * tok, hd), bf)] * parts
        + [
            jax.ShapeDtypeStruct((rank + (extra if m == 1 else 0), tok), bf)
            for m in range(1, parts)
        ]
    )
    return pl.pallas_call(
        functools.partial(riding_kernel, parts),
        out_shape=shapes,
        in_specs=[VM] * (2 + parts + len(riders)),
        out_specs=[VM] * len(shapes),
        compiler_params=params(4),
        cost_estimate=SMALL,
        name="riding_sum",
    )(keep, got, *blocks, *riders)


def down_kernel(count, group, me_ref, *rest):
    parts = rest[: count // 2]
    x_ref, keep_ref, send_ref = rest[count // 2 :]
    me = me_ref[0]
    hidden = parts[0][...]
    for part in parts[1:]:
        hidden += part[: hidden.shape[0], :].astype(jnp.float32)
    hidden = hidden.astype(jnp.bfloat16)
    for k in range(count):
        column = pl.multiple_of((me ^ k) * group, LANES)
        term = mm(hidden, x_ref[:, pl.ds(column, group)])
        to = (send_ref, keep_ref)[k % 2 == 0]
        to[:, k // 2 * group : (k // 2 + 1) * group] = term.astype(to.dtype)


def down_terms(me, parts, x):
    count = 2 * len(parts)
    model = x.shape[1]
    rank = parts[0].shape[0]
    return pl.pallas_call(
        functools.partial(down_kernel, count, model // count),
        out_shape=[
            jax.ShapeDtypeStruct((rank, model // 2), jnp.float32),
            jax.ShapeDtypeStruct((rank, model // 2), jnp.bfloat16),
        ],
        in_specs=[SMEM] + [VM] * (len(parts) + 1),
        out_specs=[VM, VM],
        compiler_params=params(8),
        cost_estimate=SMALL,
        name="down_terms",
    )(me, *parts, x)


def sum_kernel(*refs):
    total = refs[0][...]
    for ref in refs[1:-2]:
        total += ref[: total.shape[0], :].astype(jnp.float32)
    refs[-1][...] = total


def sum_terms(parts, after):
    return pl.pallas_call(
        sum_kernel,
        out_shape=jax.ShapeDtypeStruct(parts[0].shape, jnp.float32),
        in_specs=[VM] * len(parts) + [ANY],
        out_specs=VM,
        compiler_params=params(4),
        cost_estimate=SMALL,
        name="sum_terms",
    )(*parts, after)


def apart(always, phase, *operands):
    def never(*operands):
        shapes = jax.eval_shape(phase, *operands)
        return jax.tree.map(lambda shape: jnp.zeros(shape.shape, shape.dtype), shapes)

    return lax.cond(always, phase, never, *operands)


def head_chunks(per_group):
    if per_group < 2:
        return [(0, per_group)]
    return [(0, per_group - 1), (per_group - 1, 1)]


def local(
    queries, keys, values, value_layer_input, adapter_down_weight, adapter_up_weight, neighbors
):
    tok, model = queries.shape
    rank = adapter_down_weight.shape[1]
    count = lax.axis_size("context")
    index = lax.axis_index("context")
    me = index.astype(jnp.int32).reshape(1)
    hd = model // H
    group = model // count
    per_group = H // count
    tiles = neighbors.shape[0]
    slots = 3 * tiles
    chunks = head_chunks(per_group)

    mask_rows = slots + -slots % 16

    down_t = adapter_down_weight.T
    up_t = adapter_up_weight.T

    note = rank + mask_rows
    first_own = first_pack(
        me, neighbors, queries, keys, values, value_layer_input, down_t,
        count, hd, chunks[0][1], mask_rows,
    )
    joined = [[]]
    for first, nh in chunks[1:]:
        *own, send = pack(me, queries, keys, values, first_own[0], count, hd, first, nh)
        joined.append(join(own, swap(send, count, 1)))
    noted = chips(first_own, count)
    ready = [own[0] for own in joined[1:]]
    noted = noted + [swap(forward(noted, note, ready), count, 1)]
    messages = [chips(own, count) if own else [] for own in joined]

    own_up = lax.dynamic_slice_in_dim(up_t, index * group, group, 1)
    half = count // 2
    given, arrays, riders = [], [], []
    pieces = [[] for _ in range(half)]
    for c, (first, nh) in enumerate(chunks):
        last = c == len(chunks) - 1
        out = attention(
            me, messages[c], noted, own_up, given, first, nh, tok, hd, slots, mask_rows, last
        )
        blocks, given = list(out[:half]), out[-2:]
        if last:
            break
        riders.append(blocks[1])
        blocks[2:] = release(blocks[2:], messages[c + 1][1:])
        for m in [0] + list(range(2, half)):
            pieces[m] += [(len(arrays), 0, h * hd) for h in range(nh)]
            arrays.append(swap(blocks[m], count, 2 * m) if m else blocks[0])
        pieces[1] += [(-1, rank + 2 * tok * (first + h), 0) for h in range(nh)]
    pieces = [
        [(n if n >= 0 else len(arrays), row, lane) for n, row, lane in group] for group in pieces
    ]
    send, (hid, grad_up) = out[half], given

    def hidden_phase(hid, send, blocks, riders):
        total, *rest = riding_sum(hid, swap(send, count, 1), blocks, riders)
        return chips([total] + rest[half:], count), rest[:half]

    hidden, joined = apart(index < count, hidden_phase, hid, send, blocks, riders)
    keep, send = down_terms(me, hidden, value_layer_input)
    before = first * hd

    def grad_phase(keep, send, arrays, joined):
        base = None
        if before:
            got = swap(forward_rows(arrays, pieces, tok, hd), count, 1)
            moves = [(len(arrays), m * tok, tok, 0, before, 2 * m + 1, 0, 0) for m in range(half)]
            for m, group_pieces in enumerate(pieces):
                for h, (n, row, lane) in enumerate(group_pieces):
                    moves.append((n, row, tok, lane, hd, 2 * m, h * hd, 0))
            base = assemble(me, [*arrays, got], moves, group, tok, model)
        totals = pair_sum(keep, swap(send, count, 1), half, joined[1:])
        terms = chips(totals, count)
        moves = [(0, r * tok, tok, 0, nh * hd, r, before, 0) for r in range(2)]
        size = 2 * tok * nh * hd // group
        for m in range(1, half):
            step = min(size, tok)
            for row in range(0, 2 * tok, step):
                (r, to), (n, at) = divmod(row, tok), divmod(row, size)
                moves.append((m, rank + at, step, n * nh * hd, nh * hd, 2 * m + r, before, to))
        student_out = assemble(me, [joined[0], *terms[1:]], moves, group, tok, model, base)
        return sum_terms(terms, keep if base is None else base), student_out

    grad_down, student_out = apart(
        index < count, grad_phase, keep, send, [*arrays, hidden[1]], joined
    )
    return student_out, grad_down.T, grad_up.T


def solution(mesh):
    rows = P(("video", "context"), None)
    return jax.shard_map(
        local,
        mesh=mesh,
        in_specs=(rows, rows, rows, rows, P(), P(), rows),
        out_specs=(rows, rows, rows),
        check_vma=False,
    )
```

```python
import functools
import math

import jax
import jax.numpy as jnp
from jax import lax
from jax.experimental import pallas as pl
from jax.experimental.pallas import tpu as pltpu
from jax.sharding import PartitionSpec as P

H = 32
HIDDEN = -1e30
NT = (((1,), (1,)), ((), ()))
TN = (((0,), (0,)), ((), ()))
NN = (((1,), (0,)), ((), ()))


def mm(a, b, dims=NN):
    return lax.dot_general(a, b, dims, preferred_element_type=jnp.float32)


def params(mib):
    return pltpu.CompilerParams(vmem_limit_bytes=mib * 1024 * 1024)


SMEM = pl.BlockSpec(memory_space=pltpu.SMEM)
HBM = pl.BlockSpec(memory_space=pltpu.HBM)
ANY = pl.BlockSpec(memory_space=pl.ANY)
VM = pl.BlockSpec(memory_space=pltpu.VMEM)
LANES = 128
ROWS = 16
SMALL = pl.CostEstimate(flops=0, bytes_accessed=1 << 20, transcendentals=0)


def swap(block, count, bits, targets=None):
    pairs = [(i, i ^ bits) for i in range(count) if targets is None or i ^ bits in targets]
    return lax.ppermute(block, "context", pairs)


def chips(blocks, count, targets=None):
    got = [blocks[0]] + [None] * (len(blocks) - 1)
    for m in sorted(range(1, len(blocks)), key=lambda m: -m):
        got[m] = swap(blocks[m], count, 2 * m, targets)
    return got


def pack_copies(count, group, hd, first, nh, me, refs, place, sems):
    tok = refs[0].shape[0]
    copies = []
    for k in range(count):
        for h in range(nh):
            column = pl.multiple_of((me ^ k) * group + (first + h) * hd, LANES)
            for t, ref in enumerate(refs):
                row = (h * 3 + t) * tok
                copies.append(
                    pltpu.make_async_copy(
                        ref.at[:, pl.ds(column, hd)],
                        place(k, row, tok),
                        sems.at[(k * nh + h) * 3 + t],
                    )
                )
    return copies


def pack_kernel(count, group, hd, first, nh, me_ref, q_ref, k_ref, v_ref, _, *rest):
    outs, sems = rest[:-1], rest[-1]
    chunk = nh * 3 * q_ref.shape[0]

    def place(k, row, size):
        if k % 2:
            return outs[-1].at[pl.ds(k // 2 * chunk + row, size), :]
        return outs[k // 2].at[pl.ds(row, size), :]

    copies = pack_copies(
        count, group, hd, first, nh, me_ref[0], (q_ref, k_ref, v_ref), place, sems
    )
    for copy in copies:
        copy.start()
    for copy in copies:
        copy.wait()


def pack(me, q, k, v, after, count, hd, first, nh):
    tok, model = q.shape
    rows = nh * 3 * tok
    shapes = [jax.ShapeDtypeStruct((2 * rows, hd), q.dtype)] * (count // 2)
    return pl.pallas_call(
        functools.partial(pack_kernel, count, model // count, hd, first, nh),
        out_shape=shapes + [jax.ShapeDtypeStruct((count // 2 * rows, hd), q.dtype)],
        in_specs=[SMEM, HBM, HBM, HBM, ANY],
        out_specs=[VM] * (count // 2 + 1),
        scratch_shapes=[pltpu.SemaphoreType.DMA((3 * nh * count,))],
        compiler_params=params(8),
        cost_estimate=SMALL,
        name="pack",
    )(me, q, k, v, after)


def first_kernel(count, group, width, note_rows, mask_rows, tiles, me_ref, nb_ref, *rest):
    q_ref, k_ref, v_ref, x_ref, down_ref = rest[:5]
    outs, rest = rest[5 : 5 + count // 2], rest[5 + count // 2 :]
    x_s, down_s, sems, in_sems = rest
    me = me_ref[0]
    tok = q_ref.shape[0]
    loads = [
        pltpu.make_async_copy(x_ref, x_s, in_sems.at[0]),
        pltpu.make_async_copy(down_ref, down_s, in_sems.at[1]),
    ]
    copies = []
    for k in range(count):
        column = pl.multiple_of((me ^ k) * group, LANES)
        for t, ref in enumerate((q_ref, k_ref, v_ref)):
            to = outs[k // 2].at[pl.ds((k % 2 * 3 + t) * tok, tok), :]
            source = ref.at[:, pl.ds(column, width)]
            copies.append(pltpu.make_async_copy(source, to, sems.at[len(copies)]))
    for copy in loads + copies:
        copy.start()
    rows = lax.broadcasted_iota(jnp.int32, (mask_rows, tok), 0)
    lane_tile = lax.broadcasted_iota(jnp.int32, (mask_rows, tok), 1) // (tok // tiles)
    seen = jnp.zeros((mask_rows, tok), jnp.float32)
    for t in range(tiles):
        for n in range(nb_ref.shape[1]):
            slot = nb_ref[t, n] - (me - 1) * tiles
            seen = jnp.where((rows == slot) & (lane_tile == t), 1.0, seen)
    for copy in loads:
        copy.wait()
    lora = mm(down_s[...], x_s[...], NT).astype(jnp.bfloat16)
    note = jnp.concatenate([lora, seen.astype(jnp.bfloat16)], axis=0)
    for out in outs:
        for n, row in enumerate(range(0, note.shape[0], note_rows)):
            block = note[row : row + note_rows, :]
            out[6 * tok : 6 * tok + block.shape[0], n * tok : (n + 1) * tok] = block
    for copy in copies:
        copy.wait()


def fold_rows(rows, parts):
    return -(-rows // (parts * ROWS)) * ROWS


def first_pack(me, nb, q, k, v, x, down, count, width, mask_rows):
    tok, model = q.shape
    note_rows = fold_rows(down.shape[0] + mask_rows, width // tok)
    bf = q.dtype
    return pl.pallas_call(
        functools.partial(
            first_kernel, count, model // count, width, note_rows, mask_rows, nb.shape[0]
        ),
        out_shape=[jax.ShapeDtypeStruct((6 * tok + note_rows, width), bf)] * (count // 2),
        in_specs=[SMEM, SMEM] + [HBM] * 5,
        out_specs=[VM] * (count // 2),
        scratch_shapes=[
            pltpu.VMEM(x.shape, bf),
            pltpu.VMEM(down.shape, bf),
            pltpu.SemaphoreType.DMA((3 * count,)),
            pltpu.SemaphoreType.DMA((2,)),
        ],
        compiler_params=params(60),
        name="first_pack",
    )(me, nb, q, k, v, x, down)


def forward_kernel(parts, rows, *refs):
    size = refs[0].shape[0] - rows
    for m in range(parts):
        refs[-1][m * size : (m + 1) * size, :] = refs[m][rows:, :]


def forward(blocks, note, after):
    parts = len(blocks)
    rows = (blocks[0].shape[0] - note) // 2
    size = blocks[0].shape[0] - rows
    return pl.pallas_call(
        functools.partial(forward_kernel, parts, rows),
        out_shape=jax.ShapeDtypeStruct((parts * size, blocks[0].shape[1]), blocks[0].dtype),
        in_specs=[VM] * parts + [ANY] * len(after),
        out_specs=VM,
        compiler_params=params(4),
        cost_estimate=SMALL,
        name="forward",
    )(*blocks, *after)


def join_kernel(parts, got_ref, *rest):
    rows = got_ref.shape[0] // parts
    for m, out in enumerate(rest[parts:]):
        out[rows:, :] = got_ref[m * rows : (m + 1) * rows, :]


def join(blocks, got):
    parts = len(blocks)
    return pl.pallas_call(
        functools.partial(join_kernel, parts),
        out_shape=[jax.ShapeDtypeStruct(block.shape, block.dtype) for block in blocks],
        in_specs=[VM] * (1 + parts),
        out_specs=[VM] * parts,
        input_output_aliases={1 + m: m for m in range(parts)},
        compiler_params=params(4),
        cost_estimate=SMALL,
        name="join",
    )(got, *blocks)


def release_kernel(*refs):
    pass


def release(blocks, after):
    return pl.pallas_call(
        release_kernel,
        out_shape=[jax.ShapeDtypeStruct(block.shape, block.dtype) for block in blocks],
        in_specs=[ANY] * (len(blocks) + len(after)),
        out_specs=[ANY] * len(blocks),
        input_output_aliases={n: n for n in range(len(blocks))},
        compiler_params=params(4),
        cost_estimate=SMALL,
        name="release",
    )(*blocks, *after)


def forward_rows_kernel(tok, hd, pieces, *refs):
    for m, row in enumerate(pieces):
        for head, (n, start, lane) in enumerate(row):
            block = refs[n][start + tok : start + 2 * tok, lane : lane + hd]
            refs[-1][m * tok : (m + 1) * tok, head * hd : (head + 1) * hd] = block


def forward_rows(arrays, pieces, tok, hd):
    return pl.pallas_call(
        functools.partial(forward_rows_kernel, tok, hd, pieces),
        out_shape=jax.ShapeDtypeStruct(
            (len(pieces) * tok, len(pieces[0]) * hd), arrays[0].dtype
        ),
        in_specs=[VM] * len(arrays),
        out_specs=VM,
        compiler_params=params(4),
        cost_estimate=SMALL,
        name="forward_rows",
    )(*arrays)


def assemble_kernel(group, moves, me_ref, *rest):
    refs, (out, done_ref, sems) = rest[:-3], rest[-3:]
    me = me_ref[0]
    done_ref[...] = jnp.zeros_like(done_ref)
    copies = []
    for n, (array, row, size, lane, width, k, start, to) in enumerate(moves):
        column = pl.multiple_of((me ^ k) * group + start, LANES)
        copies.append(
            pltpu.make_async_copy(
                refs[array].at[pl.ds(row, size), pl.ds(lane, width)],
                out.at[pl.ds(to, size), pl.ds(column, width)],
                sems.at[n],
            )
        )
    for copy in copies:
        copy.start()
    for copy in copies:
        copy.wait()


def assemble(me, arrays, moves, group, tok, model, base=None):
    given = [] if base is None else [base]
    kernel = functools.partial(assemble_kernel, group, moves)
    if given:
        kernel = lambda me_ref, _, *rest: assemble_kernel(group, moves, me_ref, *rest)
    return pl.pallas_call(
        kernel,
        out_shape=[
            jax.ShapeDtypeStruct((tok, model), arrays[0].dtype),
            jax.ShapeDtypeStruct((8, LANES), jnp.float32),
        ],
        in_specs=[SMEM] + [ANY] * len(given) + [VM] * len(arrays),
        out_specs=[ANY, VM],
        input_output_aliases={1: 0} if given else {},
        scratch_shapes=[pltpu.SemaphoreType.DMA((len(moves),))],
        compiler_params=params(4),
        cost_estimate=SMALL,
        name="assemble",
    )(me, *given, *arrays)


def soft(scores, scale):
    top = jnp.max(scores, axis=0, keepdims=True)
    expo = jnp.exp2((scores - top) * scale)
    return expo, jnp.sum(expo, axis=0, keepdims=True)


def masked_weights(scores, mask, slots, scale):
    rows, tok = scores.shape
    bias = (mask.astype(jnp.float32)[:slots] - 1.0) * (-HIDDEN)
    scores = scores.reshape(slots, rows // slots, tok) + bias[:, None, :]
    expo, norm = soft(scores.reshape(rows, tok), scale)
    return (expo * (1.0 / norm)).astype(jnp.bfloat16)


def window(me, p, count):
    slab = me ^ p
    low = jnp.where(slab > 0, (slab - 1) ^ me, p)
    high = jnp.where(slab < count - 1, (slab + 1) ^ me, p)
    return low, p, high


def log_scale(hd):
    return hd ** (-0.5) * math.log2(math.e)


def attention_kernel(
    count, tok, hd, nh, slots, rank, before, last, factor, me_ref, *rest
):
    half = count // 2
    blocks, rest = rest[: half + (not before)], rest[half + (not before) :]
    up_ref, rest = rest[0], rest[1:]
    if before:
        note_s, hid_ref, gup_in, *rest = rest
    outs, rest = rest[:half], rest[half:]
    if last:
        send_ref, *rest = rest
    elif not before:
        note_s, *rest = rest
    hid_out, gup_ref, *rest = rest
    if last and not before:
        note_s, *rest = rest
    q_s, k_s, vt_s, svt_s, lora_s, grad_s, hid_s = rest
    head = pl.program_id(0)
    me = me_ref[0]
    scale = log_scale(hd)
    size = note_s.shape[1]

    @pl.when(head == 0)
    def _():
        for p in range(count if not before else 0):
            folded = fold_rows(size, blocks[0].shape[1] // tok)
            part = blocks[half].shape[0] // half
            ref, end = blocks[p // 2], 2 * part - folded
            if p % 2:
                ref, end = blocks[half], (p // 2 + 1) * part
            for n, row in enumerate(range(0, size, folded)):
                rows = min(folded, size - row)
                block = ref[end - folded : end - folded + rows, n * tok : (n + 1) * tok]
                note_s[p, row : row + rows, :] = block
        for p in range(count):
            lora_s[:, p * tok : (p + 1) * tok] = note_s[p, :rank, :]
        if before:
            hid_s[...] = hid_ref[...]
            gup_ref[:, : before * hd] = gup_in[...]
        else:
            hid_s[...] = jnp.zeros_like(hid_s)

    for p in range(count):
        if before:
            start = pl.multiple_of((p % 2 * nh + head) * 3 * tok, tok)
            blocks_p = [blocks[p // 2][pl.ds(start + t * tok, tok), :] for t in range(3)]
        else:
            ref, start = blocks[p // 2], 0
            if p % 2:
                ref, start = blocks[half], p // 2 * (blocks[half].shape[0] // half)
            lane = pl.ds(pl.multiple_of(head * hd, LANES), hd)
            blocks_p = [ref[start + t * tok : start + (t + 1) * tok, lane] for t in range(3)]
        q_s[p * tok : (p + 1) * tok, :] = blocks_p[0]
        k_s[p * tok : (p + 1) * tok, :] = blocks_p[1]
        vt_s[:, p * tok : (p + 1) * tok] = blocks_p[2].T
    up_t = up_ref[...]
    for p in range(count):
        cols = slice(p * tok, (p + 1) * tok)
        term = mm(up_t, lora_s[:, cols], TN)
        svt_s[p] = (vt_s[:, cols].astype(jnp.float32) + term).astype(jnp.bfloat16)
    grad_s[...] = jnp.zeros_like(grad_s)

    for start in range(0, count, 8):
        slabs = range(start, min(start + 8, count))
        queries = [q_s[p * tok : (p + 1) * tok, :] for p in slabs]
        places = [window(me, p, count) for p in slabs]
        full = [mm(k_s[...], query, NT) for query in queries]
        seen = [
            mm(
                jnp.concatenate(
                    [k_s[pl.ds(pl.multiple_of(w * tok, tok), tok), :] for w in place], axis=0
                ),
                query,
                NT,
            )
            for place, query in zip(places, queries)
        ]
        full = [soft(x, scale) for x in full]
        teachers = [mm(vt_s[...], expo.astype(jnp.bfloat16)) for expo, _ in full]
        weights = [
            masked_weights(x, note_s[p, rank:, :], slots, scale) for p, x in zip(slabs, seen)
        ]
        students = [
            mm(jnp.concatenate([svt_s[w] for w in place], axis=1), weight)
            for place, weight in zip(places, weights)
        ]
        deltas = []
        for (_, norm), teacher, student in zip(full, teachers, students):
            teacher = (teacher / norm).astype(jnp.bfloat16).astype(jnp.float32)
            deltas.append(((student - teacher) * factor).astype(jnp.bfloat16))
        grads = [mm(weight, delta, NT) for weight, delta in zip(weights, deltas)]
        for p, place, student, grad in zip(slabs, places, students, grads):
            to, row = outs[p // 2], p % 2 * tok
            if last and p % 2:
                to, row = send_ref, p // 2 * tok
            to[row : row + tok, pl.ds(pl.multiple_of(head * hd, LANES), hd)] = student.T.astype(
                jnp.bfloat16
            )
            for n, w in enumerate(place):
                grad_s[w] += grad[n * tok : (n + 1) * tok]

    grad = grad_s[...].reshape(count * tok, hd).astype(jnp.bfloat16)
    column = pl.multiple_of((before + head) * hd, LANES)
    gup_ref[:, pl.ds(column, hd)] = mm(lora_s[...], grad)
    hid_s[...] += mm(up_t, grad, NT)

    @pl.when(head == nh - 1)
    def _():
        if last:
            for m in range(half):
                even = slice(2 * m * tok, (2 * m + 1) * tok)
                odd = slice((2 * m + 1) * tok, (2 * m + 2) * tok)
                row = half * tok + m * rank
                hid_out[:, m * tok : (m + 1) * tok] = hid_s[:, even]
                send_ref[row : row + rank, :] = hid_s[:, odd].astype(jnp.bfloat16)
        else:
            hid_out[...] = hid_s[...]


def attention(me, blocks, up_t, given, first, nh, tok, hd, slots, mask_rows, last):
    count = 2 * (len(blocks) - (not first))
    rank = up_t.shape[0]
    bf, f32 = jnp.bfloat16, jnp.float32
    keys = count * tok
    heads = first + nh
    half = count // 2
    shapes = [jax.ShapeDtypeStruct(((1 if last else 2) * tok, nh * hd), bf)] * half
    if last:
        shapes.append(jax.ShapeDtypeStruct((half * (tok + rank), nh * hd), bf))
    notes = (count, rank + mask_rows, tok)
    if not first and not last:
        shapes.append(jax.ShapeDtypeStruct(notes, bf))
    shapes += [
        jax.ShapeDtypeStruct((rank, keys // 2 if last else keys), f32),
        jax.ShapeDtypeStruct((rank, heads * hd), f32),
    ]
    return pl.pallas_call(
        functools.partial(
            attention_kernel,
            count,
            tok,
            hd,
            nh,
            slots,
            rank,
            first,
            last,
            keys ** (-0.5),
        ),
        grid=(nh,),
        out_shape=shapes,
        in_specs=[SMEM]
        + [VM] * len(blocks)
        + [pl.BlockSpec((rank, hd), lambda h: (0, first + h))]
        + [VM] * len(given),
        out_specs=[VM] * len(shapes),
        scratch_shapes=[pltpu.VMEM(notes, bf)] * (last and not first)
        + [
            pltpu.VMEM((keys, hd), bf),
            pltpu.VMEM((keys, hd), bf),
            pltpu.VMEM((hd, keys), bf),
            pltpu.VMEM((count, hd, tok), bf),
            pltpu.VMEM((rank, keys), bf),
            pltpu.VMEM((count, tok, hd), f32),
            pltpu.VMEM((rank, keys), f32),
        ],
        compiler_params=params(30),
        cost_estimate=pl.CostEstimate(
            flops=nh * 4 * 10**9, bytes_accessed=4 * nh * keys * hd * 2, transcendentals=0
        ),
        name="attention",
    )(
        me,
        *blocks,
        up_t,
        *given,
    )


def pair_kernel(parts, keep_ref, got_ref, *rest):
    riders, outs = rest[:-parts], rest[-parts:]
    rank, width = keep_ref.shape[0], keep_ref.shape[1] // parts
    for m in range(parts):
        cols = slice(m * width, (m + 1) * width)
        total = keep_ref[:, cols] + got_ref[:, cols].astype(jnp.float32)
        outs[m][:rank, :] = total.astype(outs[m].dtype)
        if m:
            rider = riders[m - 1]
            lanes = rider.shape[1]
            size = outs[m].shape[0] - rank
            for n in range(width // lanes):
                block = rider[n * size : (n + 1) * size, :]
                outs[m][rank:, n * lanes : (n + 1) * lanes] = block


def pair_sum(keep, got, parts, riders):
    rank, width = keep.shape[0], keep.shape[1] // parts
    shapes = [jax.ShapeDtypeStruct((rank, width), jnp.float32)] + [
        jax.ShapeDtypeStruct((rank + rider.size // width, width), rider.dtype)
        for rider in riders
    ]
    return pl.pallas_call(
        functools.partial(pair_kernel, parts),
        out_shape=shapes,
        in_specs=[VM] * (2 + len(riders)),
        out_specs=[VM] * parts,
        compiler_params=params(4),
        cost_estimate=SMALL,
        name="pair_sum",
    )(keep, got, *riders)


def riding_kernel(parts, keep_ref, got_ref, *rest):
    blocks, rest = rest[:parts], rest[parts:]
    riders, (total_ref, *outs) = rest[: -2 * parts], rest[-2 * parts :]
    joined, sends = outs[:parts], outs[parts:]
    rank, tok = total_ref.shape
    for m in range(parts):
        row = parts * tok + m * rank
        total = keep_ref[:, m * tok : (m + 1) * tok]
        total += got_ref[row : row + rank, :].astype(jnp.float32)
        if m:
            sends[m - 1][:rank, :] = total.astype(jnp.bfloat16)
        else:
            total_ref[...] = total
        joined[m][:tok, :] = blocks[m][...]
        joined[m][tok:, :] = got_ref[m * tok : (m + 1) * tok, :]
    row = rank
    for rider in riders:
        for lane in range(0, rider.shape[1], tok):
            sends[0][row : row + 2 * tok, :] = rider[:, lane : lane + tok]
            row += 2 * tok


def riding_sum(keep, got, blocks, riders):
    parts = len(blocks)
    (tok, hd), rank, bf = blocks[0].shape, keep.shape[0], blocks[0].dtype
    extra = sum(rider.size for rider in riders) // tok
    shapes = (
        [jax.ShapeDtypeStruct((rank, tok), jnp.float32)]
        + [jax.ShapeDtypeStruct((2 * tok, hd), bf)] * parts
        + [
            jax.ShapeDtypeStruct((rank + (extra if m == 1 else 0), tok), bf)
            for m in range(1, parts)
        ]
    )
    return pl.pallas_call(
        functools.partial(riding_kernel, parts),
        out_shape=shapes,
        in_specs=[VM] * (2 + parts + len(riders)),
        out_specs=[VM] * len(shapes),
        compiler_params=params(4),
        cost_estimate=SMALL,
        name="riding_sum",
    )(keep, got, *blocks, *riders)


def down_kernel(count, group, me_ref, *rest):
    parts = rest[: count // 2]
    x_ref, keep_ref, send_ref = rest[count // 2 :]
    me = me_ref[0]
    hidden = parts[0][...]
    for part in parts[1:]:
        hidden += part[: hidden.shape[0], :].astype(jnp.float32)
    hidden = hidden.astype(jnp.bfloat16)
    for k in range(count):
        column = pl.multiple_of((me ^ k) * group, LANES)
        term = mm(hidden, x_ref[:, pl.ds(column, group)])
        to = (send_ref, keep_ref)[k % 2 == 0]
        to[:, k // 2 * group : (k // 2 + 1) * group] = term.astype(to.dtype)


def down_terms(me, parts, x):
    count = 2 * len(parts)
    model = x.shape[1]
    rank = parts[0].shape[0]
    return pl.pallas_call(
        functools.partial(down_kernel, count, model // count),
        out_shape=[
            jax.ShapeDtypeStruct((rank, model // 2), jnp.float32),
            jax.ShapeDtypeStruct((rank, model // 2), jnp.bfloat16),
        ],
        in_specs=[SMEM] + [VM] * (len(parts) + 1),
        out_specs=[VM, VM],
        compiler_params=params(8),
        cost_estimate=SMALL,
        name="down_terms",
    )(me, *parts, x)


def sum_kernel(*refs):
    total = refs[0][...]
    for ref in refs[1:-2]:
        total += ref[: total.shape[0], :].astype(jnp.float32)
    refs[-1][...] = total


def sum_terms(parts, after):
    return pl.pallas_call(
        sum_kernel,
        out_shape=jax.ShapeDtypeStruct(parts[0].shape, jnp.float32),
        in_specs=[VM] * len(parts) + [ANY],
        out_specs=VM,
        compiler_params=params(4),
        cost_estimate=SMALL,
        name="sum_terms",
    )(*parts, after)


def apart(always, phase, *operands):
    def never(*operands):
        shapes = jax.eval_shape(phase, *operands)
        return jax.tree.map(lambda shape: jnp.zeros(shape.shape, shape.dtype), shapes)

    return lax.cond(always, phase, never, *operands)


def head_chunks(per_group):
    if per_group < 2:
        return [(0, per_group)]
    return [(0, per_group - 1), (per_group - 1, 1)]


def local(
    queries, keys, values, value_layer_input, adapter_down_weight, adapter_up_weight, neighbors
):
    tok, model = queries.shape
    rank = adapter_down_weight.shape[1]
    count = lax.axis_size("context")
    index = lax.axis_index("context")
    me = index.astype(jnp.int32).reshape(1)
    hd = model // H
    group = model // count
    per_group = H // count
    tiles = neighbors.shape[0]
    slots = 3 * tiles
    chunks = head_chunks(per_group)

    mask_rows = slots + -slots % 16

    down_t = adapter_down_weight.T
    up_t = adapter_up_weight.T

    width = chunks[0][1] * hd
    note = fold_rows(rank + mask_rows, width // tok)
    first_own = first_pack(
        me, neighbors, queries, keys, values, value_layer_input, down_t, count, width, mask_rows
    )
    joined = [[]]
    for first, nh in chunks[1:]:
        *own, send = pack(me, queries, keys, values, first_own[0], count, hd, first, nh)
        joined.append(join(own, swap(send, count, 1)))
    noted = chips(first_own, count)
    ready = [own[0] for own in joined[1:]]
    noted = noted + [swap(forward(noted, note, ready), count, 1)]
    messages = [chips(own, count) if own else noted for own in joined]

    own_up = lax.dynamic_slice_in_dim(up_t, index * group, group, 1)
    half = count // 2
    given, arrays, riders = [], [], []
    pieces = [[] for _ in range(half)]
    for c, (first, nh) in enumerate(chunks):
        last = c == len(chunks) - 1
        out = attention(
            me, messages[c], own_up, given, first, nh, tok, hd, slots, mask_rows, last
        )
        blocks, given = list(out[:half]), out[half:]
        if last:
            break
        notes = out[half] if c == 0 else notes
        given = [notes, *out[-2:]]
        riders.append(blocks[1])
        blocks[2:] = release(blocks[2:], messages[c + 1][1:])
        for m in [0] + list(range(2, half)):
            pieces[m] += [(len(arrays), 0, h * hd) for h in range(nh)]
            arrays.append(swap(blocks[m], count, 2 * m) if m else blocks[0])
        pieces[1] += [(-1, rank + 2 * tok * (first + h), 0) for h in range(nh)]
    pieces = [
        [(n if n >= 0 else len(arrays), row, lane) for n, row, lane in group] for group in pieces
    ]
    send, hid, grad_up = given

    def hidden_phase(hid, send, blocks, riders):
        total, *rest = riding_sum(hid, swap(send, count, 1), blocks, riders)
        return chips([total] + rest[half:], count), rest[:half]

    hidden, joined = apart(index < count, hidden_phase, hid, send, blocks, riders)
    keep, send = down_terms(me, hidden, value_layer_input)
    before = first * hd

    def grad_phase(keep, send, arrays, joined):
        base, done = None, keep
        if before:
            got = swap(forward_rows(arrays, pieces, tok, hd), count, 1)
            moves = [(len(arrays), m * tok, tok, 0, before, 2 * m + 1, 0, 0) for m in range(half)]
            for m, group_pieces in enumerate(pieces):
                for h, (n, row, lane) in enumerate(group_pieces):
                    moves.append((n, row, tok, lane, hd, 2 * m, h * hd, 0))
            base, done = assemble(me, [*arrays, got], moves, group, tok, model)
        totals = pair_sum(keep, swap(send, count, 1), half, joined[1:])
        terms = chips(totals, count)
        moves = [(0, r * tok, tok, 0, nh * hd, r, before, 0) for r in range(2)]
        size = 2 * tok * nh * hd // group
        for m in range(1, half):
            step = min(size, tok)
            for row in range(0, 2 * tok, step):
                (r, to), (n, at) = divmod(row, tok), divmod(row, size)
                moves.append((m, rank + at, step, n * nh * hd, nh * hd, 2 * m + r, before, to))
        student_out, _ = assemble(me, [joined[0], *terms[1:]], moves, group, tok, model, base)
        return sum_terms(terms, done), student_out

    grad_down, student_out = grad_phase(keep, send, [*arrays, hidden[1]], joined)
    return student_out, grad_down.T, grad_up.T


def solution(mesh):
    rows = P(("video", "context"), None)
    return jax.shard_map(
        local,
        mesh=mesh,
        in_specs=(rows, rows, rows, rows, P(), P(), rows),
        out_specs=(rows, rows, rows),
        check_vma=False,
    )
```

```python
import functools
import math

import jax
import jax.numpy as jnp
from jax import lax
from jax.experimental import pallas as pl
from jax.experimental.pallas import tpu as pltpu
from jax.sharding import PartitionSpec as P

H = 32
HIDDEN = -1e30
NT = (((1,), (1,)), ((), ()))
TN = (((0,), (0,)), ((), ()))
NN = (((1,), (0,)), ((), ()))


def mm(a, b, dims=NN):
    return lax.dot_general(a, b, dims, preferred_element_type=jnp.float32)


def params(mib):
    return pltpu.CompilerParams(vmem_limit_bytes=mib * 1024 * 1024)


SMEM = pl.BlockSpec(memory_space=pltpu.SMEM)
HBM = pl.BlockSpec(memory_space=pltpu.HBM)
ANY = pl.BlockSpec(memory_space=pl.ANY)
VM = pl.BlockSpec(memory_space=pltpu.VMEM)
LANES = 128
ROWS = 16
SMALL = pl.CostEstimate(flops=0, bytes_accessed=1 << 20, transcendentals=0)


def swap(block, count, bits, targets=None):
    pairs = [(i, i ^ bits) for i in range(count) if targets is None or i ^ bits in targets]
    return lax.ppermute(block, "context", pairs)


def chips(blocks, count, targets=None):
    got = [blocks[0]] + [None] * (len(blocks) - 1)
    for m in sorted(range(1, len(blocks)), key=lambda m: -m):
        got[m] = swap(blocks[m], count, 2 * m, targets)
    return got


def pack_copies(count, group, hd, first, nh, me, refs, place, sems):
    tok = refs[0].shape[0]
    copies = []
    for k in range(count):
        for h in range(nh):
            column = pl.multiple_of((me ^ k) * group + (first + h) * hd, LANES)
            for t, ref in enumerate(refs):
                row = (h * 3 + t) * tok
                copies.append(
                    pltpu.make_async_copy(
                        ref.at[:, pl.ds(column, hd)],
                        place(k, row, tok),
                        sems.at[(k * nh + h) * 3 + t],
                    )
                )
    return copies


def pack_kernel(count, group, hd, first, nh, me_ref, q_ref, k_ref, v_ref, _, *rest):
    outs, sems = rest[:-1], rest[-1]
    chunk = nh * 3 * q_ref.shape[0]

    def place(k, row, size):
        if k % 2:
            return outs[-1].at[pl.ds(k // 2 * chunk + row, size), :]
        return outs[k // 2].at[pl.ds(row, size), :]

    copies = pack_copies(
        count, group, hd, first, nh, me_ref[0], (q_ref, k_ref, v_ref), place, sems
    )
    for copy in copies:
        copy.start()
    for copy in copies:
        copy.wait()


def pack(me, q, k, v, after, count, hd, first, nh):
    tok, model = q.shape
    rows = nh * 3 * tok
    shapes = [jax.ShapeDtypeStruct((2 * rows, hd), q.dtype)] * (count // 2)
    return pl.pallas_call(
        functools.partial(pack_kernel, count, model // count, hd, first, nh),
        out_shape=shapes + [jax.ShapeDtypeStruct((count // 2 * rows, hd), q.dtype)],
        in_specs=[SMEM, HBM, HBM, HBM, ANY],
        out_specs=[VM] * (count // 2 + 1),
        scratch_shapes=[pltpu.SemaphoreType.DMA((3 * nh * count,))],
        compiler_params=params(8),
        cost_estimate=SMALL,
        name="pack",
    )(me, q, k, v, after)


def first_kernel(count, group, width, note_rows, mask_rows, tiles, me_ref, nb_ref, *rest):
    q_ref, k_ref, v_ref, x_ref, down_ref = rest[:5]
    outs, rest = rest[5 : 5 + count // 2], rest[5 + count // 2 :]
    x_s, down_s, sems, in_sems = rest
    me = me_ref[0]
    tok = q_ref.shape[0]
    loads = [
        pltpu.make_async_copy(x_ref, x_s, in_sems.at[0]),
        pltpu.make_async_copy(down_ref, down_s, in_sems.at[1]),
    ]
    copies = []
    for k in range(count):
        column = pl.multiple_of((me ^ k) * group, LANES)
        for t, ref in enumerate((q_ref, k_ref, v_ref)):
            to = outs[k // 2].at[pl.ds((k % 2 * 3 + t) * tok, tok), :]
            source = ref.at[:, pl.ds(column, width)]
            copies.append(pltpu.make_async_copy(source, to, sems.at[len(copies)]))
    for copy in loads + copies:
        copy.start()
    rows = lax.broadcasted_iota(jnp.int32, (mask_rows, tok), 0)
    lane_tile = lax.broadcasted_iota(jnp.int32, (mask_rows, tok), 1) // (tok // tiles)
    seen = jnp.zeros((mask_rows, tok), jnp.float32)
    for t in range(tiles):
        for n in range(nb_ref.shape[1]):
            slot = nb_ref[t, n] - (me - 1) * tiles
            seen = jnp.where((rows == slot) & (lane_tile == t), 1.0, seen)
    for copy in loads:
        copy.wait()
    lora = mm(down_s[...], x_s[...], NT).astype(jnp.bfloat16)
    note = jnp.concatenate([lora, seen.astype(jnp.bfloat16)], axis=0)
    for out in outs:
        for n, row in enumerate(range(0, note.shape[0], note_rows)):
            block = note[row : row + note_rows, :]
            out[6 * tok : 6 * tok + block.shape[0], n * tok : (n + 1) * tok] = block
    for copy in copies:
        copy.wait()


def fold_rows(rows, parts):
    return -(-rows // (parts * ROWS)) * ROWS


def first_pack(me, nb, q, k, v, x, down, count, width, mask_rows):
    tok, model = q.shape
    note_rows = fold_rows(down.shape[0] + mask_rows, width // tok)
    bf = q.dtype
    return pl.pallas_call(
        functools.partial(
            first_kernel, count, model // count, width, note_rows, mask_rows, nb.shape[0]
        ),
        out_shape=[jax.ShapeDtypeStruct((6 * tok + note_rows, width), bf)] * (count // 2),
        in_specs=[SMEM, SMEM] + [HBM] * 5,
        out_specs=[VM] * (count // 2),
        scratch_shapes=[
            pltpu.VMEM(x.shape, bf),
            pltpu.VMEM(down.shape, bf),
            pltpu.SemaphoreType.DMA((3 * count,)),
            pltpu.SemaphoreType.DMA((2,)),
        ],
        compiler_params=params(60),
        name="first_pack",
    )(me, nb, q, k, v, x, down)


def forward_kernel(parts, rows, *refs):
    size = refs[0].shape[0] - rows
    for m in range(parts):
        refs[-1][m * size : (m + 1) * size, :] = refs[m][rows:, :]


def forward(blocks, note, after):
    parts = len(blocks)
    rows = (blocks[0].shape[0] - note) // 2
    size = blocks[0].shape[0] - rows
    return pl.pallas_call(
        functools.partial(forward_kernel, parts, rows),
        out_shape=jax.ShapeDtypeStruct((parts * size, blocks[0].shape[1]), blocks[0].dtype),
        in_specs=[VM] * parts + [ANY] * len(after),
        out_specs=VM,
        compiler_params=params(4),
        cost_estimate=SMALL,
        name="forward",
    )(*blocks, *after)


def join_kernel(parts, got_ref, *rest):
    rows = got_ref.shape[0] // parts
    for m, out in enumerate(rest[parts:]):
        out[rows:, :] = got_ref[m * rows : (m + 1) * rows, :]


def join(blocks, got):
    parts = len(blocks)
    return pl.pallas_call(
        functools.partial(join_kernel, parts),
        out_shape=[jax.ShapeDtypeStruct(block.shape, block.dtype) for block in blocks],
        in_specs=[VM] * (1 + parts),
        out_specs=[VM] * parts,
        input_output_aliases={1 + m: m for m in range(parts)},
        compiler_params=params(4),
        cost_estimate=SMALL,
        name="join",
    )(got, *blocks)


def release_kernel(*refs):
    pass


def release(blocks, after):
    return pl.pallas_call(
        release_kernel,
        out_shape=[jax.ShapeDtypeStruct(block.shape, block.dtype) for block in blocks],
        in_specs=[ANY] * (len(blocks) + len(after)),
        out_specs=[ANY] * len(blocks),
        input_output_aliases={n: n for n in range(len(blocks))},
        compiler_params=params(4),
        cost_estimate=SMALL,
        name="release",
    )(*blocks, *after)


def forward_rows_kernel(tok, hd, pieces, *refs):
    for m, row in enumerate(pieces):
        for head, (n, start, lane) in enumerate(row):
            block = refs[n][start + tok : start + 2 * tok, lane : lane + hd]
            refs[-1][m * tok : (m + 1) * tok, head * hd : (head + 1) * hd] = block


def forward_rows(arrays, pieces, tok, hd):
    return pl.pallas_call(
        functools.partial(forward_rows_kernel, tok, hd, pieces),
        out_shape=jax.ShapeDtypeStruct(
            (len(pieces) * tok, len(pieces[0]) * hd), arrays[0].dtype
        ),
        in_specs=[VM] * len(arrays),
        out_specs=VM,
        compiler_params=params(4),
        cost_estimate=SMALL,
        name="forward_rows",
    )(*arrays)


def assemble_kernel(group, moves, terms, me_ref, *rest):
    if terms:
        *rest, sum_ref, sems = rest
        rest = [*rest[1:], sems]
    refs, out, sems = rest[:-2], rest[-2], rest[-1]
    me = me_ref[0]
    copies = []
    for n, (array, row, size, lane, width, k, start, to) in enumerate(moves):
        column = pl.multiple_of((me ^ k) * group + start, LANES)
        copies.append(
            pltpu.make_async_copy(
                refs[array].at[pl.ds(row, size), pl.ds(lane, width)],
                out.at[pl.ds(to, size), pl.ds(column, width)],
                sems.at[n],
            )
        )
    for copy in copies:
        copy.start()
    if terms:
        total = refs[-1][...]
        for ref in refs[1 : terms + 1]:
            total += ref[: total.shape[0], :].astype(jnp.float32)
        sum_ref[...] = total
    for copy in copies:
        copy.wait()


def assemble(me, arrays, moves, group, tok, model):
    return pl.pallas_call(
        functools.partial(assemble_kernel, group, moves, 0),
        out_shape=jax.ShapeDtypeStruct((tok, model), arrays[0].dtype),
        in_specs=[SMEM] + [VM] * len(arrays),
        out_specs=ANY,
        scratch_shapes=[pltpu.SemaphoreType.DMA((len(moves),))],
        compiler_params=params(4),
        cost_estimate=SMALL,
        name="assemble",
    )(me, *arrays)


def finish(me, base, local, terms, moves, group):
    arrays = [local, *terms[1:], terms[0]]
    return pl.pallas_call(
        functools.partial(assemble_kernel, group, moves, len(terms) - 1),
        out_shape=[
            jax.ShapeDtypeStruct(base.shape, base.dtype),
            jax.ShapeDtypeStruct(terms[0].shape, jnp.float32),
        ],
        in_specs=[SMEM, ANY] + [VM] * len(arrays),
        out_specs=[ANY, VM],
        input_output_aliases={1: 0},
        scratch_shapes=[pltpu.SemaphoreType.DMA((len(moves),))],
        compiler_params=params(4),
        cost_estimate=SMALL,
        name="finish",
    )(me, base, *arrays)


def soft(scores, scale):
    top = jnp.max(scores, axis=0, keepdims=True)
    expo = jnp.exp2((scores - top) * scale)
    return expo, jnp.sum(expo, axis=0, keepdims=True)


def masked_weights(scores, mask, slots, scale):
    rows, tok = scores.shape
    bias = (mask.astype(jnp.float32)[:slots] - 1.0) * (-HIDDEN)
    scores = scores.reshape(slots, rows // slots, tok) + bias[:, None, :]
    expo, norm = soft(scores.reshape(rows, tok), scale)
    return (expo * (1.0 / norm)).astype(jnp.bfloat16)


def window(me, p, count):
    slab = me ^ p
    low = jnp.where(slab > 0, (slab - 1) ^ me, p)
    high = jnp.where(slab < count - 1, (slab + 1) ^ me, p)
    return low, p, high


def log_scale(hd):
    return hd ** (-0.5) * math.log2(math.e)


def attention_kernel(
    count, tok, hd, nh, slots, rank, before, last, factor, me_ref, *rest
):
    half = count // 2
    blocks, rest = rest[: half + (not before)], rest[half + (not before) :]
    up_ref, rest = rest[0], rest[1:]
    if before:
        note_s, hid_ref, gup_in, *rest = rest
    outs, rest = rest[:half], rest[half:]
    if last:
        send_ref, *rest = rest
    elif not before:
        note_s, *rest = rest
    hid_out, gup_ref, *rest = rest
    if last and not before:
        note_s, *rest = rest
    q_s, k_s, vt_s, svt_s, lora_s, grad_s, hid_s = rest
    head = pl.program_id(0)
    me = me_ref[0]
    scale = log_scale(hd)
    size = note_s.shape[1]

    @pl.when(head == 0)
    def _():
        for p in range(count if not before else 0):
            folded = fold_rows(size, blocks[0].shape[1] // tok)
            part = blocks[half].shape[0] // half
            ref, end = blocks[p // 2], 2 * part - folded
            if p % 2:
                ref, end = blocks[half], (p // 2 + 1) * part
            for n, row in enumerate(range(0, size, folded)):
                rows = min(folded, size - row)
                block = ref[end - folded : end - folded + rows, n * tok : (n + 1) * tok]
                note_s[p, row : row + rows, :] = block
        for p in range(count):
            lora_s[:, p * tok : (p + 1) * tok] = note_s[p, :rank, :]
        if before:
            hid_s[...] = hid_ref[...]
            gup_ref[:, : before * hd] = gup_in[...]
        else:
            hid_s[...] = jnp.zeros_like(hid_s)

    for p in range(count):
        if before:
            start = pl.multiple_of((p % 2 * nh + head) * 3 * tok, tok)
            blocks_p = [blocks[p // 2][pl.ds(start + t * tok, tok), :] for t in range(3)]
        else:
            ref, start = blocks[p // 2], 0
            if p % 2:
                ref, start = blocks[half], p // 2 * (blocks[half].shape[0] // half)
            lane = pl.ds(pl.multiple_of(head * hd, LANES), hd)
            blocks_p = [ref[start + t * tok : start + (t + 1) * tok, lane] for t in range(3)]
        q_s[p * tok : (p + 1) * tok, :] = blocks_p[0]
        k_s[p * tok : (p + 1) * tok, :] = blocks_p[1]
        vt_s[:, p * tok : (p + 1) * tok] = blocks_p[2].T
    up_t = up_ref[...]
    for p in range(count):
        cols = slice(p * tok, (p + 1) * tok)
        term = mm(up_t, lora_s[:, cols], TN)
        svt_s[p] = (vt_s[:, cols].astype(jnp.float32) + term).astype(jnp.bfloat16)
    grad_s[...] = jnp.zeros_like(grad_s)

    for start in range(0, count, 8):
        slabs = range(start, min(start + 8, count))
        queries = [q_s[p * tok : (p + 1) * tok, :] for p in slabs]
        places = [window(me, p, count) for p in slabs]
        full = [mm(k_s[...], query, NT) for query in queries]
        seen = [
            mm(
                jnp.concatenate(
                    [k_s[pl.ds(pl.multiple_of(w * tok, tok), tok), :] for w in place], axis=0
                ),
                query,
                NT,
            )
            for place, query in zip(places, queries)
        ]
        full = [soft(x, scale) for x in full]
        teachers = [mm(vt_s[...], expo.astype(jnp.bfloat16)) for expo, _ in full]
        weights = [
            masked_weights(x, note_s[p, rank:, :], slots, scale) for p, x in zip(slabs, seen)
        ]
        students = [
            mm(jnp.concatenate([svt_s[w] for w in place], axis=1), weight)
            for place, weight in zip(places, weights)
        ]
        deltas = []
        for (_, norm), teacher, student in zip(full, teachers, students):
            teacher = (teacher / norm).astype(jnp.bfloat16).astype(jnp.float32)
            deltas.append(((student - teacher) * factor).astype(jnp.bfloat16))
        grads = [mm(weight, delta, NT) for weight, delta in zip(weights, deltas)]
        for p, place, student, grad in zip(slabs, places, students, grads):
            to, row = outs[p // 2], p % 2 * tok
            if last and p % 2:
                to, row = send_ref, p // 2 * tok
            to[row : row + tok, pl.ds(pl.multiple_of(head * hd, LANES), hd)] = student.T.astype(
                jnp.bfloat16
            )
            for n, w in enumerate(place):
                grad_s[w] += grad[n * tok : (n + 1) * tok]

    grad = grad_s[...].reshape(count * tok, hd).astype(jnp.bfloat16)
    column = pl.multiple_of((before + head) * hd, LANES)
    gup_ref[:, pl.ds(column, hd)] = mm(lora_s[...], grad)
    hid_s[...] += mm(up_t, grad, NT)

    @pl.when(head == nh - 1)
    def _():
        if last:
            for m in range(half):
                even = slice(2 * m * tok, (2 * m + 1) * tok)
                odd = slice((2 * m + 1) * tok, (2 * m + 2) * tok)
                row = half * tok + m * rank
                hid_out[:, m * tok : (m + 1) * tok] = hid_s[:, even]
                send_ref[row : row + rank, :] = hid_s[:, odd].astype(jnp.bfloat16)
        else:
            hid_out[...] = hid_s[...]


def attention(me, blocks, up_t, given, first, nh, tok, hd, slots, mask_rows, last):
    count = 2 * (len(blocks) - (not first))
    rank = up_t.shape[0]
    bf, f32 = jnp.bfloat16, jnp.float32
    keys = count * tok
    heads = first + nh
    half = count // 2
    shapes = [jax.ShapeDtypeStruct(((1 if last else 2) * tok, nh * hd), bf)] * half
    if last:
        shapes.append(jax.ShapeDtypeStruct((half * (tok + rank), nh * hd), bf))
    notes = (count, rank + mask_rows, tok)
    if not first and not last:
        shapes.append(jax.ShapeDtypeStruct(notes, bf))
    shapes += [
        jax.ShapeDtypeStruct((rank, keys // 2 if last else keys), f32),
        jax.ShapeDtypeStruct((rank, heads * hd), f32),
    ]
    return pl.pallas_call(
        functools.partial(
            attention_kernel,
            count,
            tok,
            hd,
            nh,
            slots,
            rank,
            first,
            last,
            keys ** (-0.5),
        ),
        grid=(nh,),
        out_shape=shapes,
        in_specs=[SMEM]
        + [VM] * len(blocks)
        + [pl.BlockSpec((rank, hd), lambda h: (0, first + h))]
        + [VM] * len(given),
        out_specs=[VM] * len(shapes),
        scratch_shapes=[pltpu.VMEM(notes, bf)] * (last and not first)
        + [
            pltpu.VMEM((keys, hd), bf),
            pltpu.VMEM((keys, hd), bf),
            pltpu.VMEM((hd, keys), bf),
            pltpu.VMEM((count, hd, tok), bf),
            pltpu.VMEM((rank, keys), bf),
            pltpu.VMEM((count, tok, hd), f32),
            pltpu.VMEM((rank, keys), f32),
        ],
        compiler_params=params(30),
        cost_estimate=pl.CostEstimate(
            flops=nh * 4 * 10**9, bytes_accessed=4 * nh * keys * hd * 2, transcendentals=0
        ),
        name="attention",
    )(
        me,
        *blocks,
        up_t,
        *given,
    )


def pair_kernel(parts, keep_ref, got_ref, *rest):
    riders, outs = rest[:-parts], rest[-parts:]
    rank, width = keep_ref.shape[0], keep_ref.shape[1] // parts
    for m in range(parts):
        cols = slice(m * width, (m + 1) * width)
        total = keep_ref[:, cols] + got_ref[:, cols].astype(jnp.float32)
        outs[m][:rank, :] = total.astype(outs[m].dtype)
        if m:
            rider = riders[m - 1]
            lanes = rider.shape[1]
            size = outs[m].shape[0] - rank
            for n in range(width // lanes):
                block = rider[n * size : (n + 1) * size, :]
                outs[m][rank:, n * lanes : (n + 1) * lanes] = block


def pair_sum(keep, got, parts, riders):
    rank, width = keep.shape[0], keep.shape[1] // parts
    shapes = [jax.ShapeDtypeStruct((rank, width), jnp.float32)] + [
        jax.ShapeDtypeStruct((rank + rider.size // width, width), rider.dtype)
        for rider in riders
    ]
    return pl.pallas_call(
        functools.partial(pair_kernel, parts),
        out_shape=shapes,
        in_specs=[VM] * (2 + len(riders)),
        out_specs=[VM] * parts,
        compiler_params=params(4),
        cost_estimate=SMALL,
        name="pair_sum",
    )(keep, got, *riders)


def riding_kernel(parts, keep_ref, got_ref, *rest):
    blocks, rest = rest[:parts], rest[parts:]
    riders, (total_ref, *outs) = rest[: -2 * parts], rest[-2 * parts :]
    joined, sends = outs[:parts], outs[parts:]
    rank, tok = total_ref.shape
    for m in range(parts):
        row = parts * tok + m * rank
        total = keep_ref[:, m * tok : (m + 1) * tok]
        total += got_ref[row : row + rank, :].astype(jnp.float32)
        if m:
            sends[m - 1][:rank, :] = total.astype(jnp.bfloat16)
        else:
            total_ref[...] = total
        joined[m][:tok, :] = blocks[m][...]
        joined[m][tok:, :] = got_ref[m * tok : (m + 1) * tok, :]
    row = rank
    for rider in riders:
        for lane in range(0, rider.shape[1], tok):
            sends[0][row : row + 2 * tok, :] = rider[:, lane : lane + tok]
            row += 2 * tok


def riding_sum(keep, got, blocks, riders):
    parts = len(blocks)
    (tok, hd), rank, bf = blocks[0].shape, keep.shape[0], blocks[0].dtype
    extra = sum(rider.size for rider in riders) // tok
    shapes = (
        [jax.ShapeDtypeStruct((rank, tok), jnp.float32)]
        + [jax.ShapeDtypeStruct((2 * tok, hd), bf)] * parts
        + [
            jax.ShapeDtypeStruct((rank + (extra if m == 1 else 0), tok), bf)
            for m in range(1, parts)
        ]
    )
    return pl.pallas_call(
        functools.partial(riding_kernel, parts),
        out_shape=shapes,
        in_specs=[VM] * (2 + parts + len(riders)),
        out_specs=[VM] * len(shapes),
        compiler_params=params(4),
        cost_estimate=SMALL,
        name="riding_sum",
    )(keep, got, *blocks, *riders)


def down_kernel(count, group, me_ref, own_ref, *rest):
    parts, (x_ref, keep_ref, send_ref, own_s, part_s, sems) = rest[: count // 2 - 1], rest[-6:]
    me = me_ref[0]
    rank = own_s.shape[0]
    copies = [pltpu.make_async_copy(own_ref, own_s, sems.at[0])]
    for n, part in enumerate(parts):
        source = part.at[pl.ds(0, rank), :]
        copies.append(pltpu.make_async_copy(source, part_s.at[n], sems.at[n + 1]))
    for copy in copies:
        copy.start()
    for copy in copies:
        copy.wait()
    hidden = own_s[...]
    for n in range(len(parts)):
        hidden += part_s[n].astype(jnp.float32)
    hidden = hidden.astype(jnp.bfloat16)
    for k in range(count):
        column = pl.multiple_of((me ^ k) * group, LANES)
        term = mm(hidden, x_ref[:, pl.ds(column, group)])
        to = (send_ref, keep_ref)[k % 2 == 0]
        to[:, k // 2 * group : (k // 2 + 1) * group] = term.astype(to.dtype)


def down_terms(me, parts, x):
    count = 2 * len(parts)
    model = x.shape[1]
    rank, tok = parts[0].shape
    return pl.pallas_call(
        functools.partial(down_kernel, count, model // count),
        out_shape=[
            jax.ShapeDtypeStruct((rank, model // 2), jnp.float32),
            jax.ShapeDtypeStruct((rank, model // 2), jnp.bfloat16),
        ],
        in_specs=[SMEM] + [ANY] * len(parts) + [VM],
        out_specs=[VM, VM],
        scratch_shapes=[
            pltpu.VMEM((rank, tok), jnp.float32),
            pltpu.VMEM((len(parts) - 1, rank, tok), jnp.bfloat16),
            pltpu.SemaphoreType.DMA((len(parts),)),
        ],
        compiler_params=params(8),
        cost_estimate=SMALL,
        name="down_terms",
    )(me, *parts, x)


def apart(always, phase, *operands):
    def never(*operands):
        shapes = jax.eval_shape(phase, *operands)
        return jax.tree.map(lambda shape: jnp.zeros(shape.shape, shape.dtype), shapes)

    return lax.cond(always, phase, never, *operands)


def head_chunks(per_group):
    if per_group < 2:
        return [(0, per_group)]
    return [(0, per_group - 1), (per_group - 1, 1)]


def local(
    queries, keys, values, value_layer_input, adapter_down_weight, adapter_up_weight, neighbors
):
    tok, model = queries.shape
    rank = adapter_down_weight.shape[1]
    count = lax.axis_size("context")
    index = lax.axis_index("context")
    me = index.astype(jnp.int32).reshape(1)
    hd = model // H
    group = model // count
    per_group = H // count
    tiles = neighbors.shape[0]
    slots = 3 * tiles
    chunks = head_chunks(per_group)

    mask_rows = slots + -slots % 16

    down_t = adapter_down_weight.T
    up_t = adapter_up_weight.T

    width = chunks[0][1] * hd
    note = fold_rows(rank + mask_rows, width // tok)
    first_own = first_pack(
        me, neighbors, queries, keys, values, value_layer_input, down_t, count, width, mask_rows
    )
    joined = [[]]
    for first, nh in chunks[1:]:
        *own, send = pack(me, queries, keys, values, first_own[0], count, hd, first, nh)
        joined.append(join(own, swap(send, count, 1)))
    noted = chips(first_own, count)
    ready = [own[0] for own in joined[1:]]
    noted = noted + [swap(forward(noted, note, ready), count, 1)]
    messages = [chips(own, count) if own else noted for own in joined]

    own_up = lax.dynamic_slice_in_dim(up_t, index * group, group, 1)
    half = count // 2
    given, arrays, riders = [], [], []
    pieces = [[] for _ in range(half)]
    for c, (first, nh) in enumerate(chunks):
        last = c == len(chunks) - 1
        out = attention(
            me, messages[c], own_up, given, first, nh, tok, hd, slots, mask_rows, last
        )
        blocks, given = list(out[:half]), out[half:]
        if last:
            break
        notes = out[half] if c == 0 else notes
        given = [notes, *out[-2:]]
        riders.append(blocks[1])
        blocks[2:] = release(blocks[2:], messages[c + 1][1:])
        for m in [0] + list(range(2, half)):
            pieces[m] += [(len(arrays), 0, h * hd) for h in range(nh)]
            arrays.append(swap(blocks[m], count, 2 * m) if m else blocks[0])
        pieces[1] += [(-1, rank + 2 * tok * (first + h), 0) for h in range(nh)]
    pieces = [
        [(n if n >= 0 else len(arrays), row, lane) for n, row, lane in group] for group in pieces
    ]
    send, hid, grad_up = given

    def hidden_phase(hid, send, blocks, riders):
        total, *rest = riding_sum(hid, swap(send, count, 1), blocks, riders)
        return chips([total] + rest[half:], count), rest[:half]

    hidden, joined = apart(index < count, hidden_phase, hid, send, blocks, riders)
    keep, send = down_terms(me, hidden, value_layer_input)
    before = first * hd

    def grad_phase(keep, send, arrays, joined):
        base = jnp.zeros((tok, model), queries.dtype) if not before else None
        if before:
            got = swap(forward_rows(arrays, pieces, tok, hd), count, 1)
            moves = [(len(arrays), m * tok, tok, 0, before, 2 * m + 1, 0, 0) for m in range(half)]
            for m, group_pieces in enumerate(pieces):
                for h, (n, row, lane) in enumerate(group_pieces):
                    moves.append((n, row, tok, lane, hd, 2 * m, h * hd, 0))
            base = assemble(me, [*arrays, got], moves, group, tok, model)
        totals = pair_sum(keep, swap(send, count, 1), half, joined[1:])
        terms = chips(totals, count)
        moves = [(0, r * tok, tok, 0, nh * hd, r, before, 0) for r in range(2)]
        size = 2 * tok * nh * hd // group
        for m in range(1, half):
            step = min(size, tok)
            for row in range(0, 2 * tok, step):
                (r, to), (n, at) = divmod(row, tok), divmod(row, size)
                moves.append((m, rank + at, step, n * nh * hd, nh * hd, 2 * m + r, before, to))
        return finish(me, base, joined[0], terms, moves, group)

    student_out, grad_down = grad_phase(keep, send, [*arrays, hidden[1]], joined)
    return student_out, grad_down.T, grad_up.T


def solution(mesh):
    rows = P(("video", "context"), None)
    return jax.shard_map(
        local,
        mesh=mesh,
        in_specs=(rows, rows, rows, rows, P(), P(), rows),
        out_specs=(rows, rows, rows),
        check_vma=False,
    )
```
